128 devices in a mesh: comp: 4 (over x), cell: 32 (over y, z, core).
Axes of the slice: x: 4, y: 4, z: 4, core: 2. Of those that a mesh axis runs over, the one named last changes fastest.
Arguments:
- biomass: float32 [48, 64, 16384], P(None, None, ('comp', 'cell')), may hold values from 0.1 to 2
- patch_area: float32 [48, 16384], P(None, ('comp', 'cell')), may hold values from 0.005 to 0.04
- cohort_traits: float32 [4, 64], replicated, may hold values from 0.1 to 1
- cell_forcing: float32 [5, 16384], P(None, ('comp', 'cell')), may hold values from 0.1 to 1
- disturb_weight: float32 [4, 16384], P(None, ('comp', 'cell')), may hold values from 0 to 0.25
- transitions: float32 [4, 48, 48], replicated, may hold values from 0 to 1
- land_source: int32 [131072], P(('comp', 'cell')), may hold values from -1 to 127, as said below
- pair_share: float32 [131072], P(('comp', 'cell')), may hold values from 0.05 to 0.35
- river_target: int32 [131072], P(('comp', 'cell')), may hold values from -1 to 2047, as said below
- downstream_step: int32 [262144], P(('comp', 'cell')), may hold values from 0 to 2047
- river_water: float32 [4, 262144], P(None, ('comp', 'cell')), may hold values from 0.5 to 2
- river_rates: float32 [4, 262144], P(None, ('comp', 'cell')), may hold values from 0.05 to 0.8
- capacity: float32 [262144], P(('comp', 'cell')), may hold values from 0.5 to 5
Outputs:
- new_biomass: float32 [48, 64, 16384], P(None, None, ('comp', 'cell'))
- flooded: float32 [16384], P(('comp', 'cell'))
- river_state: float32 [4, 262144], P(None, ('comp', 'cell'))
The draws below stay inside these ranges and needn't reach their ends.
Inputs may be any that keep to these rules, and one draw needn't show every extreme that they name: `land_source`: A device's list has one block of 8 rows for each receiving device, in comp+cell order; live rows come first in every block, padding rows hold -1. Every device has at least one full block, and one receiving device gets full blocks from every device. `river_target`: row s of block i on device j is live exactly when row s of block j on device i of land_source is live, and then names the receiving river cell of device j; padding rows hold -1.
All inputs are finite; a program needn't handle non-finite values.
Results may differ from the reference program's by a relative error of at most 0.0001.
Values sent between devices are 32-bit elements; how exact they have to be, the bound alone decides.
A program may use at most 64 MiB of HBM per device.

```python
import math
import jax
import jax.numpy as jnp
from jax import lax

P_SIZE = 48
K = 64
TYPES = 4
NSUB = 12
LC = 128
RC = 2048
SLOT = 8
LAND = 16384
RIVER = 262144
LIST = 131072
N_COMP = 4
N_CELL = 32


def coupler_lists(key):
    devices = LAND // LC
    count_key, source_key, target_key, basin_key = jax.random.split(jax.random.fold_in(key, 7), 4)
    counts = jax.random.randint(count_key, (devices, devices), SLOT // 4, SLOT + 1)
    basin = jax.random.randint(basin_key, (), 0, devices)
    sender_ids = jnp.arange(devices)[:, None]
    receiver_ids = jnp.arange(devices)[None, :]
    full_block = (receiver_ids == basin) | (receiver_ids == (sender_ids + 1) % devices)
    counts = jnp.where(full_block, SLOT, counts)
    slot_ids = jnp.arange(SLOT)[None, None, :]
    is_live = slot_ids < counts[:, :, None]
    sources = jax.random.randint(source_key, (devices, devices, SLOT), 0, LC)
    targets = jax.random.randint(target_key, (devices, devices, SLOT), 0, RC)
    first_row = (slot_ids == 0) & (receiver_ids[:, :, None] == basin)
    sources = jnp.where(first_row, LC - 1, sources)
    targets = jnp.where(first_row, RC - 1, targets)
    return (jnp.where(is_live, sources, -1), jnp.where(is_live, targets, -1))


def draw_land_source(key, part):
    sources, targets = coupler_lists(key)
    return sources.reshape(-1).astype(jnp.int32)


def draw_river_target(key, part):
    sources, targets = coupler_lists(key)
    return targets.transpose(1, 0, 2).reshape(-1).astype(jnp.int32)


def draw_downstream_step(key, part):
    jump_key, outlet_key = jax.random.split(jax.random.fold_in(key, 11))
    steps = jax.random.randint(jump_key, (RIVER,), 1, RC)
    position = jnp.arange(RIVER)
    steps = jnp.where(jax.random.randint(outlet_key, (RIVER,), 0, 32) == 0, 0, steps)
    steps = jnp.where(position % RC == 0, RC - 1, steps)
    steps = jnp.where(position + steps >= RIVER, 0, steps)
    return steps.astype(jnp.int32)


def draw_transitions(key, part):
    spread_part = jax.random.uniform(jax.random.fold_in(key, 5), (TYPES, P_SIZE, P_SIZE), jnp.float32, 0.0, 1.0 / P_SIZE)
    diagonal = (jnp.arange(P_SIZE)[:, None] == jnp.arange(P_SIZE)[None, :]).astype(jnp.float32)
    return spread_part + 0.5 * diagonal[None]


def steps_of(stream_key, extent, shards, low, high):
    def one(dim, shards_of):
        heights = jax.random.uniform(jax.random.fold_in(jax.random.fold_in(stream_key, 6), dim), (shards_of,), jnp.float32, low / len(shards), high / len(shards))
        return jnp.repeat(jnp.exp(heights), extent[dim] // shards_of).reshape((-1,) + (1,) * (len(extent) - dim - 1))

    gain = one(*shards[0])
    for cut in shards[1:]:
        gain = gain * one(*cut)
    return gain


def setup_inputs(seed: int = 0) -> dict:
    key_of = jax.random.split(jax.random.key(seed), 14)
    return {
        "biomass": jnp.clip(jnp.exp(math.log(2.0) - 2.9957323 * jax.random.uniform(key_of[0], (P_SIZE, K, LAND), jnp.float32) ** steps_of(key_of[0], (P_SIZE, K, LAND), ((2, 128),), -0.2, 0.2)), 0.1, 2.0),
        "patch_area": jnp.clip(jnp.exp(math.log(0.04) - 2.0794415 * jax.random.uniform(key_of[1], (P_SIZE, LAND), jnp.float32) ** steps_of(key_of[1], (P_SIZE, LAND), ((1, 128),), -0.2, 0.2)), 0.005, 0.04),
        "cohort_traits": jnp.clip(jax.random.uniform(key_of[2], (4, K), jnp.float32, 0.1, 1.0), 0.1, 1.0),
        "cell_forcing": jnp.clip(0.1 + 0.9 * jax.random.uniform(key_of[3], (5, LAND), jnp.float32) ** steps_of(key_of[3], (5, LAND), ((1, 128),), -0.2, 0.2), 0.1, 1.0),
        "disturb_weight": jnp.clip(0.25 * jax.random.uniform(key_of[4], (TYPES, LAND), jnp.float32) ** steps_of(key_of[4], (TYPES, LAND), ((1, 128),), -0.2, 0.2), 0.0, 0.25),
        "transitions": draw_transitions(jax.random.fold_in(key_of[13], 71), 0),
        "land_source": draw_land_source(jax.random.fold_in(key_of[13], 71), 0),
        "pair_share": jnp.clip(0.05 + 0.29999999 * jax.random.uniform(key_of[7], (LIST,), jnp.float32) ** steps_of(key_of[7], (LIST,), ((0, 128),), -0.2, 0.2), 0.05, 0.35),
        "river_target": draw_river_target(jax.random.fold_in(key_of[13], 71), 0),
        "downstream_step": draw_downstream_step(jax.random.fold_in(key_of[13], 71), 0),
        "river_water": jnp.clip(jnp.exp(math.log(2.0) - 1.3862944 * jax.random.uniform(key_of[10], (4, RIVER), jnp.float32) ** steps_of(key_of[10], (4, RIVER), ((1, 128),), -0.2, 0.2)), 0.5, 2.0),
        "river_rates": jnp.clip(jnp.exp(math.log(0.8) - 2.7725887 * jax.random.uniform(key_of[11], (4, RIVER), jnp.float32) ** steps_of(key_of[11], (4, RIVER), ((1, 128),), -0.2, 0.2)), 0.05, 0.8),
        "capacity": jnp.clip(jnp.exp(math.log(5.0) - 2.3025851 * jax.random.uniform(key_of[12], (RIVER,), jnp.float32) ** steps_of(key_of[12], (RIVER,), ((0, 128),), -0.2, 0.2)), 0.5, 5.0),
    }


highest = lax.Precision.HIGHEST


def canopy(biomass, patch_area, cohort_traits, cell_forcing):
    leaf_area = biomass * cohort_traits[0][None, :, None]
    bin_count = biomass.shape[1]
    taller_mask = (jnp.arange(bin_count)[None, :] > jnp.arange(bin_count)[:, None]).astype(jnp.float32)
    leaf_above = jnp.einsum("kj,pjc->pkc", taller_mask, leaf_area, precision=highest)
    light_level = cell_forcing[0]
    assimilation = cohort_traits[1][None, :, None] * leaf_area * jnp.exp(-0.05 * leaf_above) * (light_level / (light_level + 0.5))[None, None, :]
    transpiration = 0.5 * jnp.sum(patch_area * jnp.sum(assimilation, axis=1), axis=0)
    wet_rain = cell_forcing[1] * cell_forcing[2]
    runoff = jnp.stack([wet_rain * (1.0 - cell_forcing[4]), wet_rain * cell_forcing[4], cell_forcing[3] * jnp.exp(-0.5 * transpiration)])
    grown_mass = biomass * (1.0 - 0.1 * cohort_traits[2])[None, :, None] + 0.5 * assimilation
    return grown_mass, runoff


def transit(grown_mass, disturb_weight, transitions):
    patches, bin_count, cell_count = grown_mass.shape
    flat_mass = grown_mass.reshape(patches, bin_count * cell_count)
    transited = jnp.zeros_like(grown_mass)
    for kind_index in range(transitions.shape[0]):
        moved_mass = jnp.dot(transitions[kind_index], flat_mass, precision=highest, preferred_element_type=jnp.float32)
        transited = transited + moved_mass.reshape(patches, bin_count, cell_count) * disturb_weight[kind_index][None, None, :]
    return transited


def reference(biomass, patch_area, cohort_traits, cell_forcing, disturb_weight, transitions, land_source, pair_share, river_target, downstream_step, river_water, river_rates, capacity):
    device_count = N_COMP * N_CELL
    mass_blocks = biomass.reshape(P_SIZE, K, device_count, LC).transpose(2, 0, 1, 3)
    area_blocks = patch_area.reshape(P_SIZE, device_count, LC).transpose(1, 0, 2)
    forcing_blocks = cell_forcing.reshape(5, device_count, LC).transpose(1, 0, 2)
    weight_blocks = disturb_weight.reshape(TYPES, device_count, LC).transpose(1, 0, 2)

    def land_block(inputs):
        mass_block, area_block, forcing_block, weight_block = inputs
        grown_mass, runoff_block = canopy(mass_block, area_block, cohort_traits, forcing_block)
        return transit(grown_mass, weight_block, transitions), runoff_block

    transited, runoff_blocks = lax.map(land_block, (mass_blocks, area_blocks, forcing_blocks, weight_blocks))
    runoff = runoff_blocks.transpose(1, 0, 2).reshape(3, LAND)

    device_rows = jnp.arange(device_count, dtype=jnp.int32)
    source_rows = land_source.reshape(device_count, device_count, SLOT)
    share_rows = pair_share.reshape(device_count, device_count, SLOT)
    is_live = source_rows >= 0
    land_cell = jnp.where(is_live, device_rows[:, None, None] * LC + source_rows, 0).astype(jnp.int32)
    pair_values = jnp.where(is_live[None], share_rows[None] * runoff[:, land_cell], 0.0)
    target_rows = river_target.reshape(device_count, device_count, SLOT).transpose(1, 0, 2)
    has_target = target_rows >= 0
    river_cell = jnp.where(has_target, device_rows[None, :, None] * RC + target_rows, RIVER).astype(jnp.int32)
    runoff_in = jnp.stack([jax.ops.segment_sum(pair_values[feature].reshape(-1), river_cell.reshape(-1), num_segments=RIVER + 1)[:RIVER] for feature in range(3)])

    cell_index = jnp.arange(RIVER, dtype=jnp.int32)
    down_cell = jnp.where(downstream_step > 0, cell_index + downstream_step, RIVER).astype(jnp.int32)
    fraction = 1.0 / NSUB
    surface_in = fraction * runoff_in[0:2]
    deep_in = jnp.stack([fraction * runoff_in[2], jnp.zeros_like(runoff_in[2])])
    hill_rate = river_rates[0:2]
    channel_rate = river_rates[2:4]

    def substep(sub_index, state_pair):
        hill_water, channel = state_pair
        hill_out = hill_rate * hill_water
        outflow = channel_rate * channel
        inflow = jnp.stack([jax.ops.segment_sum(outflow[tracer], down_cell, num_segments=RIVER + 1)[:RIVER] for tracer in range(2)])
        return (hill_water - hill_out + surface_in, channel - outflow + hill_out + inflow + deep_in)

    hill_water, channel = lax.fori_loop(0, NSUB, substep, (river_water[0:2], river_water[2:4]))
    stored_total = channel[0] + channel[1]
    inundation = stored_total / (stored_total + capacity)
    flood_back = jnp.where(has_target, inundation[jnp.where(has_target, river_cell, 0)], 0.0)
    flooded = jax.ops.segment_sum((share_rows * flood_back).reshape(-1), jnp.where(is_live, land_cell, LAND).reshape(-1), num_segments=LAND + 1)[:LAND]
    survival = jnp.exp(-cohort_traits[3][None, None, :, None] * flooded.reshape(device_count, LC)[:, None, None, :])
    new_biomass = (transited * survival).transpose(1, 2, 0, 3).reshape(P_SIZE, K, LAND)
    river_state = jnp.concatenate([hill_water, channel], axis=0)
    return new_biomass, flooded, river_state
```

```python
import jax
import jax.numpy as jnp
from jax import lax
from jax.experimental import pallas as pl
from jax.experimental.pallas import tpu as pltpu
from jax.sharding import PartitionSpec as P

MESH = pl.DeviceIdType.MESH
F32 = jnp.float32
BF16 = jnp.bfloat16

NSUB = 12
PATCH = 48
BINS = 64
KINDS = 4
LANES = 128
NA = 16
NB = 8
ROWS = 16
CHUNK = 4


def split2(x):
    hi = x.astype(BF16).astype(F32)
    return hi, x - hi


def split3(x):
    hi, rest = split2(x)
    mid, low = split2(rest)
    return hi, mid, low


def nt_dot(a, b):
    return lax.dot_general(a, b, (((1,), (1,)), ((), ())), preferred_element_type=F32)


def nn_dot(a, b):
    return jnp.dot(a, b, preferred_element_type=F32)


def main_kernel(
    bio, area, traits, forcing, weight, trans, src, share, tgt, step, water, rates, cap,
    tr_out, flood_out, river_out,
    grown, tmat, rhs, onehot_src, lane_rcv, row_rcv, lane_step, row_step, lhs_step, lhs_rcv, lhs_back, state,
    send_a, recv_a, send_b, recv_b, send_rb, recv_rb, send_ra, recv_ra, send_ring, recv_ring,
    sa_s, sa_r, sb_s, sb_r, rb_s, rb_r, ra_s, ra_r, ring_s, ring_r,
):
    my_x = lax.axis_index("comp")
    cell = lax.axis_index("cell")
    my_y, my_b = cell // NB, cell % NB
    my_a = my_x * 4 + my_y
    me = my_x * 32 + cell
    nxt = (me + 1) % 128
    prv = (me + 127) % 128

    def peer_a(other):
        return (other // 4, (other % 4) * NB + my_b)

    def peer_b(other):
        return (my_x, my_y * NB + other)

    barrier = pltpu.get_barrier_semaphore()

    def greet_a(k, _):
        pl.semaphore_signal(barrier, inc=1, device_id=peer_a((my_a + k) % NA), device_id_type=MESH)
        return 0

    def greet_b(k, _):
        pl.semaphore_signal(barrier, inc=1, device_id=peer_b((my_b + k) % NB), device_id_type=MESH)
        return 0

    lax.fori_loop(1, NA, greet_a, 0)
    lax.fori_loop(1, NB, greet_b, 0)
    for other in (nxt, prv):
        pl.semaphore_signal(barrier, inc=1, device_id=(other // 32, other % 32), device_id_type=MESH)

    sub8 = lax.broadcasted_iota(jnp.int32, (8, LANES), 0)
    lane8 = lax.broadcasted_iota(jnp.int32, (8, LANES), 1)
    block8 = lane8 >> 3
    sub16 = lax.broadcasted_iota(jnp.int32, (16, LANES), 0)
    sub128 = lax.broadcasted_iota(jnp.int32, (LANES, LANES), 0)

    for r in range(8):
        hot = jnp.where(sub128 == src[r : r + 1, :], 1.0, 0.0)
        onehot_src[:, r * LANES : (r + 1) * LANES] = hot.astype(BF16)

    light = forcing[0:1, :]
    light_factor = light / (light + 0.5)

    def canopy_bin(i, carry):
        above, total = carry
        k = BINS - 1 - i
        mass = bio[pl.ds(k, PATCH, stride=BINS), :]
        leaf = mass * traits[0, k]
        gain = (traits[1, k] * light_factor) * leaf * jnp.exp(-0.05 * above)
        grown[pl.ds(pl.multiple_of(k * PATCH, PATCH), PATCH), :] = mass * (1.0 - 0.1 * traits[2, k]) + 0.5 * gain
        return above + leaf, total + gain

    zero48 = jnp.zeros((PATCH, LANES), F32)
    _, total = lax.fori_loop(0, BINS, canopy_bin, (zero48, zero48), unroll=4)
    transpiration = 0.5 * jnp.sum(area[...] * total, axis=0, keepdims=True)
    wet = forcing[1:2, :] * forcing[2:3, :]
    frozen = forcing[4:5, :]
    row0 = wet * (1.0 - frozen)
    row1 = wet * frozen
    row2 = forcing[3:4, :] * jnp.exp(-0.5 * transpiration)
    runoff = jnp.where(sub8 == 0, row0, jnp.where(sub8 == 1, row1, jnp.where(sub8 == 2, row2, 0.0)))
    parts = split3(runoff)
    lhs = jnp.concatenate([*parts, jnp.zeros((8, LANES), F32)], axis=0).astype(BF16)
    picked = nn_dot(lhs, onehot_src[...])
    picked = picked[0:8] + picked[8:16] + picked[16:24]
    for r in range(8):
        send_a[r] = picked[:, r * LANES : (r + 1) * LANES] * share[r : r + 1, :]

    def copy_a(k):
        other = (my_a + k) % NA
        return pltpu.make_async_remote_copy(
            src_ref=send_a.at[other // 2], dst_ref=recv_a.at[my_a], send_sem=sa_s.at[k], recv_sem=sa_r.at[my_a],
            device_id=peer_a(other), device_id_type=MESH)

    def arrive_a(k):
        other = (my_a + k) % NA
        return pltpu.make_async_remote_copy(
            src_ref=send_a.at[0], dst_ref=recv_a.at[other], send_sem=sa_s.at[k], recv_sem=sa_r.at[other],
            device_id=peer_a(other), device_id_type=MESH)

    def copy_b(k):
        other = (my_b + k) % NB
        return pltpu.make_async_remote_copy(
            src_ref=send_b.at[other], dst_ref=recv_b.at[my_b], send_sem=sb_s.at[k], recv_sem=sb_r.at[my_b],
            device_id=peer_b(other), device_id_type=MESH)

    def arrive_b(k):
        other = (my_b + k) % NB
        return pltpu.make_async_remote_copy(
            src_ref=send_b.at[other], dst_ref=recv_b.at[other], send_sem=sb_s.at[k], recv_sem=sb_r.at[other],
            device_id=peer_b(other), device_id_type=MESH)

    def copy_rb(k):
        other = (my_b + k) % NB
        return pltpu.make_async_remote_copy(
            src_ref=send_rb.at[other], dst_ref=recv_rb.at[my_b], send_sem=rb_s.at[k], recv_sem=rb_r.at[my_b],
            device_id=peer_b(other), device_id_type=MESH)

    def arrive_rb(k):
        other = (my_b + k) % NB
        return pltpu.make_async_remote_copy(
            src_ref=send_rb.at[other], dst_ref=recv_rb.at[other], send_sem=rb_s.at[k], recv_sem=rb_r.at[other],
            device_id=peer_b(other), device_id_type=MESH)

    def copy_ra(k):
        other = (my_a + k) % NA
        return pltpu.make_async_remote_copy(
            src_ref=send_ra, dst_ref=recv_ra.at[my_a], send_sem=ra_s.at[k], recv_sem=ra_r.at[my_a],
            device_id=peer_a(other), device_id_type=MESH)

    def arrive_ra(k):
        other = (my_a + k) % NA
        return pltpu.make_async_remote_copy(
            src_ref=send_ra, dst_ref=recv_ra.at[other], send_sem=ra_s.at[k], recv_sem=ra_r.at[other],
            device_id=peer_a(other), device_id_type=MESH)

    def ring(t):
        return pltpu.make_async_remote_copy(
            src_ref=send_ring.at[t], dst_ref=recv_ring.at[t], send_sem=ring_s.at[t], recv_sem=ring_r.at[t],
            device_id=(nxt // 32, nxt % 32), device_id_type=MESH)

    def each(count, action):
        def one(k, _):
            action(k)
            return 0

        lax.fori_loop(1, count, one, 0)

    pl.semaphore_wait(barrier, NA + NB)
    each(NA, lambda k: copy_a(k).start())
    recv_a[my_a] = send_a[my_a // 2]

    flat = trans[...].reshape(KINDS * PATCH, PATCH)
    t_hi, t_low = split2(flat)
    tmat[:, 0:PATCH] = t_hi.astype(BF16)
    tmat[:, PATCH : 2 * PATCH] = t_hi.astype(BF16)
    tmat[:, 2 * PATCH : 3 * PATCH] = t_low.astype(BF16)

    def transit_chunk(j):
        for kk in range(CHUNK):
            k = j * CHUNK + kk
            hi, low = split2(grown[pl.ds(pl.multiple_of(k * PATCH, PATCH), PATCH), :])
            cols = slice(kk * LANES, (kk + 1) * LANES)
            rhs[0:PATCH, cols] = hi.astype(BF16)
            rhs[PATCH : 2 * PATCH, cols] = low.astype(BF16)
            rhs[2 * PATCH : 3 * PATCH, cols] = hi.astype(BF16)
        moved = nn_dot(tmat[...], rhs[...])
        for kk in range(CHUNK):
            cols = slice(kk * LANES, (kk + 1) * LANES)
            total = moved[0:PATCH, cols] * weight[0:1, :]
            for kind in range(1, KINDS):
                total += moved[kind * PATCH : (kind + 1) * PATCH, cols] * weight[kind : kind + 1, :]
            tr_out[pl.ds(j * CHUNK + kk, PATCH, stride=BINS), :] = total

    lane16 = lax.broadcasted_iota(jnp.int32, (ROWS, LANES), 1)
    stride = step[...]
    dest = jnp.where(stride > 0, sub16 * LANES + lane16 + stride, -1)
    dest_lane = dest & (LANES - 1)
    dest_row = dest >> 7
    sub32 = lax.broadcasted_iota(jnp.int32, (32, LANES), 0)
    for c in range(ROWS):
        hot = jnp.where(sub128 == dest_lane[c : c + 1, :], 1.0, 0.0)
        lane_step[c * LANES : (c + 1) * LANES, :] = hot.T.astype(BF16)
        row_step[:, c * LANES : (c + 1) * LANES] = jnp.where(sub32 == dest_row[c : c + 1, :], 1.0, 0.0).astype(BF16)

    listed = jnp.zeros((8, LANES), jnp.int32)
    for a in range(NA):
        row = jnp.broadcast_to(tgt[a // 2 : a // 2 + 1, :], (8, LANES))
        row = pltpu.roll(row, ((a - (a % 2) * 8) * 8) % LANES, 1)
        listed = jnp.where(((block8 - sub8) & 15) == a, row, listed)
    for bit in (1, 2, 4):
        listed = jnp.where((sub8 & bit) != 0, pltpu.roll(listed, LANES - bit * 8, 1), listed)
    list_lane = listed & (LANES - 1)
    list_row = listed >> 7
    for b in range(NB):
        cols = slice(b * LANES, (b + 1) * LANES)
        lane_rcv[:, cols] = jnp.where(sub128 == list_lane[b : b + 1, :], 1.0, 0.0).astype(BF16)
        row_rcv[:, cols] = jnp.where(sub16 == list_row[b : b + 1, :], 1.0, 0.0)

    for c in range(ROWS):
        cols = slice(c * LANES, (c + 1) * LANES)
        for q in range(4):
            state[q, c : c + 1, :] = water[q : q + 1, cols]
            state[4 + q, c : c + 1, :] = rates[q : q + 1, cols]
    transit_chunk(0)
    transit_chunk(1)

    each(NA, lambda k: arrive_a(k).wait_recv())
    half = my_a % 2
    tiles = []
    for a in range(NA):
        tiles.append(pltpu.roll(recv_a[a], (half * 64 + a * 8) % LANES, 1))
    for b in range(NB):
        mixed = jnp.zeros((8, LANES), F32)
        for a in range(NA):
            mixed = jnp.where(block8 == (a + b) % 16, tiles[a], mixed)
        send_b[b] = pltpu.roll(mixed, (LANES - b * 8) % LANES, 1)
    each(NB, lambda k: copy_b(k).start())
    recv_b[my_b] = send_b[my_b]
    transit_chunk(2)
    transit_chunk(3)
    each(NB, lambda k: arrive_b(k).wait_recv())

    for b in range(NB):
        cols = slice(b * LANES, (b + 1) * LANES)
        hot = row_rcv[:, cols]
        for s, part in enumerate(split3(recv_b[b])):
            for f in range(3):
                lhs_rcv[(s * 3 + f) * ROWS : (s * 3 + f + 1) * ROWS, cols] = (part[f : f + 1, :] * hot).astype(BF16)
    landed = nt_dot(lhs_rcv[...], lane_rcv[...])
    landed = (landed[0:48] + landed[48:96] + landed[96:144]) * (1.0 / NSUB)
    surface = (landed[0:ROWS], landed[ROWS : 2 * ROWS])
    deep = (landed[2 * ROWS : 3 * ROWS], jnp.zeros((ROWS, LANES), F32))

    def substep(t, carry):
        hill, channel = carry[0:2], carry[2:4]
        partial, hill_next = [], []
        for q in range(2):
            hill_out = state[4 + q] * hill[q]
            outflow = state[6 + q] * channel[q]
            partial.append(channel[q] - outflow + hill_out + deep[q])
            hill_next.append(hill[q] - hill_out + surface[q])
            for s, part in enumerate(split2(outflow)):
                rows = slice((q * 2 + s) * 32, (q * 2 + s + 1) * 32)
                for c in range(ROWS):
                    cols = slice(c * LANES, (c + 1) * LANES)
                    value = jnp.broadcast_to(part[c : c + 1, :], (32, LANES)).astype(BF16)
                    lhs_step[rows, cols] = value * row_step[:, cols]
        spread = nn_dot(lhs_step[...], lane_step[...])
        sums = []
        for q in range(2):
            both = spread[q * 64 : q * 64 + 32] + spread[q * 64 + 32 : q * 64 + 64]
            send_ring[t, q] = both[ROWS:]
            sums.append(both[:ROWS])
        copy = ring(t)
        copy.start()
        transit_chunk(t + 4)
        copy.wait_recv()
        new = [partial[q] + sums[q] + recv_ring[t, q] for q in range(2)]
        return (*hill_next, *new)

    final = lax.fori_loop(0, NSUB, substep, tuple(state[q] for q in range(4)))
    stored = final[2] + final[3]
    inundation = stored / (stored + cap[...])
    lhs = jnp.concatenate(split3(inundation), axis=0).astype(BF16)
    seen = nn_dot(lhs, lane_rcv[...])
    seen = (seen[0:16] + seen[16:32] + seen[32:48]) * row_rcv[...]
    for b in range(NB):
        row = jnp.sum(seen[:, b * LANES : (b + 1) * LANES], axis=0, keepdims=True)
        send_rb[b] = jnp.broadcast_to(row, (8, LANES))
    each(NB, lambda k: copy_rb(k).start())
    recv_rb[my_b] = send_rb[my_b]
    for c in range(ROWS):
        cols = slice(c * LANES, (c + 1) * LANES)
        for q in range(4):
            river_out[q : q + 1, cols] = final[q][c : c + 1, :]
    each(NB, lambda k: arrive_rb(k).wait_recv())
    gathered = jnp.zeros((8, LANES), F32)
    for b in range(NB):
        gathered = jnp.where(sub8 == b, recv_rb[b], gathered)
    send_ra[...] = gathered
    each(NA, lambda k: copy_ra(k).start())
    recv_ra[my_a] = gathered
    each(NA, lambda k: arrive_ra(k).wait_recv())
    for r in range(8):
        even = pltpu.roll(recv_ra[2 * r], (LANES - my_a * 8) % LANES, 1)
        odd = pltpu.roll(recv_ra[2 * r + 1], (64 + LANES - my_a * 8) % LANES, 1)
        pair = jnp.where(lane8 < 64, even, odd)
        for bit in (1, 2, 4):
            pair = jnp.where((sub8 & bit) != 0, pltpu.roll(pair, bit * 8, 1), pair)
        row = jnp.sum(jnp.where((block8 & 7) == sub8, pair, 0.0), axis=0, keepdims=True) * share[r : r + 1, :]
        hi, mid, low = split3(row)
        tile = jnp.where(sub16 == 0, hi, jnp.where(sub16 == 1, mid, jnp.where(sub16 == 2, low, 0.0)))
        lhs_back[:, r * LANES : (r + 1) * LANES] = tile.astype(BF16)
    felt = nt_dot(lhs_back[...], onehot_src[...])
    flood_out[...] = felt[0:1] + felt[1:2] + felt[2:3]

    each(NA, lambda k: copy_a(k).wait_send())
    each(NB, lambda k: copy_b(k).wait_send())
    each(NB, lambda k: copy_rb(k).wait_send())
    each(NA, lambda k: copy_ra(k).wait_send())

    def ring_done(t, _):
        ring(t).wait_send()
        return 0

    lax.fori_loop(0, NSUB, ring_done, 0)


def survive_kernel(mass, traits, flooded, out, survival):
    @pl.when(pl.program_id(0) == 0)
    def _():
        rows = lax.broadcasted_iota(jnp.int32, (BINS, BINS), 0)
        cols = lax.broadcasted_iota(jnp.int32, (BINS, BINS), 1)
        mortality = jnp.sum(jnp.where(rows == cols, traits[3:4, :], 0.0), axis=1, keepdims=True)
        survival[...] = jnp.exp(-mortality * flooded[...])

    for p in range(mass.shape[0] // BINS):
        rows = slice(p * BINS, (p + 1) * BINS)
        out[rows, :] = mass[rows, :] * survival[...]


def shards(
    biomass, patch_area, cohort_traits, cell_forcing, disturb_weight, transitions, land_source, pair_share,
    river_target, downstream_step, river_water, river_rates, capacity,
):
    vmem = pl.BlockSpec(memory_space=pltpu.VMEM)
    smem = pl.BlockSpec(memory_space=pltpu.SMEM)
    dma = pltpu.SemaphoreType.DMA
    tile = (8, LANES)
    n_rows = PATCH * BINS
    transited, flooded, river_state = pl.pallas_call(
        main_kernel,
        out_shape=(
            jax.ShapeDtypeStruct((n_rows, LANES), F32),
            jax.ShapeDtypeStruct((1, LANES), F32),
            jax.ShapeDtypeStruct((4, ROWS * LANES), F32),
        ),
        in_specs=[vmem, vmem, smem] + [vmem] * 10,
        out_specs=(vmem, vmem, vmem),
        scratch_shapes=[
            pltpu.VMEM((n_rows, LANES), F32),
            pltpu.VMEM((KINDS * PATCH, 3 * PATCH), BF16),
            pltpu.VMEM((3 * PATCH, CHUNK * LANES), BF16),
            pltpu.VMEM((LANES, 1024), BF16),
            pltpu.VMEM((LANES, 1024), BF16),
            pltpu.VMEM((ROWS, 1024), F32),
            pltpu.VMEM((ROWS * LANES, LANES), BF16),
            pltpu.VMEM((32, ROWS * LANES), BF16),
            pltpu.VMEM((128, ROWS * LANES), BF16),
            pltpu.VMEM((9 * ROWS, 1024), BF16),
            pltpu.VMEM((16, 1024), BF16),
            pltpu.VMEM((8, ROWS, LANES), F32),
            pltpu.VMEM((8, *tile), F32),
            pltpu.VMEM((NA, *tile), F32),
            pltpu.VMEM((NB, *tile), F32),
            pltpu.VMEM((NB, *tile), F32),
            pltpu.VMEM((NB, *tile), F32),
            pltpu.VMEM((NB, *tile), F32),
            pltpu.VMEM(tile, F32),
            pltpu.VMEM((NA, *tile), F32),
            pltpu.VMEM((NSUB, 2, ROWS, LANES), F32),
            pltpu.VMEM((NSUB, 2, ROWS, LANES), F32),
            dma((NA,)), dma((NA,)), dma((NB,)), dma((NB,)), dma((NB,)), dma((NB,)), dma((NA,)), dma((NA,)),
            dma((NSUB,)), dma((NSUB,)),
        ],
        compiler_params=pltpu.CompilerParams(
            collective_id=0, has_side_effects=True, vmem_limit_bytes=40 * 1024 * 1024),
        name="hour",
    )(
        biomass.reshape(n_rows, LANES), patch_area, cohort_traits, cell_forcing, disturb_weight, transitions,
        land_source.reshape(8, LANES), pair_share.reshape(8, LANES), river_target.reshape(8, LANES),
        downstream_step.reshape(ROWS, LANES), river_water, river_rates, capacity.reshape(ROWS, LANES),
    )
    block = 8 * BINS
    new_biomass = pl.pallas_call(
        survive_kernel,
        grid=(n_rows // block,),
        out_shape=jax.ShapeDtypeStruct((n_rows, LANES), F32),
        in_specs=[
            pl.BlockSpec((block, LANES), lambda i: (i, 0)),
            pl.BlockSpec((4, BINS), lambda i: (0, 0)),
            pl.BlockSpec((1, LANES), lambda i: (0, 0)),
        ],
        out_specs=pl.BlockSpec((block, LANES), lambda i: (i, 0)),
        scratch_shapes=[pltpu.VMEM((BINS, LANES), F32)],
        name="survive",
    )(transited, cohort_traits, flooded)
    return new_biomass.reshape(PATCH, BINS, LANES), flooded.reshape(LANES), river_state


def solution(mesh):
    both = ("comp", "cell")
    return jax.shard_map(
        shards,
        mesh=mesh,
        in_specs=(
            P(None, None, both), P(None, both), P(), P(None, both), P(None, both), P(), P(both), P(both), P(both),
            P(both), P(None, both), P(None, both), P(both),
        ),
        out_specs=(P(None, None, both), P(both), P(None, both)),
        check_vma=False,
    )
```

```python
import jax
import jax.numpy as jnp
from jax import lax
from jax.experimental import pallas as pl
from jax.experimental.pallas import tpu as pltpu
from jax.sharding import PartitionSpec as P

MESH = pl.DeviceIdType.MESH
F32 = jnp.float32
BF16 = jnp.bfloat16

NSUB = 12
PATCH = 48
BINS = 64
KINDS = 4
LANES = 128
NA = 16
NB = 8
ROWS = 16
CHUNK = 4


def split2(x):
    hi = x.astype(BF16).astype(F32)
    return hi, x - hi


def split3(x):
    hi, rest = split2(x)
    mid, low = split2(rest)
    return hi, mid, low


def nt_dot(a, b):
    return lax.dot_general(a, b, (((1,), (1,)), ((), ())), preferred_element_type=F32)


def nn_dot(a, b):
    return jnp.dot(a, b, preferred_element_type=F32)


def main_kernel(
    bio_in, area_in, traits_in, forcing_in, weight_in, trans_in, src_in, share_in, tgt_in, step_in, water_in, rates_in,
    cap_in,
    tr_hbm, flood_hbm, river_hbm,
    tr_out, flood_out, river_out, out_sem,
    bio, area, traits, forcing, weight, trans, src, share, tgt, step, water, rates, cap, in_sem, bio_sem,
    grown, tmat, rhs, onehot_src, lane_rcv, row_rcv, lane_step, row_step, lhs_step, lhs_rcv, lhs_back, state,
    send_a, recv_a, send_b, recv_b, send_rb, recv_rb, send_ra, recv_ra, send_ring, recv_ring,
    sa_s, sa_r, sb_s, sb_r, rb_s, rb_r, ra_s, ra_r, ring_s, ring_r,
):
    sources = (area_in, traits_in, forcing_in, weight_in, trans_in, src_in, share_in, tgt_in, step_in, water_in, rates_in, cap_in)
    targets = (area, traits, forcing, weight, trans, src, share, tgt, step, water, rates, cap)
    loads = [pltpu.make_async_copy(sources[i], targets[i], in_sem.at[i]) for i in range(12)]
    for i in (5, 1, 2):
        loads[i].start()
    mass_loads = [
        pltpu.make_async_copy(bio_in.at[:, pl.ds(g * 8, 8), :], bio.at[g], bio_sem.at[g]) for g in range(BINS // 8)
    ]
    for g in range(BINS // 8 - 1, -1, -1):
        mass_loads[g].start()
    for i in (0, 6, 4, 3, 8, 7, 9, 10, 11):
        loads[i].start()
    my_x = lax.axis_index("comp")
    cell = lax.axis_index("cell")
    my_y, my_b = cell // NB, cell % NB
    my_a = my_x * 4 + my_y
    me = my_x * 32 + cell
    nxt = (me + 1) % 128
    prv = (me + 127) % 128

    def peer_a(other):
        return (other // 4, (other % 4) * NB + my_b)

    def peer_b(other):
        return (my_x, my_y * NB + other)

    barrier = pltpu.get_barrier_semaphore()

    def greet_a(k, _):
        pl.semaphore_signal(barrier, inc=1, device_id=peer_a((my_a + k) % NA), device_id_type=MESH)
        return 0

    def greet_b(k, _):
        pl.semaphore_signal(barrier, inc=1, device_id=peer_b((my_b + k) % NB), device_id_type=MESH)
        return 0

    lax.fori_loop(1, NA, greet_a, 0)
    lax.fori_loop(1, NB, greet_b, 0)
    for other in (nxt, prv):
        pl.semaphore_signal(barrier, inc=1, device_id=(other // 32, other % 32), device_id_type=MESH)

    sub8 = lax.broadcasted_iota(jnp.int32, (8, LANES), 0)
    lane8 = lax.broadcasted_iota(jnp.int32, (8, LANES), 1)
    block8 = lane8 >> 3
    sub16 = lax.broadcasted_iota(jnp.int32, (16, LANES), 0)
    sub128 = lax.broadcasted_iota(jnp.int32, (LANES, LANES), 0)

    loads[5].wait()
    for r in range(8):
        hot = jnp.where(sub128 == src[r : r + 1, :], 1.0, 0.0)
        onehot_src[:, r * LANES : (r + 1) * LANES] = hot.astype(BF16)

    loads[1].wait()
    loads[2].wait()
    light = forcing[0:1, :]
    light_factor = light / (light + 0.5)

    zero48 = jnp.zeros((PATCH, LANES), F32)
    carry = (zero48, zero48)
    for g in range(BINS // 8 - 1, -1, -1):
        mass_loads[g].wait()
        group = bio.at[g].reshape(PATCH * 8, LANES)

        def canopy_bin(i, carry, g=g, group=group):
            above, total = carry
            kk = 7 - i
            k = g * 8 + kk
            mass = group[pl.ds(kk, PATCH, stride=8), :]
            leaf = mass * traits[0, k]
            gain = (traits[1, k] * light_factor) * leaf * jnp.exp(-0.05 * above)
            grown[pl.ds(pl.multiple_of(k * PATCH, PATCH), PATCH), :] = mass * (1.0 - 0.1 * traits[2, k]) + 0.5 * gain
            return above + leaf, total + gain

        carry = lax.fori_loop(0, 8, canopy_bin, carry, unroll=True)
    total = carry[1]
    loads[0].wait()
    transpiration = 0.5 * jnp.sum(area[...] * total, axis=0, keepdims=True)
    wet = forcing[1:2, :] * forcing[2:3, :]
    frozen = forcing[4:5, :]
    row0 = wet * (1.0 - frozen)
    row1 = wet * frozen
    row2 = forcing[3:4, :] * jnp.exp(-0.5 * transpiration)
    runoff = jnp.where(sub8 == 0, row0, jnp.where(sub8 == 1, row1, jnp.where(sub8 == 2, row2, 0.0)))
    parts = split3(runoff)
    lhs = jnp.concatenate([*parts, jnp.zeros((8, LANES), F32)], axis=0).astype(BF16)
    loads[6].wait()
    picked = nn_dot(lhs, onehot_src[...])
    picked = picked[0:8] + picked[8:16] + picked[16:24]
    for r in range(8):
        send_a[r] = picked[:, r * LANES : (r + 1) * LANES] * share[r : r + 1, :]

    def copy_a(k):
        other = (my_a + k) % NA
        return pltpu.make_async_remote_copy(
            src_ref=send_a.at[other // 2], dst_ref=recv_a.at[my_a], send_sem=sa_s.at[k], recv_sem=sa_r.at[my_a],
            device_id=peer_a(other), device_id_type=MESH)

    def arrive_a(k):
        other = (my_a + k) % NA
        return pltpu.make_async_remote_copy(
            src_ref=send_a.at[0], dst_ref=recv_a.at[other], send_sem=sa_s.at[k], recv_sem=sa_r.at[other],
            device_id=peer_a(other), device_id_type=MESH)

    def copy_b(k):
        other = (my_b + k) % NB
        return pltpu.make_async_remote_copy(
            src_ref=send_b.at[other], dst_ref=recv_b.at[my_b], send_sem=sb_s.at[k], recv_sem=sb_r.at[my_b],
            device_id=peer_b(other), device_id_type=MESH)

    def arrive_b(k):
        other = (my_b + k) % NB
        return pltpu.make_async_remote_copy(
            src_ref=send_b.at[other], dst_ref=recv_b.at[other], send_sem=sb_s.at[k], recv_sem=sb_r.at[other],
            device_id=peer_b(other), device_id_type=MESH)

    def copy_rb(k):
        other = (my_b + k) % NB
        return pltpu.make_async_remote_copy(
            src_ref=send_rb.at[other], dst_ref=recv_rb.at[my_b], send_sem=rb_s.at[k], recv_sem=rb_r.at[my_b],
            device_id=peer_b(other), device_id_type=MESH)

    def arrive_rb(k):
        other = (my_b + k) % NB
        return pltpu.make_async_remote_copy(
            src_ref=send_rb.at[other], dst_ref=recv_rb.at[other], send_sem=rb_s.at[k], recv_sem=rb_r.at[other],
            device_id=peer_b(other), device_id_type=MESH)

    def copy_ra(k):
        other = (my_a + k) % NA
        return pltpu.make_async_remote_copy(
            src_ref=send_ra, dst_ref=recv_ra.at[my_a], send_sem=ra_s.at[k], recv_sem=ra_r.at[my_a],
            device_id=peer_a(other), device_id_type=MESH)

    def arrive_ra(k):
        other = (my_a + k) % NA
        return pltpu.make_async_remote_copy(
            src_ref=send_ra, dst_ref=recv_ra.at[other], send_sem=ra_s.at[k], recv_sem=ra_r.at[other],
            device_id=peer_a(other), device_id_type=MESH)

    def ring(t):
        return pltpu.make_async_remote_copy(
            src_ref=send_ring.at[t], dst_ref=recv_ring.at[t], send_sem=ring_s.at[t], recv_sem=ring_r.at[t],
            device_id=(nxt // 32, nxt % 32), device_id_type=MESH)

    def each(count, action):
        def one(k, _):
            action(k)
            return 0

        lax.fori_loop(1, count, one, 0)

    pl.semaphore_wait(barrier, NA + NB)
    each(NA, lambda k: copy_a(k).start())
    recv_a[my_a] = send_a[my_a // 2]

    for i in (4, 3, 8, 7, 9, 10, 11):
        loads[i].wait()
    flat = trans[...].reshape(KINDS * PATCH, PATCH)
    t_hi, t_low = split2(flat)
    tmat[:, 0:PATCH] = t_hi.astype(BF16)
    tmat[:, PATCH : 2 * PATCH] = t_hi.astype(BF16)
    tmat[:, 2 * PATCH : 3 * PATCH] = t_low.astype(BF16)

    def transit_chunk(j):
        for kk in range(CHUNK):
            k = j * CHUNK + kk
            hi, low = split2(grown[pl.ds(pl.multiple_of(k * PATCH, PATCH), PATCH), :])
            cols = slice(kk * LANES, (kk + 1) * LANES)
            rhs[0:PATCH, cols] = hi.astype(BF16)
            rhs[PATCH : 2 * PATCH, cols] = low.astype(BF16)
            rhs[2 * PATCH : 3 * PATCH, cols] = hi.astype(BF16)
        moved = nn_dot(tmat[...], rhs[...])
        for kk in range(CHUNK):
            cols = slice(kk * LANES, (kk + 1) * LANES)
            total = moved[0:PATCH, cols] * weight[0:1, :]
            for kind in range(1, KINDS):
                total += moved[kind * PATCH : (kind + 1) * PATCH, cols] * weight[kind : kind + 1, :]
            tr_out[pl.ds(j * CHUNK + kk, PATCH, stride=BINS), :] = total

    lane16 = lax.broadcasted_iota(jnp.int32, (ROWS, LANES), 1)
    stride = step[...]
    dest = jnp.where(stride > 0, sub16 * LANES + lane16 + stride, -1)
    dest_lane = dest & (LANES - 1)
    dest_row = dest >> 7
    sub32 = lax.broadcasted_iota(jnp.int32, (32, LANES), 0)
    for c in range(ROWS):
        hot = jnp.where(sub128 == dest_lane[c : c + 1, :], 1.0, 0.0)
        lane_step[c * LANES : (c + 1) * LANES, :] = hot.T.astype(BF16)
        row_step[:, c * LANES : (c + 1) * LANES] = jnp.where(sub32 == dest_row[c : c + 1, :], 1.0, 0.0).astype(BF16)

    listed = jnp.zeros((8, LANES), jnp.int32)
    for a in range(NA):
        row = jnp.broadcast_to(tgt[a // 2 : a // 2 + 1, :], (8, LANES))
        row = pltpu.roll(row, ((a - (a % 2) * 8) * 8) % LANES, 1)
        listed = jnp.where(((block8 - sub8) & 15) == a, row, listed)
    for bit in (1, 2, 4):
        listed = jnp.where((sub8 & bit) != 0, pltpu.roll(listed, LANES - bit * 8, 1), listed)
    list_lane = listed & (LANES - 1)
    list_row = listed >> 7
    for b in range(NB):
        cols = slice(b * LANES, (b + 1) * LANES)
        lane_rcv[:, cols] = jnp.where(sub128 == list_lane[b : b + 1, :], 1.0, 0.0).astype(BF16)
        row_rcv[:, cols] = jnp.where(sub16 == list_row[b : b + 1, :], 1.0, 0.0)

    for c in range(ROWS):
        cols = slice(c * LANES, (c + 1) * LANES)
        for q in range(4):
            state[q, c : c + 1, :] = water[q : q + 1, cols]
            state[4 + q, c : c + 1, :] = rates[q : q + 1, cols]
    transit_chunk(0)
    transit_chunk(1)

    each(NA, lambda k: arrive_a(k).wait_recv())
    half = my_a % 2
    tiles = []
    for a in range(NA):
        tiles.append(pltpu.roll(recv_a[a], (half * 64 + a * 8) % LANES, 1))
    for b in range(NB):
        mixed = jnp.zeros((8, LANES), F32)
        for a in range(NA):
            mixed = jnp.where(block8 == (a + b) % 16, tiles[a], mixed)
        send_b[b] = pltpu.roll(mixed, (LANES - b * 8) % LANES, 1)
    each(NB, lambda k: copy_b(k).start())
    recv_b[my_b] = send_b[my_b]
    transit_chunk(2)
    transit_chunk(3)
    each(NB, lambda k: arrive_b(k).wait_recv())

    for b in range(NB):
        cols = slice(b * LANES, (b + 1) * LANES)
        hot = row_rcv[:, cols]
        for s, part in enumerate(split3(recv_b[b])):
            for f in range(3):
                lhs_rcv[(s * 3 + f) * ROWS : (s * 3 + f + 1) * ROWS, cols] = (part[f : f + 1, :] * hot).astype(BF16)
    landed = nt_dot(lhs_rcv[...], lane_rcv[...])
    landed = (landed[0:48] + landed[48:96] + landed[96:144]) * (1.0 / NSUB)
    surface = (landed[0:ROWS], landed[ROWS : 2 * ROWS])
    deep = (landed[2 * ROWS : 3 * ROWS], jnp.zeros((ROWS, LANES), F32))

    def substep(t, carry):
        hill, channel = carry[0:2], carry[2:4]
        partial, hill_next = [], []
        for q in range(2):
            hill_out = state[4 + q] * hill[q]
            outflow = state[6 + q] * channel[q]
            partial.append(channel[q] - outflow + hill_out + deep[q])
            hill_next.append(hill[q] - hill_out + surface[q])
            for s, part in enumerate(split2(outflow)):
                rows = slice((q * 2 + s) * 32, (q * 2 + s + 1) * 32)
                for c in range(ROWS):
                    cols = slice(c * LANES, (c + 1) * LANES)
                    value = jnp.broadcast_to(part[c : c + 1, :], (32, LANES)).astype(BF16)
                    lhs_step[rows, cols] = value * row_step[:, cols]
        spread = nn_dot(lhs_step[...], lane_step[...])
        sums = []
        for q in range(2):
            both = spread[q * 64 : q * 64 + 32] + spread[q * 64 + 32 : q * 64 + 64]
            send_ring[t, q] = both[ROWS:]
            sums.append(both[:ROWS])
        copy = ring(t)
        copy.start()
        transit_chunk(t + 4)
        copy.wait_recv()
        new = [partial[q] + sums[q] + recv_ring[t, q] for q in range(2)]
        return (*hill_next, *new)

    final = lax.fori_loop(0, NSUB, substep, tuple(state[q] for q in range(4)))
    stored = final[2] + final[3]
    inundation = stored / (stored + cap[...])
    lhs = jnp.concatenate(split3(inundation), axis=0).astype(BF16)
    seen = nn_dot(lhs, lane_rcv[...])
    seen = (seen[0:16] + seen[16:32] + seen[32:48]) * row_rcv[...]
    for b in range(NB):
        row = jnp.sum(seen[:, b * LANES : (b + 1) * LANES], axis=0, keepdims=True)
        send_rb[b] = jnp.broadcast_to(row, (8, LANES))
    each(NB, lambda k: copy_rb(k).start())
    recv_rb[my_b] = send_rb[my_b]
    for c in range(ROWS):
        cols = slice(c * LANES, (c + 1) * LANES)
        for q in range(4):
            river_out[q : q + 1, cols] = final[q][c : c + 1, :]
    stores = (
        pltpu.make_async_copy(tr_out, tr_hbm, out_sem.at[0]),
        pltpu.make_async_copy(river_out, river_hbm, out_sem.at[1]),
    )
    for copy in stores:
        copy.start()
    each(NB, lambda k: arrive_rb(k).wait_recv())
    gathered = jnp.zeros((8, LANES), F32)
    for b in range(NB):
        gathered = jnp.where(sub8 == b, recv_rb[b], gathered)
    send_ra[...] = gathered
    each(NA, lambda k: copy_ra(k).start())
    recv_ra[my_a] = gathered
    each(NA, lambda k: arrive_ra(k).wait_recv())
    for r in range(8):
        even = pltpu.roll(recv_ra[2 * r], (LANES - my_a * 8) % LANES, 1)
        odd = pltpu.roll(recv_ra[2 * r + 1], (64 + LANES - my_a * 8) % LANES, 1)
        pair = jnp.where(lane8 < 64, even, odd)
        for bit in (1, 2, 4):
            pair = jnp.where((sub8 & bit) != 0, pltpu.roll(pair, bit * 8, 1), pair)
        row = jnp.sum(jnp.where((block8 & 7) == sub8, pair, 0.0), axis=0, keepdims=True) * share[r : r + 1, :]
        hi, mid, low = split3(row)
        tile = jnp.where(sub16 == 0, hi, jnp.where(sub16 == 1, mid, jnp.where(sub16 == 2, low, 0.0)))
        lhs_back[:, r * LANES : (r + 1) * LANES] = tile.astype(BF16)
    felt = nt_dot(lhs_back[...], onehot_src[...])
    flood_out[...] = felt[0:1] + felt[1:2] + felt[2:3]
    store = pltpu.make_async_copy(flood_out, flood_hbm, out_sem.at[2])
    store.start()

    each(NA, lambda k: copy_a(k).wait_send())
    each(NB, lambda k: copy_b(k).wait_send())
    each(NB, lambda k: copy_rb(k).wait_send())
    each(NA, lambda k: copy_ra(k).wait_send())

    def ring_done(t, _):
        ring(t).wait_send()
        return 0

    lax.fori_loop(0, NSUB, ring_done, 0)
    for copy in (*stores, store):
        copy.wait()


def survive_kernel(
    mass_in, traits_in, flooded_in, river_in, out, flooded_out, river_out,
    mass, traits, flooded, survival, load_sem, store_sem,
):
    block = PATCH * BINS // 6
    small = [
        pltpu.make_async_copy(flooded_in, flooded, load_sem.at[6]),
        pltpu.make_async_copy(traits_in, traits, load_sem.at[7]),
    ]
    pieces = [pl.ds(i * block, block) for i in range(6)]
    loads = [pltpu.make_async_copy(mass_in.at[p, :], mass.at[p, :], load_sem.at[i]) for i, p in enumerate(pieces)]
    stores = [pltpu.make_async_copy(mass.at[p, :], out.at[p, :], store_sem.at[i]) for i, p in enumerate(pieces)]
    stores += [
        pltpu.make_async_copy(flooded, flooded_out, store_sem.at[6]),
        pltpu.make_async_copy(river_in, river_out, store_sem.at[7]),
    ]
    for copy in (*small, *loads, stores[7]):
        copy.start()
    for copy in small:
        copy.wait()
    stores[6].start()
    rows = lax.broadcasted_iota(jnp.int32, (BINS, BINS), 0)
    cols = lax.broadcasted_iota(jnp.int32, (BINS, BINS), 1)
    mortality = jnp.sum(jnp.where(rows == cols, traits[3:4, :], 0.0), axis=1, keepdims=True)
    survival[...] = jnp.exp(-mortality * flooded[...])
    for i in range(6):
        loads[i].wait()
        for p in range(8):
            rows = slice(i * block + p * BINS, i * block + (p + 1) * BINS)
            mass[rows, :] = mass[rows, :] * survival[...]
        stores[i].start()
    for copy in stores:
        copy.wait()


def shards(
    biomass, patch_area, cohort_traits, cell_forcing, disturb_weight, transitions, land_source, pair_share,
    river_target, downstream_step, river_water, river_rates, capacity,
):
    hbm = pl.BlockSpec(memory_space=pltpu.HBM)
    dma = pltpu.SemaphoreType.DMA
    tile = (8, LANES)
    n_rows = PATCH * BINS
    transited, flooded, river_state = pl.pallas_call(
        main_kernel,
        out_shape=(
            jax.ShapeDtypeStruct((n_rows, LANES), F32),
            jax.ShapeDtypeStruct((1, LANES), F32),
            jax.ShapeDtypeStruct((4, ROWS * LANES), F32),
        ),
        in_specs=[hbm] * 13,
        out_specs=(hbm, hbm, hbm),
        scratch_shapes=[
            pltpu.VMEM((n_rows, LANES), F32),
            pltpu.VMEM((1, LANES), F32),
            pltpu.VMEM((4, ROWS * LANES), F32),
            dma((3,)),
            pltpu.VMEM((BINS // 8, PATCH, 8, LANES), F32),
            pltpu.VMEM((PATCH, LANES), F32),
            pltpu.SMEM((4, BINS), F32),
            pltpu.VMEM((5, LANES), F32),
            pltpu.VMEM((KINDS, LANES), F32),
            pltpu.VMEM((KINDS, PATCH, PATCH), F32),
            pltpu.VMEM(tile, jnp.int32),
            pltpu.VMEM(tile, F32),
            pltpu.VMEM(tile, jnp.int32),
            pltpu.VMEM((ROWS, LANES), jnp.int32),
            pltpu.VMEM((4, ROWS * LANES), F32),
            pltpu.VMEM((4, ROWS * LANES), F32),
            pltpu.VMEM((ROWS, LANES), F32),
            dma((12,)),
            dma((BINS // 8,)),
            pltpu.VMEM((n_rows, LANES), F32),
            pltpu.VMEM((KINDS * PATCH, 3 * PATCH), BF16),
            pltpu.VMEM((3 * PATCH, CHUNK * LANES), BF16),
            pltpu.VMEM((LANES, 1024), BF16),
            pltpu.VMEM((LANES, 1024), BF16),
            pltpu.VMEM((ROWS, 1024), F32),
            pltpu.VMEM((ROWS * LANES, LANES), BF16),
            pltpu.VMEM((32, ROWS * LANES), BF16),
            pltpu.VMEM((128, ROWS * LANES), BF16),
            pltpu.VMEM((9 * ROWS, 1024), BF16),
            pltpu.VMEM((16, 1024), BF16),
            pltpu.VMEM((8, ROWS, LANES), F32),
            pltpu.VMEM((8, *tile), F32),
            pltpu.VMEM((NA, *tile), F32),
            pltpu.VMEM((NB, *tile), F32),
            pltpu.VMEM((NB, *tile), F32),
            pltpu.VMEM((NB, *tile), F32),
            pltpu.VMEM((NB, *tile), F32),
            pltpu.VMEM(tile, F32),
            pltpu.VMEM((NA, *tile), F32),
            pltpu.VMEM((NSUB, 2, ROWS, LANES), F32),
            pltpu.VMEM((NSUB, 2, ROWS, LANES), F32),
            dma((NA,)), dma((NA,)), dma((NB,)), dma((NB,)), dma((NB,)), dma((NB,)), dma((NA,)), dma((NA,)),
            dma((NSUB,)), dma((NSUB,)),
        ],
        compiler_params=pltpu.CompilerParams(
            collective_id=0, has_side_effects=True, vmem_limit_bytes=60 * 1024 * 1024),
        name="hour",
    )(
        biomass, patch_area, cohort_traits, cell_forcing, disturb_weight, transitions,
        land_source.reshape(8, LANES), pair_share.reshape(8, LANES), river_target.reshape(8, LANES),
        downstream_step.reshape(ROWS, LANES), river_water, river_rates, capacity.reshape(ROWS, LANES),
    )
    new_biomass, flooded, river_state = pl.pallas_call(
        survive_kernel,
        out_shape=(
            jax.ShapeDtypeStruct((n_rows, LANES), F32),
            jax.ShapeDtypeStruct((1, LANES), F32),
            jax.ShapeDtypeStruct((4, ROWS * LANES), F32),
        ),
        in_specs=[hbm] * 4,
        out_specs=(hbm, hbm, hbm),
        scratch_shapes=[
            pltpu.VMEM((n_rows, LANES), F32),
            pltpu.VMEM((4, BINS), F32),
            pltpu.VMEM((1, LANES), F32),
            pltpu.VMEM((BINS, LANES), F32),
            dma((8,)),
            dma((8,)),
        ],
        compiler_params=pltpu.CompilerParams(vmem_limit_bytes=60 * 1024 * 1024),
        name="survive",
    )(transited, cohort_traits, flooded, river_state)
    return new_biomass.reshape(PATCH, BINS, LANES), flooded.reshape(LANES), river_state


def solution(mesh):
    both = ("comp", "cell")
    return jax.shard_map(
        shards,
        mesh=mesh,
        in_specs=(
            P(None, None, both), P(None, both), P(), P(None, both), P(None, both), P(), P(both), P(both), P(both),
            P(both), P(None, both), P(None, both), P(both),
        ),
        out_specs=(P(None, None, both), P(both), P(None, both)),
        check_vma=False,
    )
```

```python
import jax
import jax.numpy as jnp
from jax import lax
from jax.experimental import pallas as pl
from jax.experimental.pallas import tpu as pltpu
from jax.sharding import PartitionSpec as P

MESH = pl.DeviceIdType.MESH
F32 = jnp.float32
BF16 = jnp.bfloat16

NSUB = 12
PATCH = 48
BINS = 64
KINDS = 4
LANES = 128
NA = 16
NB = 8
ROWS = 16
CHUNK = 4
G = 4
STEPS = NSUB // G
CHUNKS_STEP = 12 // STEPS
A_PATHS = 3
OFF = [ROWS * sum(j + 1 for j in range(1, k)) for k in range(1, G + 2)]


def split2(x):
    hi = x.astype(BF16).astype(F32)
    return hi, x - hi


def split3(x):
    hi, rest = split2(x)
    mid, low = split2(rest)
    return hi, mid, low


def nt_dot(a, b):
    return lax.dot_general(a, b, (((1,), (1,)), ((), ())), preferred_element_type=F32)


def nn_dot(a, b):
    return jnp.dot(a, b, preferred_element_type=F32)


def main_kernel(
    bio_in, area_in, traits_in, forcing_in, weight_in, trans_in, src_in, share_in, tgt_in, step_in, water_in, rates_in,
    cap_in,
    tr_hbm, flood_hbm, river_hbm,
    tr_out, flood_out, river_out, out_sem,
    bio, area, traits, forcing, weight, trans, src, share, tgt, step, water, rates, cap, in_sem, bio_sem,
    grown, tmat, rhs, onehot_src, lane_rcv, row_rcv, lane_step, row_step, lhs_step, lhs_rcv, lhs_back, state,
    moved_by, table, table_send, path, path_rate, st_s, st_r,
    send_a, recv_a, send_b, recv_b, send_rb, recv_rb, send_ra, recv_ra, send_ring, recv_ring,
    sa_s, sa_r, sb_s, sb_r, rb_s, rb_r, ra_s, ra_r, ring_s, ring_r,
):
    sources = (area_in, traits_in, forcing_in, weight_in, trans_in, src_in, share_in, tgt_in, step_in, water_in, rates_in, cap_in)
    targets = (area, traits, forcing, weight, trans, src, share, tgt, step, water, rates, cap)
    loads = [pltpu.make_async_copy(sources[i], targets[i], in_sem.at[i]) for i in range(12)]
    for i in (5, 1, 2):
        loads[i].start()
    mass_loads = [
        pltpu.make_async_copy(bio_in.at[:, pl.ds(g * 8, 8), :], bio.at[g], bio_sem.at[g]) for g in range(BINS // 8)
    ]
    for g in range(BINS // 8 - 1, -1, -1):
        mass_loads[g].start()
    for i in (0, 6, 4, 3, 8, 7, 9, 10, 11):
        loads[i].start()
    my_x = lax.axis_index("comp")
    cell = lax.axis_index("cell")
    my_y, my_b = cell // NB, cell % NB
    my_a = my_x * 4 + my_y
    me = my_x * 32 + cell

    def peer_a(other):
        return (other // 4, (other % 4) * NB + my_b)

    def peer_b(other):
        return (my_x, my_y * NB + other)

    barrier = pltpu.get_barrier_semaphore()

    def greet_a(k, _):
        pl.semaphore_signal(barrier, inc=1, device_id=peer_a((my_a + k) % NA), device_id_type=MESH)
        return 0

    def greet_b(k, _):
        pl.semaphore_signal(barrier, inc=1, device_id=peer_b((my_b + k) % NB), device_id_type=MESH)
        return 0

    lax.fori_loop(1, NA, greet_a, 0)
    lax.fori_loop(1, NB, greet_b, 0)
    for m in range(1, G + 1):
        for other in ((me + m) % 128, (me + 128 - m) % 128):
            pl.semaphore_signal(barrier, inc=1, device_id=(other // 32, other % 32), device_id_type=MESH)

    sub8 = lax.broadcasted_iota(jnp.int32, (8, LANES), 0)
    lane8 = lax.broadcasted_iota(jnp.int32, (8, LANES), 1)
    block8 = lane8 >> 3
    sub16 = lax.broadcasted_iota(jnp.int32, (16, LANES), 0)
    sub128 = lax.broadcasted_iota(jnp.int32, (LANES, LANES), 0)

    loads[5].wait()
    for r in range(8):
        hot = jnp.where(sub128 == src[r : r + 1, :], 1.0, 0.0)
        onehot_src[:, r * LANES : (r + 1) * LANES] = hot.astype(BF16)

    loads[1].wait()
    loads[2].wait()
    light = forcing[0:1, :]
    light_factor = light / (light + 0.5)

    zero48 = jnp.zeros((PATCH, LANES), F32)
    carry = (zero48, zero48)
    for g in range(BINS // 8 - 1, -1, -1):
        mass_loads[g].wait()
        group = bio.at[g].reshape(PATCH * 8, LANES)

        def canopy_bin(i, carry, g=g, group=group):
            above, total = carry
            kk = 7 - i
            k = g * 8 + kk
            mass = group[pl.ds(kk, PATCH, stride=8), :]
            leaf = mass * traits[0, k]
            gain = (traits[1, k] * light_factor) * leaf * jnp.exp(-0.05 * above)
            grown[pl.ds(pl.multiple_of(k * PATCH, PATCH), PATCH), :] = mass * (1.0 - 0.1 * traits[2, k]) + 0.5 * gain
            return above + leaf, total + gain

        carry = lax.fori_loop(0, 8, canopy_bin, carry, unroll=True)
    total = carry[1]
    loads[0].wait()
    transpiration = 0.5 * jnp.sum(area[...] * total, axis=0, keepdims=True)
    wet = forcing[1:2, :] * forcing[2:3, :]
    frozen = forcing[4:5, :]
    row0 = wet * (1.0 - frozen)
    row1 = wet * frozen
    row2 = forcing[3:4, :] * jnp.exp(-0.5 * transpiration)
    runoff = jnp.where(sub8 == 0, row0, jnp.where(sub8 == 1, row1, jnp.where(sub8 == 2, row2, 0.0)))
    parts = split3(runoff)
    lhs = jnp.concatenate([*parts, jnp.zeros((8, LANES), F32)], axis=0).astype(BF16)
    loads[6].wait()
    picked = nn_dot(lhs, onehot_src[...])
    picked = picked[0:8] + picked[8:16] + picked[16:24]
    for r in range(8):
        send_a[r] = picked[:, r * LANES : (r + 1) * LANES] * share[r : r + 1, :]

    def copy_a(k):
        other = (my_a + k) % NA
        return pltpu.make_async_remote_copy(
            src_ref=send_a.at[other // 2], dst_ref=recv_a.at[my_a], send_sem=sa_s.at[k], recv_sem=sa_r.at[my_a],
            device_id=peer_a(other), device_id_type=MESH)

    def arrive_a(k):
        other = (my_a + k) % NA
        return pltpu.make_async_remote_copy(
            src_ref=send_a.at[0], dst_ref=recv_a.at[other], send_sem=sa_s.at[k], recv_sem=sa_r.at[other],
            device_id=peer_a(other), device_id_type=MESH)

    def copy_b(k):
        other = (my_b + k) % NB
        return pltpu.make_async_remote_copy(
            src_ref=send_b.at[other], dst_ref=recv_b.at[my_b], send_sem=sb_s.at[k], recv_sem=sb_r.at[my_b],
            device_id=peer_b(other), device_id_type=MESH)

    def arrive_b(k):
        other = (my_b + k) % NB
        return pltpu.make_async_remote_copy(
            src_ref=send_b.at[other], dst_ref=recv_b.at[other], send_sem=sb_s.at[k], recv_sem=sb_r.at[other],
            device_id=peer_b(other), device_id_type=MESH)

    def copy_rb(k):
        other = (my_b + k) % NB
        return pltpu.make_async_remote_copy(
            src_ref=send_rb.at[other], dst_ref=recv_rb.at[my_b], send_sem=rb_s.at[k], recv_sem=rb_r.at[my_b],
            device_id=peer_b(other), device_id_type=MESH)

    def arrive_rb(k):
        other = (my_b + k) % NB
        return pltpu.make_async_remote_copy(
            src_ref=send_rb.at[other], dst_ref=recv_rb.at[other], send_sem=rb_s.at[k], recv_sem=rb_r.at[other],
            device_id=peer_b(other), device_id_type=MESH)

    def copy_ra(k):
        other = (my_a + k) % NA
        return pltpu.make_async_remote_copy(
            src_ref=send_ra, dst_ref=recv_ra.at[my_a], send_sem=ra_s.at[k], recv_sem=ra_r.at[my_a],
            device_id=peer_a(other), device_id_type=MESH)

    def arrive_ra(k):
        other = (my_a + k) % NA
        return pltpu.make_async_remote_copy(
            src_ref=send_ra, dst_ref=recv_ra.at[other], send_sem=ra_s.at[k], recv_sem=ra_r.at[other],
            device_id=peer_a(other), device_id_type=MESH)

    def ring(e, m):
        to = (me + m) % 128
        return pltpu.make_async_remote_copy(
            src_ref=send_ring.at[e, m - 1], dst_ref=recv_ring.at[e, m - 1],
            send_sem=ring_s.at[e, m - 1], recv_sem=ring_r.at[e, m - 1],
            device_id=(to // 32, to % 32), device_id_type=MESH)

    def upstream(m):
        to = (me + 128 - m) % 128
        return pltpu.make_async_remote_copy(
            src_ref=table_send, dst_ref=table.at[m], send_sem=st_s.at[m], recv_sem=st_r.at[m],
            device_id=(to // 32, to % 32), device_id_type=MESH)

    def each(count, action):
        def one(k, _):
            action(k)
            return 0

        lax.fori_loop(1, count, one, 0)

    pl.semaphore_wait(barrier, NA + NB - 2 + 2 * G)
    each(NA, lambda k: copy_a(k).start())
    recv_a[my_a] = send_a[my_a // 2]
    loads[8].wait()
    loads[10].wait()
    for c in range(ROWS):
        cols = slice(c * LANES, (c + 1) * LANES)
        for q in range(2):
            table_send[q, c : c + 1, :] = rates[2 + q : 3 + q, cols]
    table_send[2] = step[...].astype(F32)
    for m in range(1, G):
        upstream(m).start()
    table[0] = table_send[...]

    for i in (4, 3, 7, 9, 11):
        loads[i].wait()
    flat = trans[...].reshape(KINDS * PATCH, PATCH)
    t_hi, t_low = split2(flat)
    tmat[:, 0:PATCH] = t_hi.astype(BF16)
    tmat[:, PATCH : 2 * PATCH] = t_hi.astype(BF16)
    tmat[:, 2 * PATCH : 3 * PATCH] = t_low.astype(BF16)

    def transit_chunk(j):
        for kk in range(CHUNK):
            k = j * CHUNK + kk
            hi, low = split2(grown[pl.ds(pl.multiple_of(k * PATCH, PATCH), PATCH), :])
            cols = slice(kk * LANES, (kk + 1) * LANES)
            rhs[0:PATCH, cols] = hi.astype(BF16)
            rhs[PATCH : 2 * PATCH, cols] = low.astype(BF16)
            rhs[2 * PATCH : 3 * PATCH, cols] = hi.astype(BF16)
        moved = nn_dot(tmat[...], rhs[...])
        for kk in range(CHUNK):
            cols = slice(kk * LANES, (kk + 1) * LANES)
            total = moved[0:PATCH, cols] * weight[0:1, :]
            for kind in range(1, KINDS):
                total += moved[kind * PATCH : (kind + 1) * PATCH, cols] * weight[kind : kind + 1, :]
            tr_out[pl.ds(j * CHUNK + kk, PATCH, stride=BINS), :] = total

    lane16 = lax.broadcasted_iota(jnp.int32, (ROWS, LANES), 1)
    stride = step[...]
    path[1] = jnp.where(stride > 0, sub16 * LANES + lane16 + stride, -1)

    def follow(k):
        count = (k + 1) * ROWS
        sub_rows = lax.broadcasted_iota(jnp.int32, (count, LANES), 0)
        if k < G:
            fields = []
            for f in range(3):
                hi, low = split2(jnp.concatenate([table[m, f] for m in range(k + 1)], axis=0))
                fields += [hi, low]
            lookup = jnp.concatenate(fields, axis=0).astype(BF16)

        def piece(i, _):
            for j in range(4):
                c = i * 4 + j
                cells = path[k, pl.ds(c, 1), :]
                cols = pl.ds(pl.multiple_of(c * LANES, LANES), LANES)
                hot = jnp.where(sub128 == (cells & (LANES - 1)), 1.0, 0.0)
                lane_step[k - 1, cols, :] = hot.T.astype(BF16)
                rows = jnp.where(sub_rows == (cells >> 7), 1.0, 0.0)
                row_step[OFF[k - 1] : OFF[k - 1] + count, cols] = rows.astype(BF16)
                if k < G:
                    found = nn_dot(lookup, hot.astype(BF16))
                    values = []
                    for f in range(3):
                        both = found[2 * f * count : (2 * f + 1) * count] + found[(2 * f + 1) * count : (2 * f + 2) * count]
                        values.append(jnp.sum(both * rows, axis=0, keepdims=True))
                    path_rate[k, 0, pl.ds(c, 1), :] = values[0]
                    path_rate[k, 1, pl.ds(c, 1), :] = values[1]
                    hop = (values[2] + 0.5).astype(jnp.int32)
                    path[k + 1, pl.ds(c, 1), :] = jnp.where(hop > 0, cells + hop, -1)
            return 0

        lax.fori_loop(0, 4, piece, 0)

    listed = jnp.zeros((8, LANES), jnp.int32)
    for a in range(NA):
        row = jnp.broadcast_to(tgt[a // 2 : a // 2 + 1, :], (8, LANES))
        row = pltpu.roll(row, ((a - (a % 2) * 8) * 8) % LANES, 1)
        listed = jnp.where(((block8 - sub8) & 15) == a, row, listed)
    for bit in (1, 2, 4):
        listed = jnp.where((sub8 & bit) != 0, pltpu.roll(listed, LANES - bit * 8, 1), listed)
    list_lane = listed & (LANES - 1)
    list_row = listed >> 7
    for b in range(NB):
        cols = slice(b * LANES, (b + 1) * LANES)
        lane_rcv[:, cols] = jnp.where(sub128 == list_lane[b : b + 1, :], 1.0, 0.0).astype(BF16)
        row_rcv[:, cols] = jnp.where(sub16 == list_row[b : b + 1, :], 1.0, 0.0)

    for c in range(ROWS):
        cols = slice(c * LANES, (c + 1) * LANES)
        for q in range(4):
            state[q, c : c + 1, :] = water[q : q + 1, cols]
            state[4 + q, c : c + 1, :] = rates[q : q + 1, cols]
    for m in range(1, G):
        upstream(m).wait_recv()
    for k in range(1, A_PATHS):
        follow(k)

    each(NA, lambda k: arrive_a(k).wait_recv())
    half = my_a % 2
    tiles = []
    for a in range(NA):
        tiles.append(pltpu.roll(recv_a[a], (half * 64 + a * 8) % LANES, 1))
    for b in range(NB):
        mixed = jnp.zeros((8, LANES), F32)
        for a in range(NA):
            mixed = jnp.where(block8 == (a + b) % 16, tiles[a], mixed)
        send_b[b] = pltpu.roll(mixed, (LANES - b * 8) % LANES, 1)
    each(NB, lambda k: copy_b(k).start())
    recv_b[my_b] = send_b[my_b]
    for k in range(A_PATHS, G + 1):
        follow(k)
    for q in range(2):
        rate = [table[0, q]] + [path_rate[k, q] for k in range(1, G)]
        before = None
        for k in range(G + 1):
            now = {}
            for n in range(k, G + 1):
                if k == 0:
                    value = (1.0 - rate[0]) * now[n - 1] if n else jnp.ones((ROWS, LANES), F32)
                else:
                    value = rate[k - 1] * before[n - 1]
                    if n > k:
                        value += (1.0 - rate[k]) * now[n - 1]
                now[n] = value
                moved_by[q, k, n] = value
            before = now
    each(NB, lambda k: arrive_b(k).wait_recv())

    for b in range(NB):
        cols = slice(b * LANES, (b + 1) * LANES)
        hot = row_rcv[:, cols]
        for s, part in enumerate(split3(recv_b[b])):
            for f in range(3):
                lhs_rcv[(s * 3 + f) * ROWS : (s * 3 + f + 1) * ROWS, cols] = (part[f : f + 1, :] * hot).astype(BF16)
    landed = nt_dot(lhs_rcv[...], lane_rcv[...])
    landed = (landed[0:48] + landed[48:96] + landed[96:144]) * (1.0 / NSUB)
    surface = (landed[0:ROWS], landed[ROWS : 2 * ROWS])
    deep = (landed[2 * ROWS : 3 * ROWS], jnp.zeros((ROWS, LANES), F32))

    def macro_step(e, carry):
        hill, channel = carry[0:2], carry[2:4]
        hill_next, kept = [], []
        for q in range(2):
            water_now = hill[q]
            given = []
            for _ in range(G):
                hill_out = state[4 + q] * water_now
                given.append(hill_out + deep[q])
                water_now = water_now - hill_out + surface[q]
            hill_next.append(water_now)
            for k in range(G + 1):
                total = moved_by[q, k, G] * channel[q]
                for n in range(k, G):
                    total += moved_by[q, k, n] * given[G - 1 - n]
                if k == 0:
                    kept.append(total)
                    continue
                for s, part in enumerate(split2(total)):
                    start = 4 * OFF[k - 1] + (q * 2 + s) * (k + 1) * ROWS
                    for c in range(ROWS):
                        cols = slice(c * LANES, (c + 1) * LANES)
                        value = jnp.broadcast_to(part[c : c + 1, :], (ROWS, LANES)).astype(BF16)
                        value = jnp.concatenate([value] * (k + 1), axis=0)
                        lhs_step[start : start + (k + 1) * ROWS, cols] = value * row_step[OFF[k - 1] : OFF[k], cols]
        sums = [[0.0] * (G + 1) for _ in range(2)]
        for k in range(G, 0, -1):
            spread = nn_dot(lhs_step[4 * OFF[k - 1] : 4 * OFF[k], :], lane_step[k - 1])
            count = (k + 1) * ROWS
            for q in range(2):
                both = spread[2 * q * count : (2 * q + 1) * count] + spread[(2 * q + 1) * count : (2 * q + 2) * count]
                for m in range(k + 1):
                    sums[q][m] = sums[q][m] + both[m * ROWS : (m + 1) * ROWS]
        for m in range(G, 0, -1):
            for q in range(2):
                send_ring[e, m - 1, q] = sums[q][m]
            ring(e, m).start()
        for j in range(CHUNKS_STEP):
            transit_chunk(e * CHUNKS_STEP + j)
        new = [kept[q] + sums[q][0] for q in range(2)]
        for m in range(1, G + 1):
            ring(e, m).wait_recv()
            for q in range(2):
                new[q] = new[q] + recv_ring[e, m - 1, q]
        return (*hill_next, *new)

    final = lax.fori_loop(0, STEPS, macro_step, tuple(state[q] for q in range(4)))
    stored = final[2] + final[3]
    inundation = stored / (stored + cap[...])
    lhs = jnp.concatenate(split3(inundation), axis=0).astype(BF16)
    seen = nn_dot(lhs, lane_rcv[...])
    seen = (seen[0:16] + seen[16:32] + seen[32:48]) * row_rcv[...]
    for b in range(NB):
        row = jnp.sum(seen[:, b * LANES : (b + 1) * LANES], axis=0, keepdims=True)
        send_rb[b] = jnp.broadcast_to(row, (8, LANES))
    each(NB, lambda k: copy_rb(k).start())
    recv_rb[my_b] = send_rb[my_b]
    for c in range(ROWS):
        cols = slice(c * LANES, (c + 1) * LANES)
        for q in range(4):
            river_out[q : q + 1, cols] = final[q][c : c + 1, :]
    for j in range(CHUNKS_STEP * STEPS, BINS // CHUNK):
        transit_chunk(j)
    stores = (
        pltpu.make_async_copy(tr_out, tr_hbm, out_sem.at[0]),
        pltpu.make_async_copy(river_out, river_hbm, out_sem.at[1]),
    )
    for copy in stores:
        copy.start()
    each(NB, lambda k: arrive_rb(k).wait_recv())
    gathered = jnp.zeros((8, LANES), F32)
    for b in range(NB):
        gathered = jnp.where(sub8 == b, recv_rb[b], gathered)
    send_ra[...] = gathered
    each(NA, lambda k: copy_ra(k).start())
    recv_ra[my_a] = gathered
    each(NA, lambda k: arrive_ra(k).wait_recv())
    for r in range(8):
        even = pltpu.roll(recv_ra[2 * r], (LANES - my_a * 8) % LANES, 1)
        odd = pltpu.roll(recv_ra[2 * r + 1], (64 + LANES - my_a * 8) % LANES, 1)
        pair = jnp.where(lane8 < 64, even, odd)
        for bit in (1, 2, 4):
            pair = jnp.where((sub8 & bit) != 0, pltpu.roll(pair, bit * 8, 1), pair)
        row = jnp.sum(jnp.where((block8 & 7) == sub8, pair, 0.0), axis=0, keepdims=True) * share[r : r + 1, :]
        hi, mid, low = split3(row)
        tile = jnp.where(sub16 == 0, hi, jnp.where(sub16 == 1, mid, jnp.where(sub16 == 2, low, 0.0)))
        lhs_back[:, r * LANES : (r + 1) * LANES] = tile.astype(BF16)
    felt = nt_dot(lhs_back[...], onehot_src[...])
    flood_out[...] = felt[0:1] + felt[1:2] + felt[2:3]
    store = pltpu.make_async_copy(flood_out, flood_hbm, out_sem.at[2])
    store.start()

    each(NA, lambda k: copy_a(k).wait_send())
    each(NB, lambda k: copy_b(k).wait_send())
    each(NB, lambda k: copy_rb(k).wait_send())
    each(NA, lambda k: copy_ra(k).wait_send())

    for m in range(1, G):
        upstream(m).wait_send()
    for e in range(STEPS):
        for m in range(1, G + 1):
            ring(e, m).wait_send()
    for copy in (*stores, store):
        copy.wait()


def survive_kernel(
    mass_in, traits_in, flooded_in, river_in, out, flooded_out, river_out,
    mass, traits, flooded, survival, load_sem, store_sem,
):
    block = PATCH * BINS // 6
    small = [
        pltpu.make_async_copy(flooded_in, flooded, load_sem.at[6]),
        pltpu.make_async_copy(traits_in, traits, load_sem.at[7]),
    ]
    pieces = [pl.ds(i * block, block) for i in range(6)]
    loads = [pltpu.make_async_copy(mass_in.at[p, :], mass.at[p, :], load_sem.at[i]) for i, p in enumerate(pieces)]
    stores = [pltpu.make_async_copy(mass.at[p, :], out.at[p, :], store_sem.at[i]) for i, p in enumerate(pieces)]
    stores += [
        pltpu.make_async_copy(flooded, flooded_out, store_sem.at[6]),
        pltpu.make_async_copy(river_in, river_out, store_sem.at[7]),
    ]
    for copy in (*small, *loads, stores[7]):
        copy.start()
    for copy in small:
        copy.wait()
    stores[6].start()
    rows = lax.broadcasted_iota(jnp.int32, (BINS, BINS), 0)
    cols = lax.broadcasted_iota(jnp.int32, (BINS, BINS), 1)
    mortality = jnp.sum(jnp.where(rows == cols, traits[3:4, :], 0.0), axis=1, keepdims=True)
    survival[...] = jnp.exp(-mortality * flooded[...])
    for i in range(6):
        loads[i].wait()
        for p in range(8):
            rows = slice(i * block + p * BINS, i * block + (p + 1) * BINS)
            mass[rows, :] = mass[rows, :] * survival[...]
        stores[i].start()
    for copy in stores:
        copy.wait()


def shards(
    biomass, patch_area, cohort_traits, cell_forcing, disturb_weight, transitions, land_source, pair_share,
    river_target, downstream_step, river_water, river_rates, capacity,
):
    hbm = pl.BlockSpec(memory_space=pltpu.HBM)
    dma = pltpu.SemaphoreType.DMA
    tile = (8, LANES)
    n_rows = PATCH * BINS
    transited, flooded, river_state = pl.pallas_call(
        main_kernel,
        out_shape=(
            jax.ShapeDtypeStruct((n_rows, LANES), F32),
            jax.ShapeDtypeStruct((1, LANES), F32),
            jax.ShapeDtypeStruct((4, ROWS * LANES), F32),
        ),
        in_specs=[hbm] * 13,
        out_specs=(hbm, hbm, hbm),
        scratch_shapes=[
            pltpu.VMEM((n_rows, LANES), F32),
            pltpu.VMEM((1, LANES), F32),
            pltpu.VMEM((4, ROWS * LANES), F32),
            dma((3,)),
            pltpu.VMEM((BINS // 8, PATCH, 8, LANES), F32),
            pltpu.VMEM((PATCH, LANES), F32),
            pltpu.SMEM((4, BINS), F32),
            pltpu.VMEM((5, LANES), F32),
            pltpu.VMEM((KINDS, LANES), F32),
            pltpu.VMEM((KINDS, PATCH, PATCH), F32),
            pltpu.VMEM(tile, jnp.int32),
            pltpu.VMEM(tile, F32),
            pltpu.VMEM(tile, jnp.int32),
            pltpu.VMEM((ROWS, LANES), jnp.int32),
            pltpu.VMEM((4, ROWS * LANES), F32),
            pltpu.VMEM((4, ROWS * LANES), F32),
            pltpu.VMEM((ROWS, LANES), F32),
            dma((12,)),
            dma((BINS // 8,)),
            pltpu.VMEM((n_rows, LANES), F32),
            pltpu.VMEM((KINDS * PATCH, 3 * PATCH), BF16),
            pltpu.VMEM((3 * PATCH, CHUNK * LANES), BF16),
            pltpu.VMEM((LANES, 1024), BF16),
            pltpu.VMEM((LANES, 1024), BF16),
            pltpu.VMEM((ROWS, 1024), F32),
            pltpu.VMEM((G, ROWS * LANES, LANES), BF16),
            pltpu.VMEM((OFF[G], ROWS * LANES), BF16),
            pltpu.VMEM((4 * OFF[G], ROWS * LANES), BF16),
            pltpu.VMEM((9 * ROWS, 1024), BF16),
            pltpu.VMEM((16, 1024), BF16),
            pltpu.VMEM((8, ROWS, LANES), F32),
            pltpu.VMEM((2, G + 1, G + 1, ROWS, LANES), F32),
            pltpu.VMEM((G, 3, ROWS, LANES), F32),
            pltpu.VMEM((3, ROWS, LANES), F32),
            pltpu.VMEM((G + 1, ROWS, LANES), jnp.int32),
            pltpu.VMEM((G, 2, ROWS, LANES), F32),
            dma((G,)), dma((G,)),
            pltpu.VMEM((8, *tile), F32),
            pltpu.VMEM((NA, *tile), F32),
            pltpu.VMEM((NB, *tile), F32),
            pltpu.VMEM((NB, *tile), F32),
            pltpu.VMEM((NB, *tile), F32),
            pltpu.VMEM((NB, *tile), F32),
            pltpu.VMEM(tile, F32),
            pltpu.VMEM((NA, *tile), F32),
            pltpu.VMEM((STEPS, G, 2, ROWS, LANES), F32),
            pltpu.VMEM((STEPS, G, 2, ROWS, LANES), F32),
            dma((NA,)), dma((NA,)), dma((NB,)), dma((NB,)), dma((NB,)), dma((NB,)), dma((NA,)), dma((NA,)),
            dma((STEPS, G)), dma((STEPS, G)),
        ],
        compiler_params=pltpu.CompilerParams(
            collective_id=0, has_side_effects=True, vmem_limit_bytes=60 * 1024 * 1024),
        name="hour",
    )(
        biomass, patch_area, cohort_traits, cell_forcing, disturb_weight, transitions,
        land_source.reshape(8, LANES), pair_share.reshape(8, LANES), river_target.reshape(8, LANES),
        downstream_step.reshape(ROWS, LANES), river_water, river_rates, capacity.reshape(ROWS, LANES),
    )
    new_biomass, flooded, river_state = pl.pallas_call(
        survive_kernel,
        out_shape=(
            jax.ShapeDtypeStruct((n_rows, LANES), F32),
            jax.ShapeDtypeStruct((1, LANES), F32),
            jax.ShapeDtypeStruct((4, ROWS * LANES), F32),
        ),
        in_specs=[hbm] * 4,
        out_specs=(hbm, hbm, hbm),
        scratch_shapes=[
            pltpu.VMEM((n_rows, LANES), F32),
            pltpu.VMEM((4, BINS), F32),
            pltpu.VMEM((1, LANES), F32),
            pltpu.VMEM((BINS, LANES), F32),
            dma((8,)),
            dma((8,)),
        ],
        compiler_params=pltpu.CompilerParams(vmem_limit_bytes=60 * 1024 * 1024),
        name="survive",
    )(transited, cohort_traits, flooded, river_state)
    return new_biomass.reshape(PATCH, BINS, LANES), flooded.reshape(LANES), river_state


def solution(mesh):
    both = ("comp", "cell")
    return jax.shard_map(
        shards,
        mesh=mesh,
        in_specs=(
            P(None, None, both), P(None, both), P(), P(None, both), P(None, both), P(), P(both), P(both), P(both),
            P(both), P(None, both), P(None, both), P(both),
        ),
        out_specs=(P(None, None, both), P(both), P(None, both)),
        check_vma=False,
    )
```

```python
import jax
import jax.numpy as jnp
from jax import lax
from jax.experimental import pallas as pl
from jax.experimental.pallas import tpu as pltpu
from jax.sharding import PartitionSpec as P

MESH = pl.DeviceIdType.MESH
F32 = jnp.float32
BF16 = jnp.bfloat16

NSUB = 12
PATCH = 48
BINS = 64
KINDS = 4
LANES = 128
NA = 16
NB = 8
ROWS = 16
CHUNK = 4
G = 6
STEPS = NSUB // G
CHUNKS_STEP = 12 // STEPS
UNROLL = True
EARLY = False
A_PATHS = 3
WIDE = 2 * LANES
PAD = [0] + [(k + 2) // 2 * 16 for k in range(1, G + 1)]
OFF = [sum(PAD[: k + 1]) for k in range(G + 1)]


def far_first(axes):
    offsets = [()]
    for size in axes:
        offsets = [(*o, d) for o in offsets for d in range(size)]
    return sorted(offsets, key=lambda o: -sum(min(d, n - d) if n > 2 else 0.3 * d for d, n in zip(o, axes)))[:-1]


FAR_A = far_first((4, 4))
FAR_B = far_first((4, 2))


def split2(x):
    hi = x.astype(BF16).astype(F32)
    return hi, x - hi


def split3(x):
    hi, rest = split2(x)
    mid, low = split2(rest)
    return hi, mid, low


def nt_dot(a, b):
    return lax.dot_general(a, b, (((1,), (1,)), ((), ())), preferred_element_type=F32)


def nn_dot(a, b):
    return jnp.dot(a, b, preferred_element_type=F32)


def main_kernel(
    bio_in, area_in, traits_in, forcing_in, weight_in, trans_in, src_in, share_in, tgt_in, step_in, water_in, rates_in,
    cap_in,
    tr_hbm, flood_hbm, river_hbm,
    tr_out, flood_out, river_out, out_sem,
    bio, area, traits, forcing, weight, trans, src, share, tgt, step, water, rates, cap, in_sem, bio_sem,
    grown, tmat, rhs, onehot_src, lane_rcv, row_rcv, lane_step, row_step, lhs_step, lhs_rcv, lhs_back, state,
    fold, moved_by, table, table_send, path, path_rate, st_s, st_r,
    send_a, recv_a, send_b, recv_b, send_rb, recv_rb, send_ra, recv_ra, send_ring, recv_ring,
    sa_s, sa_r, sb_s, sb_r, rb_s, rb_r, ra_s, ra_r, ring_s, ring_r,
):
    sources = (area_in, traits_in, forcing_in, weight_in, trans_in, src_in, share_in, tgt_in, step_in, water_in, rates_in, cap_in)
    targets = (area, traits, forcing, weight, trans, src, share, tgt, step, water, rates, cap)
    loads = [pltpu.make_async_copy(sources[i], targets[i], in_sem.at[i]) for i in range(12)]
    for i in (5, 1, 2):
        loads[i].start()
    mass_loads = [
        pltpu.make_async_copy(bio_in.at[:, pl.ds(g * 8, 8), :], bio.at[g], bio_sem.at[g]) for g in range(BINS // 8)
    ]
    for g in range(BINS // 8 - 1, -1, -1):
        mass_loads[g].start()
    for i in (0, 6, 4, 3, 8, 7, 9, 10, 11):
        loads[i].start()
    my_x = lax.axis_index("comp")
    cell = lax.axis_index("cell")
    my_y, my_b = cell // NB, cell % NB
    my_a = my_x * 4 + my_y
    me = my_x * 32 + cell

    def peer_a(other):
        return (other // 4, (other % 4) * NB + my_b)

    def peer_b(other):
        return (my_x, my_y * NB + other)

    barrier = pltpu.get_barrier_semaphore()

    def greet_a(k, _):
        pl.semaphore_signal(barrier, inc=1, device_id=peer_a((my_a + k) % NA), device_id_type=MESH)
        return 0

    def greet_b(k, _):
        pl.semaphore_signal(barrier, inc=1, device_id=peer_b((my_b + k) % NB), device_id_type=MESH)
        return 0

    lax.fori_loop(1, NA, greet_a, 0)
    lax.fori_loop(1, NB, greet_b, 0)
    for m in range(1, G + 1):
        for other in ((me + m) % 128, (me + 128 - m) % 128):
            pl.semaphore_signal(barrier, inc=1, device_id=(other // 32, other % 32), device_id_type=MESH)

    sub8 = lax.broadcasted_iota(jnp.int32, (8, LANES), 0)
    lane8 = lax.broadcasted_iota(jnp.int32, (8, LANES), 1)
    block8 = lane8 >> 3
    sub16 = lax.broadcasted_iota(jnp.int32, (16, LANES), 0)
    sub128 = lax.broadcasted_iota(jnp.int32, (LANES, LANES), 0)

    loads[5].wait()
    for r in range(8):
        hot = jnp.where(sub128 == src[r : r + 1, :], 1.0, 0.0)
        onehot_src[:, r * LANES : (r + 1) * LANES] = hot.astype(BF16)

    loads[1].wait()
    loads[2].wait()
    light = forcing[0:1, :]
    light_factor = light / (light + 0.5)

    zero48 = jnp.zeros((PATCH, LANES), F32)
    carry = (zero48, zero48)
    for g in range(BINS // 8 - 1, -1, -1):
        mass_loads[g].wait()
        group = bio.at[g].reshape(PATCH * 8, LANES)

        def canopy_bin(i, carry, g=g, group=group):
            above, total = carry
            kk = 7 - i
            k = g * 8 + kk
            mass = group[pl.ds(kk, PATCH, stride=8), :]
            leaf = mass * traits[0, k]
            gain = (traits[1, k] * light_factor) * leaf * jnp.exp(-0.05 * above)
            grown[pl.ds(pl.multiple_of(k * PATCH, PATCH), PATCH), :] = mass * (1.0 - 0.1 * traits[2, k]) + 0.5 * gain
            return above + leaf, total + gain

        carry = lax.fori_loop(0, 8, canopy_bin, carry, unroll=True)
    total = carry[1]
    loads[0].wait()
    transpiration = 0.5 * jnp.sum(area[...] * total, axis=0, keepdims=True)
    wet = forcing[1:2, :] * forcing[2:3, :]
    frozen = forcing[4:5, :]
    row0 = wet * (1.0 - frozen)
    row1 = wet * frozen
    row2 = forcing[3:4, :] * jnp.exp(-0.5 * transpiration)
    runoff = jnp.where(sub8 == 0, row0, jnp.where(sub8 == 1, row1, jnp.where(sub8 == 2, row2, 0.0)))
    parts = split3(runoff)
    lhs = jnp.concatenate([*parts, jnp.zeros((8, LANES), F32)], axis=0).astype(BF16)
    loads[6].wait()
    picked = nn_dot(lhs, onehot_src[...])
    picked = picked[0:8] + picked[8:16] + picked[16:24]
    for r in range(8):
        send_a[r] = picked[:, r * LANES : (r + 1) * LANES] * share[r : r + 1, :]

    def at_a(k):
        dx, dy = FAR_A[k - 1]
        return (my_x + dx) % 4 * 4 + (my_y + dy) % 4

    def at_b(k):
        dz, dc = FAR_B[k - 1]
        return (my_b // 2 + dz) % 4 * 2 + (my_b + dc) % 2

    def copy_a(k):
        other = at_a(k)
        return pltpu.make_async_remote_copy(
            src_ref=send_a.at[other // 2], dst_ref=recv_a.at[my_a], send_sem=sa_s.at[k], recv_sem=sa_r.at[my_a],
            device_id=peer_a(other), device_id_type=MESH)

    def arrive_a(k):
        other = at_a(k)
        return pltpu.make_async_remote_copy(
            src_ref=send_a.at[0], dst_ref=recv_a.at[other], send_sem=sa_s.at[k], recv_sem=sa_r.at[other],
            device_id=peer_a(other), device_id_type=MESH)

    def copy_b(k):
        other = at_b(k)
        return pltpu.make_async_remote_copy(
            src_ref=send_b.at[other], dst_ref=recv_b.at[my_b], send_sem=sb_s.at[k], recv_sem=sb_r.at[my_b],
            device_id=peer_b(other), device_id_type=MESH)

    def arrive_b(k):
        other = at_b(k)
        return pltpu.make_async_remote_copy(
            src_ref=send_b.at[other], dst_ref=recv_b.at[other], send_sem=sb_s.at[k], recv_sem=sb_r.at[other],
            device_id=peer_b(other), device_id_type=MESH)

    def copy_rb(k):
        other = at_b(k)
        return pltpu.make_async_remote_copy(
            src_ref=send_rb.at[other], dst_ref=recv_rb.at[my_b], send_sem=rb_s.at[k], recv_sem=rb_r.at[my_b],
            device_id=peer_b(other), device_id_type=MESH)

    def arrive_rb(k):
        other = at_b(k)
        return pltpu.make_async_remote_copy(
            src_ref=send_rb.at[other], dst_ref=recv_rb.at[other], send_sem=rb_s.at[k], recv_sem=rb_r.at[other],
            device_id=peer_b(other), device_id_type=MESH)

    def copy_ra(k):
        other = at_a(k)
        return pltpu.make_async_remote_copy(
            src_ref=send_ra, dst_ref=recv_ra.at[my_a], send_sem=ra_s.at[k], recv_sem=ra_r.at[my_a],
            device_id=peer_a(other), device_id_type=MESH)

    def arrive_ra(k):
        other = at_a(k)
        return pltpu.make_async_remote_copy(
            src_ref=send_ra, dst_ref=recv_ra.at[other], send_sem=ra_s.at[k], recv_sem=ra_r.at[other],
            device_id=peer_a(other), device_id_type=MESH)

    def ring(e, m):
        to = (me + m) % 128
        return pltpu.make_async_remote_copy(
            src_ref=send_ring.at[e, m - 1], dst_ref=recv_ring.at[e, m - 1],
            send_sem=ring_s.at[e, m - 1], recv_sem=ring_r.at[e, m - 1],
            device_id=(to // 32, to % 32), device_id_type=MESH)

    def upstream(m):
        to = (me + 128 - m) % 128
        return pltpu.make_async_remote_copy(
            src_ref=table_send, dst_ref=table.at[m], send_sem=st_s.at[m], recv_sem=st_r.at[m],
            device_id=(to // 32, to % 32), device_id_type=MESH)

    def each(count, action):
        for k in range(1, count):
            action(k)

    pl.semaphore_wait(barrier, NA + NB - 2 + 2 * G)
    each(NA, lambda k: copy_a(k).start())
    recv_a[my_a] = send_a[my_a // 2]
    loads[8].wait()
    loads[10].wait()
    for c in range(ROWS):
        cols = slice(c * LANES, (c + 1) * LANES)
        wide = slice(c % 2 * LANES, (c % 2 + 1) * LANES)
        for q in range(2):
            table_send[q, c // 2 : c // 2 + 1, wide] = rates[2 + q : 3 + q, cols]
    for p in range(2):
        table_send[2, :, p * LANES : (p + 1) * LANES] = step[pl.ds(p, 8, stride=2), :].astype(F32)
    for m in range(1, G):
        upstream(m).start()
    table[0] = table_send[...]

    for i in (4, 3, 7, 9, 11):
        loads[i].wait()
    flat = trans[...].reshape(KINDS * PATCH, PATCH)
    t_hi, t_low = split2(flat)
    tmat[:, 0:PATCH] = t_hi.astype(BF16)
    tmat[:, PATCH : 2 * PATCH] = t_hi.astype(BF16)
    tmat[:, 2 * PATCH : 3 * PATCH] = t_low.astype(BF16)

    def transit_chunk(j):
        for kk in range(CHUNK):
            k = j * CHUNK + kk
            hi, low = split2(grown[pl.ds(pl.multiple_of(k * PATCH, PATCH), PATCH), :])
            cols = slice(kk * LANES, (kk + 1) * LANES)
            rhs[0:PATCH, cols] = hi.astype(BF16)
            rhs[PATCH : 2 * PATCH, cols] = low.astype(BF16)
            rhs[2 * PATCH : 3 * PATCH, cols] = hi.astype(BF16)
        moved = nn_dot(tmat[...], rhs[...])
        for kk in range(CHUNK):
            cols = slice(kk * LANES, (kk + 1) * LANES)
            total = moved[0:PATCH, cols] * weight[0:1, :]
            for kind in range(1, KINDS):
                total += moved[kind * PATCH : (kind + 1) * PATCH, cols] * weight[kind : kind + 1, :]
            tr_out[pl.ds(j * CHUNK + kk, PATCH, stride=BINS), :] = total

    lane16 = lax.broadcasted_iota(jnp.int32, (ROWS, LANES), 1)
    stride = step[...]
    path[1] = jnp.where(stride > 0, sub16 * LANES + lane16 + stride, -1)

    sub256 = lax.broadcasted_iota(jnp.int32, (WIDE, LANES), 0)

    def follow(k):
        count = (k + 1) * 8
        sub_rows = lax.broadcasted_iota(jnp.int32, (PAD[k], LANES), 0)
        if k < G:
            fields = []
            for f in range(3):
                hi, low = split2(jnp.concatenate([table[m, f] for m in range(k + 1)], axis=0))
                fields += [hi, low]
            lookup = jnp.concatenate(fields, axis=0).astype(BF16)

        def piece(i, _):
            for j in range(4):
                c = i * 4 + j
                cells = path[k, pl.ds(c, 1), :]
                cols = pl.ds(pl.multiple_of(c * LANES, LANES), LANES)
                hot = jnp.where(sub256 == (cells & (WIDE - 1)), 1.0, 0.0).astype(BF16)
                lane_step[k - 1, :, cols] = hot
                rows = jnp.where(sub_rows == (cells >> 8), 1.0, 0.0)
                row_step[OFF[k - 1] : OFF[k], cols] = rows.astype(BF16)
                if k < G:
                    found = nn_dot(lookup, hot)
                    values = []
                    for f in range(3):
                        both = found[2 * f * count : (2 * f + 1) * count] + found[(2 * f + 1) * count : (2 * f + 2) * count]
                        values.append(jnp.sum(both * rows[:count], axis=0, keepdims=True))
                    path_rate[k, 0, pl.ds(c, 1), :] = values[0]
                    path_rate[k, 1, pl.ds(c, 1), :] = values[1]
                    hop = (values[2] + 0.5).astype(jnp.int32)
                    path[k + 1, pl.ds(c, 1), :] = jnp.where(hop > 0, cells + hop, -1)
            return 0

        lax.fori_loop(0, 4, piece, 0, unroll=UNROLL)

    listed = jnp.zeros((8, LANES), jnp.int32)
    for a in range(NA):
        row = jnp.broadcast_to(tgt[a // 2 : a // 2 + 1, :], (8, LANES))
        row = pltpu.roll(row, ((a - (a % 2) * 8) * 8) % LANES, 1)
        listed = jnp.where(((block8 - sub8) & 15) == a, row, listed)
    for bit in (1, 2, 4):
        listed = jnp.where((sub8 & bit) != 0, pltpu.roll(listed, LANES - bit * 8, 1), listed)
    list_lane = listed & (LANES - 1)
    list_row = listed >> 7
    for b in range(NB):
        cols = slice(b * LANES, (b + 1) * LANES)
        lane_rcv[:, cols] = jnp.where(sub128 == list_lane[b : b + 1, :], 1.0, 0.0).astype(BF16)
        row_rcv[:, cols] = jnp.where(sub16 == list_row[b : b + 1, :], 1.0, 0.0)

    for c in range(ROWS):
        cols = slice(c * LANES, (c + 1) * LANES)
        for q in range(4):
            state[q, c : c + 1, :] = water[q : q + 1, cols]
            state[4 + q, c : c + 1, :] = rates[q : q + 1, cols]
    for m in range(1, G):
        upstream(m).wait_recv()
    for k in range(1, A_PATHS):
        follow(k)

    each(NA, lambda k: arrive_a(k).wait_recv())
    half = my_a % 2
    tiles = []
    for a in range(NA):
        tiles.append(pltpu.roll(recv_a[a], (half * 64 + a * 8) % LANES, 1))
    for b in range(NB):
        mixed = jnp.zeros((8, LANES), F32)
        for a in range(NA):
            mixed = jnp.where(block8 == (a + b) % 16, tiles[a], mixed)
        send_b[b] = pltpu.roll(mixed, (LANES - b * 8) % LANES, 1)
    each(NB, lambda k: copy_b(k).start())
    recv_b[my_b] = send_b[my_b]
    for k in range(A_PATHS, G + 1):
        follow(k)
    for q in range(2):
        rate = [state[6 + q]] + [path_rate[k, q] for k in range(1, G)]
        before = None
        for k in range(G + 1):
            now = {}
            for n in range(k, G + 1):
                if k == 0:
                    value = (1.0 - rate[0]) * now[n - 1] if n else jnp.ones((ROWS, LANES), F32)
                else:
                    value = rate[k - 1] * before[n - 1]
                    if n > k:
                        value += (1.0 - rate[k]) * now[n - 1]
                now[n] = value
                moved_by[q, k, n] = value
            before = now
    each(NB, lambda k: arrive_b(k).wait_recv())

    for b in range(NB):
        cols = slice(b * LANES, (b + 1) * LANES)
        hot = row_rcv[:, cols]
        for s, part in enumerate(split3(recv_b[b])):
            for f in range(3):
                lhs_rcv[(s * 3 + f) * ROWS : (s * 3 + f + 1) * ROWS, cols] = (part[f : f + 1, :] * hot).astype(BF16)
    landed = nt_dot(lhs_rcv[...], lane_rcv[...])
    landed = (landed[0:48] + landed[48:96] + landed[96:144]) * (1.0 / NSUB)
    surface = (landed[0:ROWS], landed[ROWS : 2 * ROWS])
    deep = (landed[2 * ROWS : 3 * ROWS], jnp.zeros((ROWS, LANES), F32))

    def macro_step(e, carry):
        hill, channel = carry[0:2], carry[2:4]
        hill_next, kept, masses = [], [], [{}, {}]
        for q in range(2):
            water_now = hill[q]
            given = []
            for _ in range(G):
                hill_out = state[4 + q] * water_now
                given.append(hill_out + deep[q])
                water_now = water_now - hill_out + surface[q]
            hill_next.append(water_now)
            for k in range(G + 1):
                total = moved_by[q, k, G] * channel[q]
                for n in range(k, G):
                    total += moved_by[q, k, n] * given[G - 1 - n]
                if k == 0:
                    kept.append(total)
                    continue
                masses[q][k] = total
        sums = [[0.0] * (G + 1) for _ in range(2)]

        def send(m):
            for q in range(2):
                send_ring[e, m - 1, q] = sums[q][m]
            ring(e, m).start()

        for k in range(G, 0, -1):
            pad = PAD[k]
            for q in range(2):
                for s, part in enumerate(split2(masses[q][k])):
                    start = 4 * OFF[k - 1] + (q * 2 + s) * pad
                    for c in range(ROWS):
                        cols = slice(c * LANES, (c + 1) * LANES)
                        value = jnp.broadcast_to(part[c : c + 1, :], (16, LANES)).astype(BF16)
                        value = jnp.concatenate([value] * (pad // 16), axis=0)
                        lhs_step[start : start + pad, cols] = value * row_step[OFF[k - 1] : OFF[k], cols]
            spread = nt_dot(lhs_step[4 * OFF[k - 1] : 4 * OFF[k], :], lane_step[k - 1])
            for q in range(2):
                both = spread[2 * q * pad : (2 * q + 1) * pad] + spread[(2 * q + 1) * pad : (2 * q + 2) * pad]
                for m in range(k + 1):
                    sums[q][m] = sums[q][m] + both[m * 8 : (m + 1) * 8]
            if EARLY:
                send(k)
        if not EARLY:
            for m in range(G, 0, -1):
                send(m)
        for j in range(CHUNKS_STEP):
            transit_chunk(e * CHUNKS_STEP + j)
        came = [sums[q][0] for q in range(2)]
        for m in range(1, G + 1):
            ring(e, m).wait_recv()
            for q in range(2):
                came[q] = came[q] + recv_ring[e, m - 1, q]
        for q in range(2):
            fold[q, pl.ds(0, 8, stride=2), :] = came[q][:, :LANES]
            fold[q, pl.ds(1, 8, stride=2), :] = came[q][:, LANES:]
        new = [kept[q] + fold[q] for q in range(2)]
        return (*hill_next, *new)

    final = lax.fori_loop(0, STEPS, macro_step, tuple(state[q] for q in range(4)))
    stored = final[2] + final[3]
    inundation = stored / (stored + cap[...])
    lhs = jnp.concatenate(split3(inundation), axis=0).astype(BF16)
    seen = nn_dot(lhs, lane_rcv[...])
    seen = (seen[0:16] + seen[16:32] + seen[32:48]) * row_rcv[...]
    for b in range(NB):
        row = jnp.sum(seen[:, b * LANES : (b + 1) * LANES], axis=0, keepdims=True)
        send_rb[b] = jnp.broadcast_to(row, (8, LANES))
    each(NB, lambda k: copy_rb(k).start())
    recv_rb[my_b] = send_rb[my_b]
    for c in range(ROWS):
        cols = slice(c * LANES, (c + 1) * LANES)
        for q in range(4):
            river_out[q : q + 1, cols] = final[q][c : c + 1, :]
    for j in range(CHUNKS_STEP * STEPS, BINS // CHUNK):
        transit_chunk(j)
    stores = (
        pltpu.make_async_copy(tr_out, tr_hbm, out_sem.at[0]),
        pltpu.make_async_copy(river_out, river_hbm, out_sem.at[1]),
    )
    for copy in stores:
        copy.start()
    each(NB, lambda k: arrive_rb(k).wait_recv())
    gathered = jnp.zeros((8, LANES), F32)
    for b in range(NB):
        gathered = jnp.where(sub8 == b, recv_rb[b], gathered)
    send_ra[...] = gathered
    each(NA, lambda k: copy_ra(k).start())
    recv_ra[my_a] = gathered
    each(NA, lambda k: arrive_ra(k).wait_recv())
    for r in range(8):
        even = pltpu.roll(recv_ra[2 * r], (LANES - my_a * 8) % LANES, 1)
        odd = pltpu.roll(recv_ra[2 * r + 1], (64 + LANES - my_a * 8) % LANES, 1)
        pair = jnp.where(lane8 < 64, even, odd)
        for bit in (1, 2, 4):
            pair = jnp.where((sub8 & bit) != 0, pltpu.roll(pair, bit * 8, 1), pair)
        row = jnp.sum(jnp.where((block8 & 7) == sub8, pair, 0.0), axis=0, keepdims=True) * share[r : r + 1, :]
        hi, mid, low = split3(row)
        tile = jnp.where(sub16 == 0, hi, jnp.where(sub16 == 1, mid, jnp.where(sub16 == 2, low, 0.0)))
        lhs_back[:, r * LANES : (r + 1) * LANES] = tile.astype(BF16)
    felt = nt_dot(lhs_back[...], onehot_src[...])
    flood_out[...] = felt[0:1] + felt[1:2] + felt[2:3]
    store = pltpu.make_async_copy(flood_out, flood_hbm, out_sem.at[2])
    store.start()

    each(NA, lambda k: copy_a(k).wait_send())
    each(NB, lambda k: copy_b(k).wait_send())
    each(NB, lambda k: copy_rb(k).wait_send())
    each(NA, lambda k: copy_ra(k).wait_send())

    for m in range(1, G):
        upstream(m).wait_send()
    for e in range(STEPS):
        for m in range(1, G + 1):
            ring(e, m).wait_send()
    for copy in (*stores, store):
        copy.wait()


def survive_kernel(
    mass_in, traits_in, flooded_in, river_in, out, flooded_out, river_out,
    mass, traits, flooded, survival, load_sem, store_sem,
):
    block = PATCH * BINS // 6
    small = [
        pltpu.make_async_copy(flooded_in, flooded, load_sem.at[6]),
        pltpu.make_async_copy(traits_in, traits, load_sem.at[7]),
    ]
    pieces = [pl.ds(i * block, block) for i in range(6)]
    loads = [pltpu.make_async_copy(mass_in.at[p, :], mass.at[p, :], load_sem.at[i]) for i, p in enumerate(pieces)]
    stores = [pltpu.make_async_copy(mass.at[p, :], out.at[p, :], store_sem.at[i]) for i, p in enumerate(pieces)]
    stores += [
        pltpu.make_async_copy(flooded, flooded_out, store_sem.at[6]),
        pltpu.make_async_copy(river_in, river_out, store_sem.at[7]),
    ]
    for copy in (*small, *loads, stores[7]):
        copy.start()
    for copy in small:
        copy.wait()
    stores[6].start()
    rows = lax.broadcasted_iota(jnp.int32, (BINS, BINS), 0)
    cols = lax.broadcasted_iota(jnp.int32, (BINS, BINS), 1)
    mortality = jnp.sum(jnp.where(rows == cols, traits[3:4, :], 0.0), axis=1, keepdims=True)
    survival[...] = jnp.exp(-mortality * flooded[...])
    for i in range(6):
        loads[i].wait()
        for p in range(8):
            rows = slice(i * block + p * BINS, i * block + (p + 1) * BINS)
            mass[rows, :] = mass[rows, :] * survival[...]
        stores[i].start()
    for copy in stores:
        copy.wait()


def shards(
    biomass, patch_area, cohort_traits, cell_forcing, disturb_weight, transitions, land_source, pair_share,
    river_target, downstream_step, river_water, river_rates, capacity,
):
    hbm = pl.BlockSpec(memory_space=pltpu.HBM)
    dma = pltpu.SemaphoreType.DMA
    tile = (8, LANES)
    n_rows = PATCH * BINS
    transited, flooded, river_state = pl.pallas_call(
        main_kernel,
        out_shape=(
            jax.ShapeDtypeStruct((n_rows, LANES), F32),
            jax.ShapeDtypeStruct((1, LANES), F32),
            jax.ShapeDtypeStruct((4, ROWS * LANES), F32),
        ),
        in_specs=[hbm] * 13,
        out_specs=(hbm, hbm, hbm),
        scratch_shapes=[
            pltpu.VMEM((n_rows, LANES), F32),
            pltpu.VMEM((1, LANES), F32),
            pltpu.VMEM((4, ROWS * LANES), F32),
            dma((3,)),
            pltpu.VMEM((BINS // 8, PATCH, 8, LANES), F32),
            pltpu.VMEM((PATCH, LANES), F32),
            pltpu.SMEM((4, BINS), F32),
            pltpu.VMEM((5, LANES), F32),
            pltpu.VMEM((KINDS, LANES), F32),
            pltpu.VMEM((KINDS, PATCH, PATCH), F32),
            pltpu.VMEM(tile, jnp.int32),
            pltpu.VMEM(tile, F32),
            pltpu.VMEM(tile, jnp.int32),
            pltpu.VMEM((ROWS, LANES), jnp.int32),
            pltpu.VMEM((4, ROWS * LANES), F32),
            pltpu.VMEM((4, ROWS * LANES), F32),
            pltpu.VMEM((ROWS, LANES), F32),
            dma((12,)),
            dma((BINS // 8,)),
            pltpu.VMEM((n_rows, LANES), F32),
            pltpu.VMEM((KINDS * PATCH, 3 * PATCH), BF16),
            pltpu.VMEM((3 * PATCH, CHUNK * LANES), BF16),
            pltpu.VMEM((LANES, 1024), BF16),
            pltpu.VMEM((LANES, 1024), BF16),
            pltpu.VMEM((ROWS, 1024), F32),
            pltpu.VMEM((G, WIDE, ROWS * LANES), BF16),
            pltpu.VMEM((OFF[G], ROWS * LANES), BF16),
            pltpu.VMEM((4 * OFF[G], ROWS * LANES), BF16),
            pltpu.VMEM((9 * ROWS, 1024), BF16),
            pltpu.VMEM((16, 1024), BF16),
            pltpu.VMEM((8, ROWS, LANES), F32),
            pltpu.VMEM((2, ROWS, LANES), F32),
            pltpu.VMEM((2, G + 1, G + 1, ROWS, LANES), F32),
            pltpu.VMEM((G, 3, 8, WIDE), F32),
            pltpu.VMEM((3, 8, WIDE), F32),
            pltpu.VMEM((G + 1, ROWS, LANES), jnp.int32),
            pltpu.VMEM((G, 2, ROWS, LANES), F32),
            dma((G,)), dma((G,)),
            pltpu.VMEM((8, *tile), F32),
            pltpu.VMEM((NA, *tile), F32),
            pltpu.VMEM((NB, *tile), F32),
            pltpu.VMEM((NB, *tile), F32),
            pltpu.VMEM((NB, *tile), F32),
            pltpu.VMEM((NB, *tile), F32),
            pltpu.VMEM(tile, F32),
            pltpu.VMEM((NA, *tile), F32),
            pltpu.VMEM((STEPS, G, 2, 8, WIDE), F32),
            pltpu.VMEM((STEPS, G, 2, 8, WIDE), F32),
            dma((NA,)), dma((NA,)), dma((NB,)), dma((NB,)), dma((NB,)), dma((NB,)), dma((NA,)), dma((NA,)),
            dma((STEPS, G)), dma((STEPS, G)),
        ],
        compiler_params=pltpu.CompilerParams(
            collective_id=0, has_side_effects=True, vmem_limit_bytes=60 * 1024 * 1024),
        name="hour",
    )(
        biomass, patch_area, cohort_traits, cell_forcing, disturb_weight, transitions,
        land_source.reshape(8, LANES), pair_share.reshape(8, LANES), river_target.reshape(8, LANES),
        downstream_step.reshape(ROWS, LANES), river_water, river_rates, capacity.reshape(ROWS, LANES),
    )
    new_biomass, flooded, river_state = pl.pallas_call(
        survive_kernel,
        out_shape=(
            jax.ShapeDtypeStruct((n_rows, LANES), F32),
            jax.ShapeDtypeStruct((1, LANES), F32),
            jax.ShapeDtypeStruct((4, ROWS * LANES), F32),
        ),
        in_specs=[hbm] * 4,
        out_specs=(hbm, hbm, hbm),
        scratch_shapes=[
            pltpu.VMEM((n_rows, LANES), F32),
            pltpu.VMEM((4, BINS), F32),
            pltpu.VMEM((1, LANES), F32),
            pltpu.VMEM((BINS, LANES), F32),
            dma((8,)),
            dma((8,)),
        ],
        compiler_params=pltpu.CompilerParams(vmem_limit_bytes=60 * 1024 * 1024),
        name="survive",
    )(transited, cohort_traits, flooded, river_state)
    return new_biomass.reshape(PATCH, BINS, LANES), flooded.reshape(LANES), river_state


def solution(mesh):
    both = ("comp", "cell")
    return jax.shard_map(
        shards,
        mesh=mesh,
        in_specs=(
            P(None, None, both), P(None, both), P(), P(None, both), P(None, both), P(), P(both), P(both), P(both),
            P(both), P(None, both), P(None, both), P(both),
        ),
        out_specs=(P(None, None, both), P(both), P(None, both)),
        check_vma=False,
    )
```

```python
import jax
import jax.numpy as jnp
from jax import lax
from jax.experimental import pallas as pl
from jax.experimental.pallas import tpu as pltpu
from jax.sharding import PartitionSpec as P

MESH = pl.DeviceIdType.MESH
F32 = jnp.float32
BF16 = jnp.bfloat16

NSUB = 12
PATCH = 48
BINS = 64
KINDS = 4
LANES = 128
NA = 16
NB = 8
ROWS = 16
CHUNK = 4
G = 6
STEPS = NSUB // G
CHUNKS_STEP = 12 // STEPS
UNROLL = True
EARLY = False
A_PATHS = 3
WIDE = 2 * LANES
PAD = [0] + [(k + 2) // 2 * 16 for k in range(1, G + 1)]
OFF = [sum(PAD[: k + 1]) for k in range(G + 1)]


def far_first(axes):
    offsets = [()]
    for size in axes:
        offsets = [(*o, d) for o in offsets for d in range(size)]
    return sorted(offsets, key=lambda o: -sum(min(d, n - d) if n > 2 else 0.3 * d for d, n in zip(o, axes)))[:-1]


FAR_A = far_first((4, 4))
FAR_B = far_first((4, 2))


def split2(x):
    hi = x.astype(BF16).astype(F32)
    return hi, x - hi


def split3(x):
    hi, rest = split2(x)
    mid, low = split2(rest)
    return hi, mid, low


def nt_dot(a, b):
    return lax.dot_general(a, b, (((1,), (1,)), ((), ())), preferred_element_type=F32)


def nn_dot(a, b):
    return jnp.dot(a, b, preferred_element_type=F32)


def main_kernel(
    bio_in, area_in, traits_in, forcing_in, weight_in, trans_in, src_in, share_in, tgt_in, step_in, water_in, rates_in,
    cap_in,
    tr_hbm, flood_hbm, river_hbm,
    tr_out, flood_out, river_out, out_sem,
    bio, area, traits, forcing, weight, trans, src, share, tgt, step, water, rates, cap, in_sem, bio_sem,
    grown, tmat, rhs, onehot_src, lane_rcv, row_rcv, lane_step, row_step, lhs_step, lhs_rcv, lhs_back, state,
    fold, moved_by, table, table_send, path, path_rate, st_s, st_r,
    send_a, recv_a, send_b, recv_b, send_rb, recv_rb, send_ra, recv_ra, send_ring, recv_ring,
    sa_s, sa_r, sb_s, sb_r, rb_s, rb_r, ra_s, ra_r, ring_s, ring_r,
):
    sources = (area_in, traits_in, forcing_in, weight_in, trans_in, src_in, share_in, tgt_in, step_in, water_in, rates_in, cap_in)
    targets = (area, traits, forcing, weight, trans, src, share, tgt, step, water, rates, cap)
    loads = [pltpu.make_async_copy(sources[i], targets[i], in_sem.at[i]) for i in range(12)]
    for i in (5, 1, 2):
        loads[i].start()
    mass_loads = [
        pltpu.make_async_copy(bio_in.at[:, pl.ds(g * 8, 8), :], bio.at[g], bio_sem.at[g]) for g in range(BINS // 8)
    ]
    for g in range(BINS // 8 - 1, -1, -1):
        mass_loads[g].start()
    for i in (0, 6, 4, 3, 8, 7, 9, 10, 11):
        loads[i].start()
    my_x = lax.axis_index("comp")
    cell = lax.axis_index("cell")
    my_y, my_b = cell // NB, cell % NB
    my_a = my_x * 4 + my_y
    me = my_x * 32 + cell

    def peer_a(other):
        return (other // 4, (other % 4) * NB + my_b)

    def peer_b(other):
        return (my_x, my_y * NB + other)

    barrier = pltpu.get_barrier_semaphore()

    def greet_a(k, _):
        pl.semaphore_signal(barrier, inc=1, device_id=peer_a((my_a + k) % NA), device_id_type=MESH)
        return 0

    def greet_b(k, _):
        pl.semaphore_signal(barrier, inc=1, device_id=peer_b((my_b + k) % NB), device_id_type=MESH)
        return 0

    lax.fori_loop(1, NA, greet_a, 0)
    lax.fori_loop(1, NB, greet_b, 0)
    for m in range(1, G + 1):
        for other in ((me + m) % 128, (me + 128 - m) % 128):
            pl.semaphore_signal(barrier, inc=1, device_id=(other // 32, other % 32), device_id_type=MESH)

    sub8 = lax.broadcasted_iota(jnp.int32, (8, LANES), 0)
    lane8 = lax.broadcasted_iota(jnp.int32, (8, LANES), 1)
    block8 = lane8 >> 3
    sub16 = lax.broadcasted_iota(jnp.int32, (16, LANES), 0)
    sub128 = lax.broadcasted_iota(jnp.int32, (LANES, LANES), 0)

    loads[5].wait()
    for r in range(8):
        hot = jnp.where(sub128 == src[r : r + 1, :], 1.0, 0.0)
        onehot_src[:, r * LANES : (r + 1) * LANES] = hot.astype(BF16)

    loads[1].wait()
    loads[2].wait()
    light = forcing[0:1, :]
    light_factor = light / (light + 0.5)

    zero48 = jnp.zeros((PATCH, LANES), F32)
    carry = (zero48, zero48)
    for g in range(BINS // 8 - 1, -1, -1):
        mass_loads[g].wait()
        group = bio.at[g].reshape(PATCH * 8, LANES)

        def canopy_bin(i, carry, g=g, group=group):
            above, total = carry
            kk = 7 - i
            k = g * 8 + kk
            mass = group[pl.ds(kk, PATCH, stride=8), :]
            leaf = mass * traits[0, k]
            gain = (traits[1, k] * light_factor) * leaf * jnp.exp(-0.05 * above)
            grown[pl.ds(pl.multiple_of(k * PATCH, PATCH), PATCH), :] = mass * (1.0 - 0.1 * traits[2, k]) + 0.5 * gain
            return above + leaf, total + gain

        carry = lax.fori_loop(0, 8, canopy_bin, carry, unroll=True)
    total = carry[1]
    loads[0].wait()
    transpiration = 0.5 * jnp.sum(area[...] * total, axis=0, keepdims=True)
    wet = forcing[1:2, :] * forcing[2:3, :]
    frozen = forcing[4:5, :]
    row0 = wet * (1.0 - frozen)
    row1 = wet * frozen
    row2 = forcing[3:4, :] * jnp.exp(-0.5 * transpiration)
    runoff = jnp.where(sub8 == 0, row0, jnp.where(sub8 == 1, row1, jnp.where(sub8 == 2, row2, 0.0)))
    parts = split3(runoff)
    lhs = jnp.concatenate([*parts, jnp.zeros((8, LANES), F32)], axis=0).astype(BF16)
    loads[6].wait()
    picked = nn_dot(lhs, onehot_src[...])
    picked = picked[0:8] + picked[8:16] + picked[16:24]
    for r in range(8):
        send_a[r] = picked[:, r * LANES : (r + 1) * LANES] * share[r : r + 1, :]

    def at_a(k):
        dx, dy = FAR_A[k - 1]
        return (my_x + dx) % 4 * 4 + (my_y + dy) % 4

    def at_b(k):
        dz, dc = FAR_B[k - 1]
        return (my_b // 2 + dz) % 4 * 2 + (my_b + dc) % 2

    def copy_a(k):
        other = at_a(k)
        return pltpu.make_async_remote_copy(
            src_ref=send_a.at[other // 2], dst_ref=recv_a.at[my_a], send_sem=sa_s.at[k], recv_sem=sa_r.at[my_a],
            device_id=peer_a(other), device_id_type=MESH)

    def arrive_a(k):
        other = at_a(k)
        return pltpu.make_async_remote_copy(
            src_ref=send_a.at[0], dst_ref=recv_a.at[other], send_sem=sa_s.at[k], recv_sem=sa_r.at[other],
            device_id=peer_a(other), device_id_type=MESH)

    def copy_b(k):
        other = at_b(k)
        return pltpu.make_async_remote_copy(
            src_ref=send_b.at[other], dst_ref=recv_b.at[my_b], send_sem=sb_s.at[k], recv_sem=sb_r.at[my_b],
            device_id=peer_b(other), device_id_type=MESH)

    def arrive_b(k):
        other = at_b(k)
        return pltpu.make_async_remote_copy(
            src_ref=send_b.at[other], dst_ref=recv_b.at[other], send_sem=sb_s.at[k], recv_sem=sb_r.at[other],
            device_id=peer_b(other), device_id_type=MESH)

    def copy_rb(k):
        other = at_b(k)
        return pltpu.make_async_remote_copy(
            src_ref=send_rb.at[other], dst_ref=recv_rb.at[my_b], send_sem=rb_s.at[k], recv_sem=rb_r.at[my_b],
            device_id=peer_b(other), device_id_type=MESH)

    def arrive_rb(k):
        other = at_b(k)
        return pltpu.make_async_remote_copy(
            src_ref=send_rb.at[other], dst_ref=recv_rb.at[other], send_sem=rb_s.at[k], recv_sem=rb_r.at[other],
            device_id=peer_b(other), device_id_type=MESH)

    def copy_ra(k):
        other = at_a(k)
        return pltpu.make_async_remote_copy(
            src_ref=send_ra, dst_ref=recv_ra.at[my_a], send_sem=ra_s.at[k], recv_sem=ra_r.at[my_a],
            device_id=peer_a(other), device_id_type=MESH)

    def arrive_ra(k):
        other = at_a(k)
        return pltpu.make_async_remote_copy(
            src_ref=send_ra, dst_ref=recv_ra.at[other], send_sem=ra_s.at[k], recv_sem=ra_r.at[other],
            device_id=peer_a(other), device_id_type=MESH)

    def ring(e, m):
        to = (me + m) % 128
        return pltpu.make_async_remote_copy(
            src_ref=send_ring.at[e, m - 1], dst_ref=recv_ring.at[e, m - 1],
            send_sem=ring_s.at[e, m - 1], recv_sem=ring_r.at[e, m - 1],
            device_id=(to // 32, to % 32), device_id_type=MESH)

    def upstream(m):
        to = (me + 128 - m) % 128
        return pltpu.make_async_remote_copy(
            src_ref=table_send, dst_ref=table.at[m], send_sem=st_s.at[m], recv_sem=st_r.at[m],
            device_id=(to // 32, to % 32), device_id_type=MESH)

    def each(count, action):
        for k in range(1, count):
            action(k)

    pl.semaphore_wait(barrier, NA + NB - 2 + 2 * G)
    each(NA, lambda k: copy_a(k).start())
    recv_a[my_a] = send_a[my_a // 2]
    loads[8].wait()
    loads[10].wait()
    for c in range(ROWS):
        cols = slice(c * LANES, (c + 1) * LANES)
        wide = slice(c % 2 * LANES, (c % 2 + 1) * LANES)
        for q in range(2):
            table_send[q, c // 2 : c // 2 + 1, wide] = rates[2 + q : 3 + q, cols]
    for p in range(2):
        table_send[2, :, p * LANES : (p + 1) * LANES] = step[pl.ds(p, 8, stride=2), :].astype(F32)
    for m in range(1, G):
        upstream(m).start()
    table[0] = table_send[...]

    for i in (4, 3, 7, 9, 11):
        loads[i].wait()
    flat = trans[...].reshape(KINDS * PATCH, PATCH)
    t_hi, t_low = split2(flat)
    tmat[:, 0:PATCH] = t_hi.astype(BF16)
    tmat[:, PATCH : 2 * PATCH] = t_hi.astype(BF16)
    tmat[:, 2 * PATCH : 3 * PATCH] = t_low.astype(BF16)

    def transit_chunk(j):
        for kk in range(CHUNK):
            k = j * CHUNK + kk
            hi, low = split2(grown[pl.ds(pl.multiple_of(k * PATCH, PATCH), PATCH), :])
            cols = slice(kk * LANES, (kk + 1) * LANES)
            rhs[0:PATCH, cols] = hi.astype(BF16)
            rhs[PATCH : 2 * PATCH, cols] = low.astype(BF16)
            rhs[2 * PATCH : 3 * PATCH, cols] = hi.astype(BF16)
        moved = nn_dot(tmat[...], rhs[...])
        for kk in range(CHUNK):
            cols = slice(kk * LANES, (kk + 1) * LANES)
            total = moved[0:PATCH, cols] * weight[0:1, :]
            for kind in range(1, KINDS):
                total += moved[kind * PATCH : (kind + 1) * PATCH, cols] * weight[kind : kind + 1, :]
            tr_out[pl.ds(j * CHUNK + kk, PATCH, stride=BINS), :] = total

    lane16 = lax.broadcasted_iota(jnp.int32, (ROWS, LANES), 1)
    stride = step[...]
    path[1] = jnp.where(stride > 0, sub16 * LANES + lane16 + stride, -1)

    sub256 = lax.broadcasted_iota(jnp.int32, (WIDE, LANES), 0).astype(F32).astype(BF16)

    def follow(k):
        count = (k + 1) * 8
        sub_rows = lax.broadcasted_iota(jnp.int32, (PAD[k], LANES), 0)
        if k < G:
            fields = []
            for f in range(3):
                hi, low = split2(jnp.concatenate([table[m, f] for m in range(k + 1)], axis=0))
                fields += [hi, low]
            lookup = jnp.concatenate(fields, axis=0).astype(BF16)

        def piece(i, _):
            for j in range(4):
                c = i * 4 + j
                cells = path[k, pl.ds(c, 1), :]
                cols = pl.ds(pl.multiple_of(c * LANES, LANES), LANES)
                lane = jnp.broadcast_to((cells & (WIDE - 1)).astype(F32), (16, LANES)).astype(BF16)
                lane = jnp.concatenate([lane] * (WIDE // 16), axis=0)
                hot = jnp.where(sub256 == lane, jnp.ones_like(lane), jnp.zeros_like(lane))
                lane_step[k - 1, cols, :] = hot.T
                rows = jnp.where(sub_rows == (cells >> 8), 1.0, 0.0)
                row_step[OFF[k - 1] : OFF[k], cols] = rows.astype(BF16)
                if k < G:
                    found = nn_dot(lookup, hot)
                    values = []
                    for f in range(3):
                        both = found[2 * f * count : (2 * f + 1) * count] + found[(2 * f + 1) * count : (2 * f + 2) * count]
                        values.append(jnp.sum(both * rows[:count], axis=0, keepdims=True))
                    path_rate[k, 0, pl.ds(c, 1), :] = values[0]
                    path_rate[k, 1, pl.ds(c, 1), :] = values[1]
                    hop = (values[2] + 0.5).astype(jnp.int32)
                    path[k + 1, pl.ds(c, 1), :] = jnp.where(hop > 0, cells + hop, -1)
            return 0

        lax.fori_loop(0, 4, piece, 0, unroll=UNROLL)

    listed = jnp.zeros((8, LANES), jnp.int32)
    for a in range(NA):
        row = jnp.broadcast_to(tgt[a // 2 : a // 2 + 1, :], (8, LANES))
        row = pltpu.roll(row, ((a - (a % 2) * 8) * 8) % LANES, 1)
        listed = jnp.where(((block8 - sub8) & 15) == a, row, listed)
    for bit in (1, 2, 4):
        listed = jnp.where((sub8 & bit) != 0, pltpu.roll(listed, LANES - bit * 8, 1), listed)
    list_lane = listed & (LANES - 1)
    list_row = listed >> 7
    for b in range(NB):
        cols = slice(b * LANES, (b + 1) * LANES)
        lane_rcv[:, cols] = jnp.where(sub128 == list_lane[b : b + 1, :], 1.0, 0.0).astype(BF16)
        row_rcv[:, cols] = jnp.where(sub16 == list_row[b : b + 1, :], 1.0, 0.0)

    for c in range(ROWS):
        cols = slice(c * LANES, (c + 1) * LANES)
        for q in range(4):
            state[q, c : c + 1, :] = water[q : q + 1, cols]
            state[4 + q, c : c + 1, :] = rates[q : q + 1, cols]
    for m in range(1, G):
        upstream(m).wait_recv()
    for k in range(1, A_PATHS):
        follow(k)

    each(NA, lambda k: arrive_a(k).wait_recv())
    half = my_a % 2
    tiles = []
    for a in range(NA):
        tiles.append(pltpu.roll(recv_a[a], (half * 64 + a * 8) % LANES, 1))
    for b in range(NB):
        mixed = jnp.zeros((8, LANES), F32)
        for a in range(NA):
            mixed = jnp.where(block8 == (a + b) % 16, tiles[a], mixed)
        send_b[b] = pltpu.roll(mixed, (LANES - b * 8) % LANES, 1)
    each(NB, lambda k: copy_b(k).start())
    recv_b[my_b] = send_b[my_b]
    for k in range(A_PATHS, G + 1):
        follow(k)
    for q in range(2):
        rate = [state[6 + q]] + [path_rate[k, q] for k in range(1, G)]
        before = None
        for k in range(G + 1):
            now = {}
            for n in range(k, G + 1):
                if k == 0:
                    value = (1.0 - rate[0]) * now[n - 1] if n else jnp.ones((ROWS, LANES), F32)
                else:
                    value = rate[k - 1] * before[n - 1]
                    if n > k:
                        value += (1.0 - rate[k]) * now[n - 1]
                now[n] = value
                moved_by[q, k, n] = value
            before = now
    each(NB, lambda k: arrive_b(k).wait_recv())

    for b in range(NB):
        cols = slice(b * LANES, (b + 1) * LANES)
        hot = row_rcv[:, cols]
        for s, part in enumerate(split3(recv_b[b])):
            for f in range(3):
                lhs_rcv[(s * 3 + f) * ROWS : (s * 3 + f + 1) * ROWS, cols] = (part[f : f + 1, :] * hot).astype(BF16)
    landed = nt_dot(lhs_rcv[...], lane_rcv[...])
    landed = (landed[0:48] + landed[48:96] + landed[96:144]) * (1.0 / NSUB)
    surface = (landed[0:ROWS], landed[ROWS : 2 * ROWS])
    deep = (landed[2 * ROWS : 3 * ROWS], jnp.zeros((ROWS, LANES), F32))

    def macro_step(e, carry):
        hill, channel = carry[0:2], carry[2:4]
        hill_next, kept, masses = [], [], [{}, {}]
        for q in range(2):
            water_now = hill[q]
            given = []
            for _ in range(G):
                hill_out = state[4 + q] * water_now
                given.append(hill_out + deep[q])
                water_now = water_now - hill_out + surface[q]
            hill_next.append(water_now)
            for k in range(G + 1):
                total = moved_by[q, k, G] * channel[q]
                for n in range(k, G):
                    total += moved_by[q, k, n] * given[G - 1 - n]
                if k == 0:
                    kept.append(total)
                    continue
                masses[q][k] = total
        sums = [[0.0] * (G + 1) for _ in range(2)]

        def send(m):
            for q in range(2):
                send_ring[e, m - 1, q] = sums[q][m]
            ring(e, m).start()

        for k in range(G, 0, -1):
            pad = PAD[k]
            for q in range(2):
                for s, part in enumerate(split2(masses[q][k])):
                    start = 4 * OFF[k - 1] + (q * 2 + s) * pad
                    for c in range(ROWS):
                        cols = slice(c * LANES, (c + 1) * LANES)
                        value = jnp.broadcast_to(part[c : c + 1, :], (16, LANES)).astype(BF16)
                        value = jnp.concatenate([value] * (pad // 16), axis=0)
                        lhs_step[start : start + pad, cols] = value * row_step[OFF[k - 1] : OFF[k], cols]
            spread = nn_dot(lhs_step[4 * OFF[k - 1] : 4 * OFF[k], :], lane_step[k - 1])
            for q in range(2):
                both = spread[2 * q * pad : (2 * q + 1) * pad] + spread[(2 * q + 1) * pad : (2 * q + 2) * pad]
                for m in range(k + 1):
                    sums[q][m] = sums[q][m] + both[m * 8 : (m + 1) * 8]
            if EARLY:
                send(k)
        if not EARLY:
            for m in range(G, 0, -1):
                send(m)
        for j in range(CHUNKS_STEP):
            transit_chunk(e * CHUNKS_STEP + j)
        came = [sums[q][0] for q in range(2)]
        for m in range(1, G + 1):
            ring(e, m).wait_recv()
            for q in range(2):
                came[q] = came[q] + recv_ring[e, m - 1, q]
        for q in range(2):
            fold[q, pl.ds(0, 8, stride=2), :] = came[q][:, :LANES]
            fold[q, pl.ds(1, 8, stride=2), :] = came[q][:, LANES:]
        new = [kept[q] + fold[q] for q in range(2)]
        return (*hill_next, *new)

    final = lax.fori_loop(0, STEPS, macro_step, tuple(state[q] for q in range(4)))
    stored = final[2] + final[3]
    inundation = stored / (stored + cap[...])
    lhs = jnp.concatenate(split3(inundation), axis=0).astype(BF16)
    seen = nn_dot(lhs, lane_rcv[...])
    seen = (seen[0:16] + seen[16:32] + seen[32:48]) * row_rcv[...]
    for b in range(NB):
        row = jnp.sum(seen[:, b * LANES : (b + 1) * LANES], axis=0, keepdims=True)
        send_rb[b] = jnp.broadcast_to(row, (8, LANES))
    each(NB, lambda k: copy_rb(k).start())
    recv_rb[my_b] = send_rb[my_b]
    for c in range(ROWS):
        cols = slice(c * LANES, (c + 1) * LANES)
        for q in range(4):
            river_out[q : q + 1, cols] = final[q][c : c + 1, :]
    for j in range(CHUNKS_STEP * STEPS, BINS // CHUNK):
        transit_chunk(j)
    stores = (
        pltpu.make_async_copy(tr_out, tr_hbm, out_sem.at[0]),
        pltpu.make_async_copy(river_out, river_hbm, out_sem.at[1]),
    )
    for copy in stores:
        copy.start()
    each(NB, lambda k: arrive_rb(k).wait_recv())
    gathered = jnp.zeros((8, LANES), F32)
    for b in range(NB):
        gathered = jnp.where(sub8 == b, recv_rb[b], gathered)
    send_ra[...] = gathered
    each(NA, lambda k: copy_ra(k).start())
    recv_ra[my_a] = gathered
    each(NA, lambda k: arrive_ra(k).wait_recv())
    for r in range(8):
        even = pltpu.roll(recv_ra[2 * r], (LANES - my_a * 8) % LANES, 1)
        odd = pltpu.roll(recv_ra[2 * r + 1], (64 + LANES - my_a * 8) % LANES, 1)
        pair = jnp.where(lane8 < 64, even, odd)
        for bit in (1, 2, 4):
            pair = jnp.where((sub8 & bit) != 0, pltpu.roll(pair, bit * 8, 1), pair)
        row = jnp.sum(jnp.where((block8 & 7) == sub8, pair, 0.0), axis=0, keepdims=True) * share[r : r + 1, :]
        hi, mid, low = split3(row)
        tile = jnp.where(sub16 == 0, hi, jnp.where(sub16 == 1, mid, jnp.where(sub16 == 2, low, 0.0)))
        lhs_back[:, r * LANES : (r + 1) * LANES] = tile.astype(BF16)
    felt = nt_dot(lhs_back[...], onehot_src[...])
    flood_out[...] = felt[0:1] + felt[1:2] + felt[2:3]
    store = pltpu.make_async_copy(flood_out, flood_hbm, out_sem.at[2])
    store.start()

    each(NA, lambda k: copy_a(k).wait_send())
    each(NB, lambda k: copy_b(k).wait_send())
    each(NB, lambda k: copy_rb(k).wait_send())
    each(NA, lambda k: copy_ra(k).wait_send())

    for m in range(1, G):
        upstream(m).wait_send()
    for e in range(STEPS):
        for m in range(1, G + 1):
            ring(e, m).wait_send()
    for copy in (*stores, store):
        copy.wait()


def survive_kernel(
    mass_in, traits_in, flooded_in, river_in, out, flooded_out, river_out,
    mass, traits, flooded, survival, load_sem, store_sem,
):
    block = PATCH * BINS // 6
    small = [
        pltpu.make_async_copy(flooded_in, flooded, load_sem.at[6]),
        pltpu.make_async_copy(traits_in, traits, load_sem.at[7]),
    ]
    pieces = [pl.ds(i * block, block) for i in range(6)]
    loads = [pltpu.make_async_copy(mass_in.at[p, :], mass.at[p, :], load_sem.at[i]) for i, p in enumerate(pieces)]
    stores = [pltpu.make_async_copy(mass.at[p, :], out.at[p, :], store_sem.at[i]) for i, p in enumerate(pieces)]
    stores += [
        pltpu.make_async_copy(flooded, flooded_out, store_sem.at[6]),
        pltpu.make_async_copy(river_in, river_out, store_sem.at[7]),
    ]
    for copy in (*small, *loads, stores[7]):
        copy.start()
    for copy in small:
        copy.wait()
    stores[6].start()
    rows = lax.broadcasted_iota(jnp.int32, (BINS, BINS), 0)
    cols = lax.broadcasted_iota(jnp.int32, (BINS, BINS), 1)
    mortality = jnp.sum(jnp.where(rows == cols, traits[3:4, :], 0.0), axis=1, keepdims=True)
    survival[...] = jnp.exp(-mortality * flooded[...])
    for i in range(6):
        loads[i].wait()
        for p in range(8):
            rows = slice(i * block + p * BINS, i * block + (p + 1) * BINS)
            mass[rows, :] = mass[rows, :] * survival[...]
        stores[i].start()
    for copy in stores:
        copy.wait()


def shards(
    biomass, patch_area, cohort_traits, cell_forcing, disturb_weight, transitions, land_source, pair_share,
    river_target, downstream_step, river_water, river_rates, capacity,
):
    hbm = pl.BlockSpec(memory_space=pltpu.HBM)
    dma = pltpu.SemaphoreType.DMA
    tile = (8, LANES)
    n_rows = PATCH * BINS
    transited, flooded, river_state = pl.pallas_call(
        main_kernel,
        out_shape=(
            jax.ShapeDtypeStruct((n_rows, LANES), F32),
            jax.ShapeDtypeStruct((1, LANES), F32),
            jax.ShapeDtypeStruct((4, ROWS * LANES), F32),
        ),
        in_specs=[hbm] * 13,
        out_specs=(hbm, hbm, hbm),
        scratch_shapes=[
            pltpu.VMEM((n_rows, LANES), F32),
            pltpu.VMEM((1, LANES), F32),
            pltpu.VMEM((4, ROWS * LANES), F32),
            dma((3,)),
            pltpu.VMEM((BINS // 8, PATCH, 8, LANES), F32),
            pltpu.VMEM((PATCH, LANES), F32),
            pltpu.SMEM((4, BINS), F32),
            pltpu.VMEM((5, LANES), F32),
            pltpu.VMEM((KINDS, LANES), F32),
            pltpu.VMEM((KINDS, PATCH, PATCH), F32),
            pltpu.VMEM(tile, jnp.int32),
            pltpu.VMEM(tile, F32),
            pltpu.VMEM(tile, jnp.int32),
            pltpu.VMEM((ROWS, LANES), jnp.int32),
            pltpu.VMEM((4, ROWS * LANES), F32),
            pltpu.VMEM((4, ROWS * LANES), F32),
            pltpu.VMEM((ROWS, LANES), F32),
            dma((12,)),
            dma((BINS // 8,)),
            pltpu.VMEM((n_rows, LANES), F32),
            pltpu.VMEM((KINDS * PATCH, 3 * PATCH), BF16),
            pltpu.VMEM((3 * PATCH, CHUNK * LANES), BF16),
            pltpu.VMEM((LANES, 1024), BF16),
            pltpu.VMEM((LANES, 1024), BF16),
            pltpu.VMEM((ROWS, 1024), F32),
            pltpu.VMEM((G, ROWS * LANES, WIDE), BF16),
            pltpu.VMEM((OFF[G], ROWS * LANES), BF16),
            pltpu.VMEM((4 * OFF[G], ROWS * LANES), BF16),
            pltpu.VMEM((9 * ROWS, 1024), BF16),
            pltpu.VMEM((16, 1024), BF16),
            pltpu.VMEM((8, ROWS, LANES), F32),
            pltpu.VMEM((2, ROWS, LANES), F32),
            pltpu.VMEM((2, G + 1, G + 1, ROWS, LANES), F32),
            pltpu.VMEM((G, 3, 8, WIDE), F32),
            pltpu.VMEM((3, 8, WIDE), F32),
            pltpu.VMEM((G + 1, ROWS, LANES), jnp.int32),
            pltpu.VMEM((G, 2, ROWS, LANES), F32),
            dma((G,)), dma((G,)),
            pltpu.VMEM((8, *tile), F32),
            pltpu.VMEM((NA, *tile), F32),
            pltpu.VMEM((NB, *tile), F32),
            pltpu.VMEM((NB, *tile), F32),
            pltpu.VMEM((NB, *tile), F32),
            pltpu.VMEM((NB, *tile), F32),
            pltpu.VMEM(tile, F32),
            pltpu.VMEM((NA, *tile), F32),
            pltpu.VMEM((STEPS, G, 2, 8, WIDE), F32),
            pltpu.VMEM((STEPS, G, 2, 8, WIDE), F32),
            dma((NA,)), dma((NA,)), dma((NB,)), dma((NB,)), dma((NB,)), dma((NB,)), dma((NA,)), dma((NA,)),
            dma((STEPS, G)), dma((STEPS, G)),
        ],
        compiler_params=pltpu.CompilerParams(
            collective_id=0, has_side_effects=True, vmem_limit_bytes=60 * 1024 * 1024),
        name="hour",
    )(
        biomass, patch_area, cohort_traits, cell_forcing, disturb_weight, transitions,
        land_source.reshape(8, LANES), pair_share.reshape(8, LANES), river_target.reshape(8, LANES),
        downstream_step.reshape(ROWS, LANES), river_water, river_rates, capacity.reshape(ROWS, LANES),
    )
    new_biomass, flooded, river_state = pl.pallas_call(
        survive_kernel,
        out_shape=(
            jax.ShapeDtypeStruct((n_rows, LANES), F32),
            jax.ShapeDtypeStruct((1, LANES), F32),
            jax.ShapeDtypeStruct((4, ROWS * LANES), F32),
        ),
        in_specs=[hbm] * 4,
        out_specs=(hbm, hbm, hbm),
        scratch_shapes=[
            pltpu.VMEM((n_rows, LANES), F32),
            pltpu.VMEM((4, BINS), F32),
            pltpu.VMEM((1, LANES), F32),
            pltpu.VMEM((BINS, LANES), F32),
            dma((8,)),
            dma((8,)),
        ],
        compiler_params=pltpu.CompilerParams(vmem_limit_bytes=60 * 1024 * 1024),
        name="survive",
    )(transited, cohort_traits, flooded, river_state)
    return new_biomass.reshape(PATCH, BINS, LANES), flooded.reshape(LANES), river_state


def solution(mesh):
    both = ("comp", "cell")
    return jax.shard_map(
        shards,
        mesh=mesh,
        in_specs=(
            P(None, None, both), P(None, both), P(), P(None, both), P(None, both), P(), P(both), P(both), P(both),
            P(both), P(None, both), P(None, both), P(both),
        ),
        out_specs=(P(None, None, both), P(both), P(None, both)),
        check_vma=False,
    )
```

```python
import jax
import jax.numpy as jnp
from jax import lax
from jax.experimental import pallas as pl
from jax.experimental.pallas import tpu as pltpu
from jax.sharding import PartitionSpec as P

MESH = pl.DeviceIdType.MESH
F32 = jnp.float32
BF16 = jnp.bfloat16

NSUB = 12
PATCH = 48
BINS = 64
KINDS = 4
LANES = 128
NA = 16
NB = 8
ROWS = 16
CHUNK = 4
G = 6
STEPS = NSUB // G
CHUNKS_STEP = 12 // STEPS
UNROLL = True
EARLY = 3
A_PATHS = 3
WIDE = 2 * LANES
PAD = [0] + [(k + 2) // 2 * 16 for k in range(1, G + 1)]
OFF = [sum(PAD[: k + 1]) for k in range(G + 1)]


def far_first(axes):
    offsets = [()]
    for size in axes:
        offsets = [(*o, d) for o in offsets for d in range(size)]
    return sorted(offsets, key=lambda o: -sum(min(d, n - d) if n > 2 else 0.3 * d for d, n in zip(o, axes)))[:-1]


FAR_A = far_first((4, 4))
FAR_B = far_first((4, 2))


def split2(x):
    hi = x.astype(BF16).astype(F32)
    return hi, x - hi


def split3(x):
    hi, rest = split2(x)
    mid, low = split2(rest)
    return hi, mid, low


def nn_dot(a, b):
    return jnp.dot(a, b, preferred_element_type=F32)


def main_kernel(
    bio_in, area_in, traits_in, forcing_in, weight_in, trans_in, src_in, share_in, tgt_in, step_in, water_in, rates_in,
    cap_in,
    tr_hbm, flood_hbm, river_hbm,
    tr_out, flood_out, river_out, out_sem,
    bio, area, traits, forcing, weight, trans, src, share, tgt, step, water, rates, cap, in_sem, bio_sem,
    grown, tmat, rhs, onehot_src, lane_rcv_t, onehot_src_t, lane_rcv, row_rcv, lane_step, row_step, lhs_step, lhs_rcv, lhs_back, state,
    fold, moved_by, table, table_send, path, path_rate, st_s, st_r,
    send_a, recv_a, send_b, recv_b, send_rb, recv_rb, send_ra, recv_ra, send_ring, recv_ring,
    sa_s, sa_r, sb_s, sb_r, rb_s, rb_r, ra_s, ra_r, ring_s, ring_r,
):
    my_x = lax.axis_index("comp")
    cell = lax.axis_index("cell")
    my_y, my_b = cell // NB, cell % NB
    my_a = my_x * 4 + my_y
    me = my_x * 32 + cell

    def peer_a(other):
        return (other // 4, (other % 4) * NB + my_b)

    def peer_b(other):
        return (my_x, my_y * NB + other)

    barrier = pltpu.get_barrier_semaphore()

    for dx, dy in FAR_A:
        peer = peer_a((my_x + dx) % 4 * 4 + (my_y + dy) % 4)
        pl.semaphore_signal(barrier, inc=1, device_id=peer, device_id_type=MESH)
    for dz, dc in FAR_B:
        peer = peer_b((my_b // 2 + dz) % 4 * 2 + (my_b + dc) % 2)
        pl.semaphore_signal(barrier, inc=1, device_id=peer, device_id_type=MESH)
    for m in range(1, G + 1):
        for other in ((me + m) % 128, (me + 128 - m) % 128):
            pl.semaphore_signal(barrier, inc=1, device_id=(other // 32, other % 32), device_id_type=MESH)

    sources = (area_in, traits_in, forcing_in, weight_in, trans_in, src_in, share_in, tgt_in, step_in, water_in, rates_in, cap_in)
    targets = (area, traits, forcing, weight, trans, src, share, tgt, step, water, rates, cap)
    loads = [pltpu.make_async_copy(sources[i], targets[i], in_sem.at[i]) for i in range(12)]
    for i in (5, 1, 2):
        loads[i].start()
    mass_loads = [
        pltpu.make_async_copy(bio_in.at[:, pl.ds(g * 8, 8), :], bio.at[g], bio_sem.at[g]) for g in range(BINS // 8)
    ]
    for g in range(BINS // 8 - 1, -1, -1):
        mass_loads[g].start()
    for i in (0, 6, 4, 3, 8, 7, 9, 10, 11):
        loads[i].start()
    sub8 = lax.broadcasted_iota(jnp.int32, (8, LANES), 0)
    lane8 = lax.broadcasted_iota(jnp.int32, (8, LANES), 1)
    block8 = lane8 >> 3
    sub16 = lax.broadcasted_iota(jnp.int32, (16, LANES), 0)
    sub128 = lax.broadcasted_iota(jnp.int32, (LANES, LANES), 0)

    loads[5].wait()
    for r in range(8):
        hot = jnp.where(sub128 == src[r : r + 1, :], 1.0, 0.0)
        onehot_src[:, r * LANES : (r + 1) * LANES] = hot.astype(BF16)

    loads[1].wait()
    loads[2].wait()
    light = forcing[0:1, :]
    light_factor = light / (light + 0.5)

    zero48 = jnp.zeros((PATCH, LANES), F32)
    carry = (zero48, zero48)
    for g in range(BINS // 8 - 1, -1, -1):
        mass_loads[g].wait()
        group = bio.at[g].reshape(PATCH * 8, LANES)

        def canopy_bin(i, carry, g=g, group=group):
            above, total = carry
            kk = 7 - i
            k = g * 8 + kk
            mass = group[pl.ds(kk, PATCH, stride=8), :]
            leaf = mass * traits[0, k]
            gain = (traits[1, k] * light_factor) * leaf * jnp.exp(-0.05 * above)
            grown[pl.ds(pl.multiple_of(k * PATCH, PATCH), PATCH), :] = mass * (1.0 - 0.1 * traits[2, k]) + 0.5 * gain
            return above + leaf, total + gain

        carry = lax.fori_loop(0, 8, canopy_bin, carry, unroll=True)
    total = carry[1]
    loads[0].wait()
    transpiration = 0.5 * jnp.sum(area[...] * total, axis=0, keepdims=True)
    wet = forcing[1:2, :] * forcing[2:3, :]
    frozen = forcing[4:5, :]
    row0 = wet * (1.0 - frozen)
    row1 = wet * frozen
    row2 = forcing[3:4, :] * jnp.exp(-0.5 * transpiration)
    runoff = jnp.where(sub8 == 0, row0, jnp.where(sub8 == 1, row1, jnp.where(sub8 == 2, row2, 0.0)))
    parts = split3(runoff)
    lhs = jnp.concatenate([*parts, jnp.zeros((8, LANES), F32)], axis=0).astype(BF16)
    loads[6].wait()
    picked = nn_dot(lhs, onehot_src[...])
    picked = picked[0:8] + picked[8:16] + picked[16:24]
    for r in range(8):
        send_a[r] = picked[:, r * LANES : (r + 1) * LANES] * share[r : r + 1, :]

    def at_a(k):
        dx, dy = FAR_A[k - 1]
        return (my_x + dx) % 4 * 4 + (my_y + dy) % 4

    def at_b(k):
        dz, dc = FAR_B[k - 1]
        return (my_b // 2 + dz) % 4 * 2 + (my_b + dc) % 2

    def copy_a(k):
        other = at_a(k)
        return pltpu.make_async_remote_copy(
            src_ref=send_a.at[other // 2], dst_ref=recv_a.at[my_a], send_sem=sa_s.at[k], recv_sem=sa_r.at[my_a],
            device_id=peer_a(other), device_id_type=MESH)

    def arrive_a(k):
        other = at_a(k)
        return pltpu.make_async_remote_copy(
            src_ref=send_a.at[0], dst_ref=recv_a.at[other], send_sem=sa_s.at[k], recv_sem=sa_r.at[other],
            device_id=peer_a(other), device_id_type=MESH)

    def copy_b(k):
        other = at_b(k)
        return pltpu.make_async_remote_copy(
            src_ref=send_b.at[other], dst_ref=recv_b.at[my_b], send_sem=sb_s.at[k], recv_sem=sb_r.at[my_b],
            device_id=peer_b(other), device_id_type=MESH)

    def arrive_b(k):
        other = at_b(k)
        return pltpu.make_async_remote_copy(
            src_ref=send_b.at[other], dst_ref=recv_b.at[other], send_sem=sb_s.at[k], recv_sem=sb_r.at[other],
            device_id=peer_b(other), device_id_type=MESH)

    def copy_rb(k):
        other = at_b(k)
        return pltpu.make_async_remote_copy(
            src_ref=send_rb.at[other], dst_ref=recv_rb.at[my_b], send_sem=rb_s.at[k], recv_sem=rb_r.at[my_b],
            device_id=peer_b(other), device_id_type=MESH)

    def arrive_rb(k):
        other = at_b(k)
        return pltpu.make_async_remote_copy(
            src_ref=send_rb.at[other], dst_ref=recv_rb.at[other], send_sem=rb_s.at[k], recv_sem=rb_r.at[other],
            device_id=peer_b(other), device_id_type=MESH)

    def copy_ra(k):
        other = at_a(k)
        return pltpu.make_async_remote_copy(
            src_ref=send_ra, dst_ref=recv_ra.at[my_a], send_sem=ra_s.at[k], recv_sem=ra_r.at[my_a],
            device_id=peer_a(other), device_id_type=MESH)

    def arrive_ra(k):
        other = at_a(k)
        return pltpu.make_async_remote_copy(
            src_ref=send_ra, dst_ref=recv_ra.at[other], send_sem=ra_s.at[k], recv_sem=ra_r.at[other],
            device_id=peer_a(other), device_id_type=MESH)

    def ring(e, m):
        to = (me + m) % 128
        return pltpu.make_async_remote_copy(
            src_ref=send_ring.at[e, m - 1], dst_ref=recv_ring.at[e, m - 1],
            send_sem=ring_s.at[e, m - 1], recv_sem=ring_r.at[e, m - 1],
            device_id=(to // 32, to % 32), device_id_type=MESH)

    def upstream(m):
        to = (me + 128 - m) % 128
        return pltpu.make_async_remote_copy(
            src_ref=table_send, dst_ref=table.at[m], send_sem=st_s.at[m], recv_sem=st_r.at[m],
            device_id=(to // 32, to % 32), device_id_type=MESH)

    def each(count, action):
        for k in range(1, count):
            action(k)

    pl.semaphore_wait(barrier, NA + NB - 2 + 2 * G)
    each(NA, lambda k: copy_a(k).start())
    recv_a[my_a] = send_a[my_a // 2]
    loads[8].wait()
    loads[10].wait()
    for c in range(ROWS):
        cols = slice(c * LANES, (c + 1) * LANES)
        wide = slice(c % 2 * LANES, (c % 2 + 1) * LANES)
        for q in range(2):
            table_send[q, c // 2 : c // 2 + 1, wide] = rates[2 + q : 3 + q, cols]
    for p in range(2):
        table_send[2, :, p * LANES : (p + 1) * LANES] = step[pl.ds(p, 8, stride=2), :].astype(F32)
    for m in range(1, G):
        upstream(m).start()
    table[0] = table_send[...]

    for i in (4, 3, 7, 9, 11):
        loads[i].wait()
    flat = trans[...].reshape(KINDS * PATCH, PATCH)
    t_hi, t_low = split2(flat)
    tmat[:, 0:PATCH] = t_hi.astype(BF16)
    tmat[:, PATCH : 2 * PATCH] = t_hi.astype(BF16)
    tmat[:, 2 * PATCH : 3 * PATCH] = t_low.astype(BF16)

    def transit_chunk(j):
        for kk in range(CHUNK):
            k = j * CHUNK + kk
            hi, low = split2(grown[pl.ds(pl.multiple_of(k * PATCH, PATCH), PATCH), :])
            cols = slice(kk * LANES, (kk + 1) * LANES)
            rhs[0:PATCH, cols] = hi.astype(BF16)
            rhs[PATCH : 2 * PATCH, cols] = low.astype(BF16)
            rhs[2 * PATCH : 3 * PATCH, cols] = hi.astype(BF16)
        moved = nn_dot(tmat[...], rhs[...])
        for kk in range(CHUNK):
            cols = slice(kk * LANES, (kk + 1) * LANES)
            total = moved[0:PATCH, cols] * weight[0:1, :]
            for kind in range(1, KINDS):
                total += moved[kind * PATCH : (kind + 1) * PATCH, cols] * weight[kind : kind + 1, :]
            tr_out[pl.ds(j * CHUNK + kk, PATCH, stride=BINS), :] = total

    lane16 = lax.broadcasted_iota(jnp.int32, (ROWS, LANES), 1)
    stride = step[...]
    path[1] = jnp.where(stride > 0, sub16 * LANES + lane16 + stride, -1)

    sub256 = lax.broadcasted_iota(jnp.int32, (WIDE, LANES), 0).astype(F32).astype(BF16)

    def follow(k):
        count = (k + 1) * 8
        sub_rows = lax.broadcasted_iota(jnp.int32, (PAD[k], LANES), 0)
        if k < G:
            fields = []
            for f in range(3):
                hi, low = split2(jnp.concatenate([table[m, f] for m in range(k + 1)], axis=0))
                fields += [hi, low]
            lookup = jnp.concatenate(fields, axis=0).astype(BF16)

        def piece(i, _):
            for j in range(4):
                c = i * 4 + j
                cells = path[k, pl.ds(c, 1), :]
                cols = pl.ds(pl.multiple_of(c * LANES, LANES), LANES)
                lane = jnp.broadcast_to((cells & (WIDE - 1)).astype(F32), (16, LANES)).astype(BF16)
                lane = jnp.concatenate([lane] * (WIDE // 16), axis=0)
                hot = jnp.where(sub256 == lane, jnp.ones_like(lane), jnp.zeros_like(lane))
                lane_step[k - 1, cols, :] = hot.T
                rows = jnp.where(sub_rows == (cells >> 8), 1.0, 0.0)
                row_step[OFF[k - 1] : OFF[k], cols] = rows.astype(BF16)
                if k < G:
                    found = nn_dot(lookup, hot)
                    values = []
                    for f in range(3):
                        both = found[2 * f * count : (2 * f + 1) * count] + found[(2 * f + 1) * count : (2 * f + 2) * count]
                        values.append(jnp.sum(both * rows[:count], axis=0, keepdims=True))
                    path_rate[k, 0, pl.ds(c, 1), :] = values[0]
                    path_rate[k, 1, pl.ds(c, 1), :] = values[1]
                    hop = (values[2] + 0.5).astype(jnp.int32)
                    path[k + 1, pl.ds(c, 1), :] = jnp.where(hop > 0, cells + hop, -1)
            return 0

        lax.fori_loop(0, 4, piece, 0, unroll=UNROLL)

    listed = jnp.zeros((8, LANES), jnp.int32)
    for a in range(NA):
        row = jnp.broadcast_to(tgt[a // 2 : a // 2 + 1, :], (8, LANES))
        row = pltpu.roll(row, ((a - (a % 2) * 8) * 8) % LANES, 1)
        listed = jnp.where(((block8 - sub8) & 15) == a, row, listed)
    for bit in (1, 2, 4):
        listed = jnp.where((sub8 & bit) != 0, pltpu.roll(listed, LANES - bit * 8, 1), listed)
    list_lane = listed & (LANES - 1)
    list_row = listed >> 7
    for b in range(NB):
        cols = slice(b * LANES, (b + 1) * LANES)
        hot = jnp.where(sub128 == list_lane[b : b + 1, :], 1.0, 0.0).astype(BF16)
        lane_rcv[:, cols] = hot
        lane_rcv_t[cols, :] = hot.T
        row_rcv[:, cols] = jnp.where(sub16 == list_row[b : b + 1, :], 1.0, 0.0)

    for c in range(ROWS):
        cols = slice(c * LANES, (c + 1) * LANES)
        for q in range(4):
            state[q, c : c + 1, :] = water[q : q + 1, cols]
            state[4 + q, c : c + 1, :] = rates[q : q + 1, cols]
    for k in range(1, A_PATHS):
        upstream(k).wait_recv()
        follow(k)

    each(NA, lambda k: arrive_a(k).wait_recv())
    half = my_a % 2
    tiles = []
    for a in range(NA):
        tiles.append(pltpu.roll(recv_a[a], (half * 64 + a * 8) % LANES, 1))
    for b in range(NB):
        mixed = jnp.zeros((8, LANES), F32)
        for a in range(NA):
            mixed = jnp.where(block8 == (a + b) % 16, tiles[a], mixed)
        send_b[b] = pltpu.roll(mixed, (LANES - b * 8) % LANES, 1)
    each(NB, lambda k: copy_b(k).start())
    recv_b[my_b] = send_b[my_b]
    for k in range(A_PATHS, G + 1):
        if k < G:
            upstream(k).wait_recv()
        follow(k)
    for q in range(2):
        rate = [state[6 + q]] + [path_rate[k, q] for k in range(1, G)]
        before = None
        for k in range(G + 1):
            now = {}
            for n in range(k, G + 1):
                if k == 0:
                    value = (1.0 - rate[0]) * now[n - 1] if n else jnp.ones((ROWS, LANES), F32)
                else:
                    value = rate[k - 1] * before[n - 1]
                    if n > k:
                        value += (1.0 - rate[k]) * now[n - 1]
                now[n] = value
                moved_by[q, k, n] = value
            before = now
    each(NB, lambda k: arrive_b(k).wait_recv())

    for b in range(NB):
        cols = slice(b * LANES, (b + 1) * LANES)
        hot = row_rcv[:, cols]
        for s, part in enumerate(split3(recv_b[b])):
            for f in range(3):
                lhs_rcv[(s * 3 + f) * ROWS : (s * 3 + f + 1) * ROWS, cols] = (part[f : f + 1, :] * hot).astype(BF16)
    landed = nn_dot(lhs_rcv[...], lane_rcv_t[...])
    landed = (landed[0:48] + landed[48:96] + landed[96:144]) * (1.0 / NSUB)
    surface = (landed[0:ROWS], landed[ROWS : 2 * ROWS])
    deep = (landed[2 * ROWS : 3 * ROWS], jnp.zeros((ROWS, LANES), F32))

    def macro_step(e, carry):
        hill, channel = carry[0:2], carry[2:4]
        hill_next, kept, masses = [], [], [{}, {}]
        for q in range(2):
            water_now = hill[q]
            given = []
            for _ in range(G):
                hill_out = state[4 + q] * water_now
                given.append(hill_out + deep[q])
                water_now = water_now - hill_out + surface[q]
            hill_next.append(water_now)
            for k in range(G + 1):
                total = moved_by[q, k, G] * channel[q]
                for n in range(k, G):
                    total += moved_by[q, k, n] * given[G - 1 - n]
                if k == 0:
                    kept.append(total)
                    continue
                masses[q][k] = total
        sums = [[0.0] * (G + 1) for _ in range(2)]

        def send(m):
            for q in range(2):
                send_ring[e, m - 1, q] = sums[q][m]
            ring(e, m).start()

        for k in range(G, 0, -1):
            pad = PAD[k]
            for q in range(2):
                for s, part in enumerate(split2(masses[q][k])):
                    start = 4 * OFF[k - 1] + (q * 2 + s) * pad
                    for c in range(ROWS):
                        cols = slice(c * LANES, (c + 1) * LANES)
                        value = jnp.broadcast_to(part[c : c + 1, :], (16, LANES)).astype(BF16)
                        value = jnp.concatenate([value] * (pad // 16), axis=0)
                        lhs_step[start : start + pad, cols] = value * row_step[OFF[k - 1] : OFF[k], cols]
            spread = nn_dot(lhs_step[4 * OFF[k - 1] : 4 * OFF[k], :], lane_step[k - 1])
            for q in range(2):
                both = spread[2 * q * pad : (2 * q + 1) * pad] + spread[(2 * q + 1) * pad : (2 * q + 2) * pad]
                for m in range(k + 1):
                    sums[q][m] = sums[q][m] + both[m * 8 : (m + 1) * 8]
            if k == EARLY:
                for m in range(G, EARLY - 1, -1):
                    send(m)
        for m in range(EARLY - 1, 0, -1):
            send(m)
        for j in range(CHUNKS_STEP):
            transit_chunk(e * CHUNKS_STEP + j)
        came = [sums[q][0] for q in range(2)]
        for m in range(1, G + 1):
            ring(e, m).wait_recv()
            for q in range(2):
                came[q] = came[q] + recv_ring[e, m - 1, q]
        for q in range(2):
            fold[q, pl.ds(0, 8, stride=2), :] = came[q][:, :LANES]
            fold[q, pl.ds(1, 8, stride=2), :] = came[q][:, LANES:]
        new = [kept[q] + fold[q] for q in range(2)]
        return (*hill_next, *new)

    final = lax.fori_loop(0, STEPS, macro_step, tuple(state[q] for q in range(4)))
    stored = final[2] + final[3]
    inundation = stored / (stored + cap[...])
    lhs = jnp.concatenate(split3(inundation), axis=0).astype(BF16)
    seen = nn_dot(lhs, lane_rcv[...])
    seen = (seen[0:16] + seen[16:32] + seen[32:48]) * row_rcv[...]
    for b in range(NB):
        row = jnp.sum(seen[:, b * LANES : (b + 1) * LANES], axis=0, keepdims=True)
        send_rb[b] = jnp.broadcast_to(row, (8, LANES))
    each(NB, lambda k: copy_rb(k).start())
    recv_rb[my_b] = send_rb[my_b]
    for c in range(ROWS):
        cols = slice(c * LANES, (c + 1) * LANES)
        for q in range(4):
            river_out[q : q + 1, cols] = final[q][c : c + 1, :]
    for r in range(8):
        cols = slice(r * LANES, (r + 1) * LANES)
        onehot_src_t[cols, :] = onehot_src[:, cols].T
    for j in range(CHUNKS_STEP * STEPS, BINS // CHUNK):
        transit_chunk(j)
    stores = (
        pltpu.make_async_copy(tr_out, tr_hbm, out_sem.at[0]),
        pltpu.make_async_copy(river_out, river_hbm, out_sem.at[1]),
    )
    for copy in stores:
        copy.start()
    each(NB, lambda k: arrive_rb(k).wait_recv())
    gathered = jnp.zeros((8, LANES), F32)
    for b in range(NB):
        gathered = jnp.where(sub8 == b, recv_rb[b], gathered)
    send_ra[...] = gathered
    each(NA, lambda k: copy_ra(k).start())
    recv_ra[my_a] = gathered
    each(NA, lambda k: arrive_ra(k).wait_recv())
    for r in range(8):
        even = pltpu.roll(recv_ra[2 * r], (LANES - my_a * 8) % LANES, 1)
        odd = pltpu.roll(recv_ra[2 * r + 1], (64 + LANES - my_a * 8) % LANES, 1)
        pair = jnp.where(lane8 < 64, even, odd)
        for bit in (1, 2, 4):
            pair = jnp.where((sub8 & bit) != 0, pltpu.roll(pair, bit * 8, 1), pair)
        row = jnp.sum(jnp.where((block8 & 7) == sub8, pair, 0.0), axis=0, keepdims=True) * share[r : r + 1, :]
        hi, mid, low = split3(row)
        tile = jnp.where(sub16 == 0, hi, jnp.where(sub16 == 1, mid, jnp.where(sub16 == 2, low, 0.0)))
        lhs_back[:, r * LANES : (r + 1) * LANES] = tile.astype(BF16)
    felt = nn_dot(lhs_back[...], onehot_src_t[...])
    flood_out[...] = felt[0:1] + felt[1:2] + felt[2:3]
    store = pltpu.make_async_copy(flood_out, flood_hbm, out_sem.at[2])
    store.start()

    each(NA, lambda k: copy_a(k).wait_send())
    each(NB, lambda k: copy_b(k).wait_send())
    each(NB, lambda k: copy_rb(k).wait_send())
    each(NA, lambda k: copy_ra(k).wait_send())

    for m in range(1, G):
        upstream(m).wait_send()
    for e in range(STEPS):
        for m in range(1, G + 1):
            ring(e, m).wait_send()
    for copy in (*stores, store):
        copy.wait()


def survive_kernel(
    mass_in, traits_in, flooded_in, river_in, out, flooded_out, river_out,
    mass, traits, flooded, survival, load_sem, store_sem,
):
    block = PATCH * BINS // 6
    small = [
        pltpu.make_async_copy(flooded_in, flooded, load_sem.at[6]),
        pltpu.make_async_copy(traits_in, traits, load_sem.at[7]),
    ]
    pieces = [pl.ds(i * block, block) for i in range(6)]
    loads = [pltpu.make_async_copy(mass_in.at[p, :], mass.at[p, :], load_sem.at[i]) for i, p in enumerate(pieces)]
    stores = [pltpu.make_async_copy(mass.at[p, :], out.at[p, :], store_sem.at[i]) for i, p in enumerate(pieces)]
    stores += [
        pltpu.make_async_copy(flooded, flooded_out, store_sem.at[6]),
        pltpu.make_async_copy(river_in, river_out, store_sem.at[7]),
    ]
    for copy in (*small, *loads, stores[7]):
        copy.start()
    for copy in small:
        copy.wait()
    stores[6].start()
    rows = lax.broadcasted_iota(jnp.int32, (BINS, BINS), 0)
    cols = lax.broadcasted_iota(jnp.int32, (BINS, BINS), 1)
    mortality = jnp.sum(jnp.where(rows == cols, traits[3:4, :], 0.0), axis=1, keepdims=True)
    survival[...] = jnp.exp(-mortality * flooded[...])
    for i in range(6):
        loads[i].wait()
        for p in range(8):
            rows = slice(i * block + p * BINS, i * block + (p + 1) * BINS)
            mass[rows, :] = mass[rows, :] * survival[...]
        stores[i].start()
    for copy in stores:
        copy.wait()


def shards(
    biomass, patch_area, cohort_traits, cell_forcing, disturb_weight, transitions, land_source, pair_share,
    river_target, downstream_step, river_water, river_rates, capacity,
):
    hbm = pl.BlockSpec(memory_space=pltpu.HBM)
    dma = pltpu.SemaphoreType.DMA
    tile = (8, LANES)
    n_rows = PATCH * BINS
    transited, flooded, river_state = pl.pallas_call(
        main_kernel,
        out_shape=(
            jax.ShapeDtypeStruct((n_rows, LANES), F32),
            jax.ShapeDtypeStruct((1, LANES), F32),
            jax.ShapeDtypeStruct((4, ROWS * LANES), F32),
        ),
        in_specs=[hbm] * 13,
        out_specs=(hbm, hbm, hbm),
        scratch_shapes=[
            pltpu.VMEM((n_rows, LANES), F32),
            pltpu.VMEM((1, LANES), F32),
            pltpu.VMEM((4, ROWS * LANES), F32),
            dma((3,)),
            pltpu.VMEM((BINS // 8, PATCH, 8, LANES), F32),
            pltpu.VMEM((PATCH, LANES), F32),
            pltpu.SMEM((4, BINS), F32),
            pltpu.VMEM((5, LANES), F32),
            pltpu.VMEM((KINDS, LANES), F32),
            pltpu.VMEM((KINDS, PATCH, PATCH), F32),
            pltpu.VMEM(tile, jnp.int32),
            pltpu.VMEM(tile, F32),
            pltpu.VMEM(tile, jnp.int32),
            pltpu.VMEM((ROWS, LANES), jnp.int32),
            pltpu.VMEM((4, ROWS * LANES), F32),
            pltpu.VMEM((4, ROWS * LANES), F32),
            pltpu.VMEM((ROWS, LANES), F32),
            dma((12,)),
            dma((BINS // 8,)),
            pltpu.VMEM((n_rows, LANES), F32),
            pltpu.VMEM((KINDS * PATCH, 3 * PATCH), BF16),
            pltpu.VMEM((3 * PATCH, CHUNK * LANES), BF16),
            pltpu.VMEM((LANES, 1024), BF16),
            pltpu.VMEM((1024, LANES), BF16),
            pltpu.VMEM((1024, LANES), BF16),
            pltpu.VMEM((LANES, 1024), BF16),
            pltpu.VMEM((ROWS, 1024), F32),
            pltpu.VMEM((G, ROWS * LANES, WIDE), BF16),
            pltpu.VMEM((OFF[G], ROWS * LANES), BF16),
            pltpu.VMEM((4 * OFF[G], ROWS * LANES), BF16),
            pltpu.VMEM((9 * ROWS, 1024), BF16),
            pltpu.VMEM((16, 1024), BF16),
            pltpu.VMEM((8, ROWS, LANES), F32),
            pltpu.VMEM((2, ROWS, LANES), F32),
            pltpu.VMEM((2, G + 1, G + 1, ROWS, LANES), F32),
            pltpu.VMEM((G, 3, 8, WIDE), F32),
            pltpu.VMEM((3, 8, WIDE), F32),
            pltpu.VMEM((G + 1, ROWS, LANES), jnp.int32),
            pltpu.VMEM((G, 2, ROWS, LANES), F32),
            dma((G,)), dma((G,)),
            pltpu.VMEM((8, *tile), F32),
            pltpu.VMEM((NA, *tile), F32),
            pltpu.VMEM((NB, *tile), F32),
            pltpu.VMEM((NB, *tile), F32),
            pltpu.VMEM((NB, *tile), F32),
            pltpu.VMEM((NB, *tile), F32),
            pltpu.VMEM(tile, F32),
            pltpu.VMEM((NA, *tile), F32),
            pltpu.VMEM((STEPS, G, 2, 8, WIDE), F32),
            pltpu.VMEM((STEPS, G, 2, 8, WIDE), F32),
            dma((NA,)), dma((NA,)), dma((NB,)), dma((NB,)), dma((NB,)), dma((NB,)), dma((NA,)), dma((NA,)),
            dma((STEPS, G)), dma((STEPS, G)),
        ],
        compiler_params=pltpu.CompilerParams(
            collective_id=0, has_side_effects=True, vmem_limit_bytes=60 * 1024 * 1024),
        name="hour",
    )(
        biomass, patch_area, cohort_traits, cell_forcing, disturb_weight, transitions,
        land_source.reshape(8, LANES), pair_share.reshape(8, LANES), river_target.reshape(8, LANES),
        downstream_step.reshape(ROWS, LANES), river_water, river_rates, capacity.reshape(ROWS, LANES),
    )
    new_biomass, flooded, river_state = pl.pallas_call(
        survive_kernel,
        out_shape=(
            jax.ShapeDtypeStruct((n_rows, LANES), F32),
            jax.ShapeDtypeStruct((1, LANES), F32),
            jax.ShapeDtypeStruct((4, ROWS * LANES), F32),
        ),
        in_specs=[hbm] * 4,
        out_specs=(hbm, hbm, hbm),
        scratch_shapes=[
            pltpu.VMEM((n_rows, LANES), F32),
            pltpu.VMEM((4, BINS), F32),
            pltpu.VMEM((1, LANES), F32),
            pltpu.VMEM((BINS, LANES), F32),
            dma((8,)),
            dma((8,)),
        ],
        compiler_params=pltpu.CompilerParams(vmem_limit_bytes=60 * 1024 * 1024),
        name="survive",
    )(transited, cohort_traits, flooded, river_state)
    return new_biomass.reshape(PATCH, BINS, LANES), flooded.reshape(LANES), river_state


def solution(mesh):
    both = ("comp", "cell")
    return jax.shard_map(
        shards,
        mesh=mesh,
        in_specs=(
            P(None, None, both), P(None, both), P(), P(None, both), P(None, both), P(), P(both), P(both), P(both),
            P(both), P(None, both), P(None, both), P(both),
        ),
        out_specs=(P(None, None, both), P(both), P(None, both)),
        check_vma=False,
    )
```

```python
import jax
import jax.numpy as jnp
from jax import lax
from jax.experimental import pallas as pl
from jax.experimental.pallas import tpu as pltpu
from jax.sharding import PartitionSpec as P

MESH = pl.DeviceIdType.MESH
F32 = jnp.float32
BF16 = jnp.bfloat16

NSUB = 12
PATCH = 48
BINS = 64
KINDS = 4
LANES = 128
NA = 16
NB = 8
ROWS = 16
CHUNK = 4
G = 6
STEPS = NSUB // G
CHUNKS_STEP = 12 // STEPS
UNROLL = True
EARLY = 3
A_PATHS = 2
WIDE = 2 * LANES
PAD = [0] + [(k + 2) // 2 * 16 for k in range(1, G + 1)]
OFF = [sum(PAD[: k + 1]) for k in range(G + 1)]


def far_first(axes):
    offsets = [()]
    for size in axes:
        offsets = [(*o, d) for o in offsets for d in range(size)]
    return sorted(offsets, key=lambda o: -sum(min(d, n - d) if n > 2 else 0.3 * d for d, n in zip(o, axes)))[:-1]


FAR_A = far_first((4, 4))
FAR_B = far_first((4, 2))


def split2(x):
    hi = x.astype(BF16).astype(F32)
    return hi, x - hi


def split3(x):
    hi, rest = split2(x)
    mid, low = split2(rest)
    return hi, mid, low


def nn_dot(a, b):
    return jnp.dot(a, b, preferred_element_type=F32)


def main_kernel(
    bio_in, area_in, traits_in, forcing_in, weight_in, trans_in, src_in, share_in, tgt_in, step_in, water_in, rates_in,
    cap_in,
    tr_hbm, flood_hbm, river_hbm,
    tr_out, flood_out, river_out, out_sem,
    bio, area, traits, forcing, weight, trans, src, share, tgt, step, water, rates, cap, in_sem, bio_sem,
    grown, tmat, rhs, onehot_src, lane_rcv_t, onehot_src_t, lane_rcv, row_rcv, lane_step, row_step, lhs_step, lhs_rcv, lhs_back, state,
    fold, moved_by, table, table_send, path, path_rate, st_s, st_r,
    send_a, recv_a, send_b, recv_b, send_rb, recv_rb, send_ra, recv_ra, send_ring, recv_ring,
    sa_s, sa_r, sb_s, sb_r, rb_s, rb_r, ra_s, ra_r, ring_s, ring_r,
):
    my_x = lax.axis_index("comp")
    cell = lax.axis_index("cell")
    my_y, my_b = cell // NB, cell % NB
    my_a = my_x * 4 + my_y
    me = my_x * 32 + cell

    def peer_a(other):
        return (other // 4, (other % 4) * NB + my_b)

    def peer_b(other):
        return (my_x, my_y * NB + other)

    barrier = pltpu.get_barrier_semaphore()

    for dx, dy in FAR_A:
        peer = peer_a((my_x + dx) % 4 * 4 + (my_y + dy) % 4)
        pl.semaphore_signal(barrier, inc=1, device_id=peer, device_id_type=MESH)
    for dz, dc in FAR_B:
        peer = peer_b((my_b // 2 + dz) % 4 * 2 + (my_b + dc) % 2)
        pl.semaphore_signal(barrier, inc=1, device_id=peer, device_id_type=MESH)
    for m in range(1, G + 1):
        for other in ((me + m) % 128, (me + 128 - m) % 128):
            pl.semaphore_signal(barrier, inc=1, device_id=(other // 32, other % 32), device_id_type=MESH)

    sources = (area_in, traits_in, forcing_in, weight_in, trans_in, src_in, share_in, tgt_in, step_in, water_in, rates_in, cap_in)
    targets = (area, traits, forcing, weight, trans, src, share, tgt, step, water, rates, cap)
    loads = [pltpu.make_async_copy(sources[i], targets[i], in_sem.at[i]) for i in range(12)]
    for i in (5, 1, 2):
        loads[i].start()
    mass_loads = [
        pltpu.make_async_copy(bio_in.at[:, pl.ds(g * 8, 8), :], bio.at[g], bio_sem.at[g]) for g in range(BINS // 8)
    ]
    for g in range(BINS // 8 - 1, -1, -1):
        mass_loads[g].start()
    for i in (0, 6, 4, 3, 8, 7, 9, 10, 11):
        loads[i].start()
    sub8 = lax.broadcasted_iota(jnp.int32, (8, LANES), 0)
    lane8 = lax.broadcasted_iota(jnp.int32, (8, LANES), 1)
    block8 = lane8 >> 3
    sub16 = lax.broadcasted_iota(jnp.int32, (16, LANES), 0)
    sub128 = lax.broadcasted_iota(jnp.int32, (LANES, LANES), 0)

    loads[5].wait()
    for r in range(8):
        hot = jnp.where(sub128 == src[r : r + 1, :], 1.0, 0.0)
        onehot_src[:, r * LANES : (r + 1) * LANES] = hot.astype(BF16)

    loads[1].wait()
    loads[2].wait()
    light = forcing[0:1, :]
    light_factor = light / (light + 0.5)

    zero48 = jnp.zeros((PATCH, LANES), F32)
    carry = (zero48, zero48)
    for g in range(BINS // 8 - 1, -1, -1):
        mass_loads[g].wait()
        group = bio.at[g].reshape(PATCH * 8, LANES)

        def canopy_bin(i, carry, g=g, group=group):
            above, total = carry
            kk = 7 - i
            k = g * 8 + kk
            mass = group[pl.ds(kk, PATCH, stride=8), :]
            leaf = mass * traits[0, k]
            gain = (traits[1, k] * light_factor) * leaf * jnp.exp(-0.05 * above)
            grown[pl.ds(pl.multiple_of(k * PATCH, PATCH), PATCH), :] = mass * (1.0 - 0.1 * traits[2, k]) + 0.5 * gain
            return above + leaf, total + gain

        carry = lax.fori_loop(0, 8, canopy_bin, carry, unroll=True)
    total = carry[1]
    loads[0].wait()
    transpiration = 0.5 * jnp.sum(area[...] * total, axis=0, keepdims=True)
    wet = forcing[1:2, :] * forcing[2:3, :]
    frozen = forcing[4:5, :]
    row0 = wet * (1.0 - frozen)
    row1 = wet * frozen
    row2 = forcing[3:4, :] * jnp.exp(-0.5 * transpiration)
    runoff = jnp.where(sub8 == 0, row0, jnp.where(sub8 == 1, row1, jnp.where(sub8 == 2, row2, 0.0)))
    parts = split3(runoff)
    lhs = jnp.concatenate([*parts, jnp.zeros((8, LANES), F32)], axis=0).astype(BF16)
    loads[6].wait()
    picked = nn_dot(lhs, onehot_src[...])
    picked = picked[0:8] + picked[8:16] + picked[16:24]
    for r in range(8):
        send_a[r] = picked[:, r * LANES : (r + 1) * LANES] * share[r : r + 1, :]

    def at_a(k):
        dx, dy = FAR_A[k - 1]
        return (my_x + dx) % 4 * 4 + (my_y + dy) % 4

    def at_b(k):
        dz, dc = FAR_B[k - 1]
        return (my_b // 2 + dz) % 4 * 2 + (my_b + dc) % 2

    def copy_a(k):
        other = at_a(k)
        return pltpu.make_async_remote_copy(
            src_ref=send_a.at[other // 2], dst_ref=recv_a.at[my_a], send_sem=sa_s.at[k], recv_sem=sa_r.at[my_a],
            device_id=peer_a(other), device_id_type=MESH)

    def arrive_a(k):
        other = at_a(k)
        return pltpu.make_async_remote_copy(
            src_ref=send_a.at[0], dst_ref=recv_a.at[other], send_sem=sa_s.at[k], recv_sem=sa_r.at[other],
            device_id=peer_a(other), device_id_type=MESH)

    def copy_b(k):
        other = at_b(k)
        return pltpu.make_async_remote_copy(
            src_ref=send_b.at[other], dst_ref=recv_b.at[my_b], send_sem=sb_s.at[k], recv_sem=sb_r.at[my_b],
            device_id=peer_b(other), device_id_type=MESH)

    def arrive_b(k):
        other = at_b(k)
        return pltpu.make_async_remote_copy(
            src_ref=send_b.at[other], dst_ref=recv_b.at[other], send_sem=sb_s.at[k], recv_sem=sb_r.at[other],
            device_id=peer_b(other), device_id_type=MESH)

    def copy_rb(k):
        other = at_b(k)
        return pltpu.make_async_remote_copy(
            src_ref=send_rb.at[other], dst_ref=recv_rb.at[my_b], send_sem=rb_s.at[k], recv_sem=rb_r.at[my_b],
            device_id=peer_b(other), device_id_type=MESH)

    def arrive_rb(k):
        other = at_b(k)
        return pltpu.make_async_remote_copy(
            src_ref=send_rb.at[other], dst_ref=recv_rb.at[other], send_sem=rb_s.at[k], recv_sem=rb_r.at[other],
            device_id=peer_b(other), device_id_type=MESH)

    def copy_ra(k):
        other = at_a(k)
        return pltpu.make_async_remote_copy(
            src_ref=send_ra, dst_ref=recv_ra.at[my_a], send_sem=ra_s.at[k], recv_sem=ra_r.at[my_a],
            device_id=peer_a(other), device_id_type=MESH)

    def arrive_ra(k):
        other = at_a(k)
        return pltpu.make_async_remote_copy(
            src_ref=send_ra, dst_ref=recv_ra.at[other], send_sem=ra_s.at[k], recv_sem=ra_r.at[other],
            device_id=peer_a(other), device_id_type=MESH)

    def ring(e, m):
        to = (me + m) % 128
        return pltpu.make_async_remote_copy(
            src_ref=send_ring.at[e, m - 1], dst_ref=recv_ring.at[e, m - 1],
            send_sem=ring_s.at[e, m - 1], recv_sem=ring_r.at[e, m - 1],
            device_id=(to // 32, to % 32), device_id_type=MESH)

    def upstream(m):
        to = (me + 128 - m) % 128
        return pltpu.make_async_remote_copy(
            src_ref=table_send, dst_ref=table.at[m], send_sem=st_s.at[m], recv_sem=st_r.at[m],
            device_id=(to // 32, to % 32), device_id_type=MESH)

    def each(count, action):
        for k in range(1, count):
            action(k)

    pl.semaphore_wait(barrier, NA + NB - 2 + 2 * G)
    each(NA, lambda k: copy_a(k).start())
    recv_a[my_a] = send_a[my_a // 2]
    loads[8].wait()
    loads[10].wait()
    for c in range(ROWS):
        cols = slice(c * LANES, (c + 1) * LANES)
        wide = slice(c % 2 * LANES, (c % 2 + 1) * LANES)
        for q in range(2):
            table_send[q, c // 2 : c // 2 + 1, wide] = rates[2 + q : 3 + q, cols]
    for p in range(2):
        table_send[2, :, p * LANES : (p + 1) * LANES] = step[pl.ds(p, 8, stride=2), :].astype(F32)
    for m in range(1, G):
        upstream(m).start()
    table[0] = table_send[...]

    for i in (4, 3, 7, 9, 11):
        loads[i].wait()
    flat = trans[...].reshape(KINDS * PATCH, PATCH)
    t_hi, t_low = split2(flat)
    tmat[:, 0:PATCH] = t_hi.astype(BF16)
    tmat[:, PATCH : 2 * PATCH] = t_hi.astype(BF16)
    tmat[:, 2 * PATCH : 3 * PATCH] = t_low.astype(BF16)

    def transit_chunk(j):
        for kk in range(CHUNK):
            k = j * CHUNK + kk
            hi, low = split2(grown[pl.ds(pl.multiple_of(k * PATCH, PATCH), PATCH), :])
            cols = slice(kk * LANES, (kk + 1) * LANES)
            rhs[0:PATCH, cols] = hi.astype(BF16)
            rhs[PATCH : 2 * PATCH, cols] = low.astype(BF16)
            rhs[2 * PATCH : 3 * PATCH, cols] = hi.astype(BF16)
        moved = nn_dot(tmat[...], rhs[...])
        for kk in range(CHUNK):
            cols = slice(kk * LANES, (kk + 1) * LANES)
            total = moved[0:PATCH, cols] * weight[0:1, :]
            for kind in range(1, KINDS):
                total += moved[kind * PATCH : (kind + 1) * PATCH, cols] * weight[kind : kind + 1, :]
            tr_out[pl.ds(j * CHUNK + kk, PATCH, stride=BINS), :] = total

    lane16 = lax.broadcasted_iota(jnp.int32, (ROWS, LANES), 1)
    stride = step[...]
    path[1] = jnp.where(stride > 0, sub16 * LANES + lane16 + stride, -1)

    sub256 = lax.broadcasted_iota(jnp.int32, (WIDE, LANES), 0).astype(F32).astype(BF16)

    def follow(k):
        count = (k + 1) * 8
        sub_rows = lax.broadcasted_iota(jnp.int32, (PAD[k], LANES), 0)
        if k < G:
            fields = []
            for f in range(3):
                hi, low = split2(jnp.concatenate([table[m, f] for m in range(k + 1)], axis=0))
                fields += [hi, low]
            lookup = jnp.concatenate(fields, axis=0).astype(BF16)

        def piece(i, _):
            for j in range(4):
                c = i * 4 + j
                cells = path[k, pl.ds(c, 1), :]
                cols = pl.ds(pl.multiple_of(c * LANES, LANES), LANES)
                lane = jnp.broadcast_to((cells & (WIDE - 1)).astype(F32), (16, LANES)).astype(BF16)
                lane = jnp.concatenate([lane] * (WIDE // 16), axis=0)
                hot = jnp.where(sub256 == lane, jnp.ones_like(lane), jnp.zeros_like(lane))
                lane_step[k - 1, cols, :] = hot.T
                rows = jnp.where(sub_rows == (cells >> 8), 1.0, 0.0)
                row_step[OFF[k - 1] : OFF[k], cols] = rows.astype(BF16)
                if k < G:
                    found = nn_dot(lookup, hot)
                    values = []
                    for f in range(3):
                        both = found[2 * f * count : (2 * f + 1) * count] + found[(2 * f + 1) * count : (2 * f + 2) * count]
                        values.append(jnp.sum(both * rows[:count], axis=0, keepdims=True))
                    path_rate[k, 0, pl.ds(c, 1), :] = values[0]
                    path_rate[k, 1, pl.ds(c, 1), :] = values[1]
                    hop = (values[2] + 0.5).astype(jnp.int32)
                    path[k + 1, pl.ds(c, 1), :] = jnp.where(hop > 0, cells + hop, -1)
            return 0

        lax.fori_loop(0, 4, piece, 0, unroll=UNROLL)

    listed = jnp.zeros((8, LANES), jnp.int32)
    for a in range(NA):
        row = jnp.broadcast_to(tgt[a // 2 : a // 2 + 1, :], (8, LANES))
        row = pltpu.roll(row, ((a - (a % 2) * 8) * 8) % LANES, 1)
        listed = jnp.where(((block8 - sub8) & 15) == a, row, listed)
    for bit in (1, 2, 4):
        listed = jnp.where((sub8 & bit) != 0, pltpu.roll(listed, LANES - bit * 8, 1), listed)
    list_lane = listed & (LANES - 1)
    list_row = listed >> 7
    for b in range(NB):
        cols = slice(b * LANES, (b + 1) * LANES)
        hot = jnp.where(sub128 == list_lane[b : b + 1, :], 1.0, 0.0).astype(BF16)
        lane_rcv[:, cols] = hot
        lane_rcv_t[cols, :] = hot.T
        row_rcv[:, cols] = jnp.where(sub16 == list_row[b : b + 1, :], 1.0, 0.0)

    for c in range(ROWS):
        cols = slice(c * LANES, (c + 1) * LANES)
        for q in range(4):
            state[q, c : c + 1, :] = water[q : q + 1, cols]
            state[4 + q, c : c + 1, :] = rates[q : q + 1, cols]
    for k in range(1, A_PATHS):
        upstream(k).wait_recv()
        follow(k)

    each(NA, lambda k: arrive_a(k).wait_recv())
    half = my_a % 2
    tiles = []
    for a in range(NA):
        tiles.append(pltpu.roll(recv_a[a], (half * 64 + a * 8) % LANES, 1))
    for b in range(NB):
        mixed = jnp.zeros((8, LANES), F32)
        for a in range(NA):
            mixed = jnp.where(block8 == (a + b) % 16, tiles[a], mixed)
        send_b[b] = pltpu.roll(mixed, (LANES - b * 8) % LANES, 1)
    each(NB, lambda k: copy_b(k).start())
    recv_b[my_b] = send_b[my_b]
    for k in range(A_PATHS, G + 1):
        if k < G:
            upstream(k).wait_recv()
        follow(k)
    for q in range(2):
        rate = [state[6 + q]] + [path_rate[k, q] for k in range(1, G)]
        before = None
        for k in range(G + 1):
            now = {}
            for n in range(k, G + 1):
                if k == 0:
                    value = (1.0 - rate[0]) * now[n - 1] if n else jnp.ones((ROWS, LANES), F32)
                else:
                    value = rate[k - 1] * before[n - 1]
                    if n > k:
                        value += (1.0 - rate[k]) * now[n - 1]
                now[n] = value
                moved_by[q, k, n] = value
            before = now
    each(NB, lambda k: arrive_b(k).wait_recv())

    for b in range(NB):
        cols = slice(b * LANES, (b + 1) * LANES)
        hot = row_rcv[:, cols]
        for s, part in enumerate(split3(recv_b[b])):
            for f in range(3):
                lhs_rcv[(s * 3 + f) * ROWS : (s * 3 + f + 1) * ROWS, cols] = (part[f : f + 1, :] * hot).astype(BF16)
    landed = nn_dot(lhs_rcv[...], lane_rcv_t[...])
    landed = (landed[0:48] + landed[48:96] + landed[96:144]) * (1.0 / NSUB)
    surface = (landed[0:ROWS], landed[ROWS : 2 * ROWS])
    deep = (landed[2 * ROWS : 3 * ROWS], jnp.zeros((ROWS, LANES), F32))

    def macro_step(e, carry):
        hill, channel = carry[0:2], carry[2:4]
        hill_next, kept, masses = [], [], [{}, {}]
        for q in range(2):
            water_now = hill[q]
            given = []
            for _ in range(G):
                hill_out = state[4 + q] * water_now
                given.append(hill_out + deep[q])
                water_now = water_now - hill_out + surface[q]
            hill_next.append(water_now)
            for k in range(G + 1):
                total = moved_by[q, k, G] * channel[q]
                for n in range(k, G):
                    total += moved_by[q, k, n] * given[G - 1 - n]
                if k == 0:
                    kept.append(total)
                    continue
                masses[q][k] = total
        sums = [[0.0] * (G + 1) for _ in range(2)]

        def send(m):
            for q in range(2):
                send_ring[e, m - 1, q] = sums[q][m]
            ring(e, m).start()

        for k in range(G, 0, -1):
            pad = PAD[k]
            for q in range(2):
                for s, part in enumerate(split2(masses[q][k])):
                    start = 4 * OFF[k - 1] + (q * 2 + s) * pad
                    for c in range(ROWS):
                        cols = slice(c * LANES, (c + 1) * LANES)
                        value = jnp.broadcast_to(part[c : c + 1, :], (16, LANES)).astype(BF16)
                        value = jnp.concatenate([value] * (pad // 16), axis=0)
                        lhs_step[start : start + pad, cols] = value * row_step[OFF[k - 1] : OFF[k], cols]
            spread = nn_dot(lhs_step[4 * OFF[k - 1] : 4 * OFF[k], :], lane_step[k - 1])
            for q in range(2):
                both = spread[2 * q * pad : (2 * q + 1) * pad] + spread[(2 * q + 1) * pad : (2 * q + 2) * pad]
                for m in range(k + 1):
                    sums[q][m] = sums[q][m] + both[m * 8 : (m + 1) * 8]
            if k == EARLY:
                for m in range(G, EARLY - 1, -1):
                    send(m)
        for m in range(EARLY - 1, 0, -1):
            send(m)
        for j in range(CHUNKS_STEP):
            transit_chunk(e * CHUNKS_STEP + j)
        came = [sums[q][0] for q in range(2)]
        for m in range(1, G + 1):
            ring(e, m).wait_recv()
            for q in range(2):
                came[q] = came[q] + recv_ring[e, m - 1, q]
        for q in range(2):
            fold[q, pl.ds(0, 8, stride=2), :] = came[q][:, :LANES]
            fold[q, pl.ds(1, 8, stride=2), :] = came[q][:, LANES:]
        new = [kept[q] + fold[q] for q in range(2)]
        return (*hill_next, *new)

    final = lax.fori_loop(0, STEPS, macro_step, tuple(state[q] for q in range(4)))
    stored = final[2] + final[3]
    inundation = stored / (stored + cap[...])
    lhs = jnp.concatenate(split3(inundation), axis=0).astype(BF16)
    seen = nn_dot(lhs, lane_rcv[...])
    seen = (seen[0:16] + seen[16:32] + seen[32:48]) * row_rcv[...]
    for b in range(NB):
        row = jnp.sum(seen[:, b * LANES : (b + 1) * LANES], axis=0, keepdims=True)
        send_rb[b] = jnp.broadcast_to(row, (8, LANES))
    each(NB, lambda k: copy_rb(k).start())
    recv_rb[my_b] = send_rb[my_b]
    for c in range(ROWS):
        cols = slice(c * LANES, (c + 1) * LANES)
        for q in range(4):
            river_out[q : q + 1, cols] = final[q][c : c + 1, :]
    for r in range(8):
        cols = slice(r * LANES, (r + 1) * LANES)
        onehot_src_t[cols, :] = onehot_src[:, cols].T
    for j in range(CHUNKS_STEP * STEPS, BINS // CHUNK):
        transit_chunk(j)
    stores = (
        pltpu.make_async_copy(tr_out, tr_hbm, out_sem.at[0]),
        pltpu.make_async_copy(river_out, river_hbm, out_sem.at[1]),
    )
    for copy in stores:
        copy.start()
    each(NB, lambda k: arrive_rb(k).wait_recv())
    gathered = jnp.zeros((8, LANES), F32)
    for b in range(NB):
        gathered = jnp.where(sub8 == b, recv_rb[b], gathered)
    send_ra[...] = gathered
    each(NA, lambda k: copy_ra(k).start())
    recv_ra[my_a] = gathered
    each(NA, lambda k: arrive_ra(k).wait_recv())
    for r in range(8):
        even = pltpu.roll(recv_ra[2 * r], (LANES - my_a * 8) % LANES, 1)
        odd = pltpu.roll(recv_ra[2 * r + 1], (64 + LANES - my_a * 8) % LANES, 1)
        pair = jnp.where(lane8 < 64, even, odd)
        for bit in (1, 2, 4):
            pair = jnp.where((sub8 & bit) != 0, pltpu.roll(pair, bit * 8, 1), pair)
        row = jnp.sum(jnp.where((block8 & 7) == sub8, pair, 0.0), axis=0, keepdims=True) * share[r : r + 1, :]
        hi, mid, low = split3(row)
        tile = jnp.where(sub16 == 0, hi, jnp.where(sub16 == 1, mid, jnp.where(sub16 == 2, low, 0.0)))
        lhs_back[:, r * LANES : (r + 1) * LANES] = tile.astype(BF16)
    felt = nn_dot(lhs_back[...], onehot_src_t[...])
    flood_out[...] = felt[0:1] + felt[1:2] + felt[2:3]
    store = pltpu.make_async_copy(flood_out, flood_hbm, out_sem.at[2])
    store.start()

    each(NA, lambda k: copy_a(k).wait_send())
    each(NB, lambda k: copy_b(k).wait_send())
    each(NB, lambda k: copy_rb(k).wait_send())
    each(NA, lambda k: copy_ra(k).wait_send())

    for m in range(1, G):
        upstream(m).wait_send()
    for e in range(STEPS):
        for m in range(1, G + 1):
            ring(e, m).wait_send()
    for copy in (*stores, store):
        copy.wait()


def survive_kernel(
    mass_in, traits_in, flooded_in, river_in, out, flooded_out, river_out,
    mass, traits, flooded, survival, load_sem, store_sem,
):
    block = PATCH * BINS // 6
    small = [
        pltpu.make_async_copy(flooded_in, flooded, load_sem.at[6]),
        pltpu.make_async_copy(traits_in, traits, load_sem.at[7]),
    ]
    pieces = [pl.ds(i * block, block) for i in range(6)]
    loads = [pltpu.make_async_copy(mass_in.at[p, :], mass.at[p, :], load_sem.at[i]) for i, p in enumerate(pieces)]
    stores = [pltpu.make_async_copy(mass.at[p, :], out.at[p, :], store_sem.at[i]) for i, p in enumerate(pieces)]
    stores += [
        pltpu.make_async_copy(flooded, flooded_out, store_sem.at[6]),
        pltpu.make_async_copy(river_in, river_out, store_sem.at[7]),
    ]
    for copy in (*small, *loads, stores[7]):
        copy.start()
    for copy in small:
        copy.wait()
    stores[6].start()
    rows = lax.broadcasted_iota(jnp.int32, (BINS, BINS), 0)
    cols = lax.broadcasted_iota(jnp.int32, (BINS, BINS), 1)
    mortality = jnp.sum(jnp.where(rows == cols, traits[3:4, :], 0.0), axis=1, keepdims=True)
    survival[...] = jnp.exp(-mortality * flooded[...])
    for i in range(6):
        loads[i].wait()
        for p in range(8):
            rows = slice(i * block + p * BINS, i * block + (p + 1) * BINS)
            mass[rows, :] = mass[rows, :] * survival[...]
        stores[i].start()
    for copy in stores:
        copy.wait()


def shards(
    biomass, patch_area, cohort_traits, cell_forcing, disturb_weight, transitions, land_source, pair_share,
    river_target, downstream_step, river_water, river_rates, capacity,
):
    hbm = pl.BlockSpec(memory_space=pltpu.HBM)
    dma = pltpu.SemaphoreType.DMA
    tile = (8, LANES)
    n_rows = PATCH * BINS
    transited, flooded, river_state = pl.pallas_call(
        main_kernel,
        out_shape=(
            jax.ShapeDtypeStruct((n_rows, LANES), F32),
            jax.ShapeDtypeStruct((1, LANES), F32),
            jax.ShapeDtypeStruct((4, ROWS * LANES), F32),
        ),
        in_specs=[hbm] * 13,
        out_specs=(hbm, hbm, hbm),
        scratch_shapes=[
            pltpu.VMEM((n_rows, LANES), F32),
            pltpu.VMEM((1, LANES), F32),
            pltpu.VMEM((4, ROWS * LANES), F32),
            dma((3,)),
            pltpu.VMEM((BINS // 8, PATCH, 8, LANES), F32),
            pltpu.VMEM((PATCH, LANES), F32),
            pltpu.SMEM((4, BINS), F32),
            pltpu.VMEM((5, LANES), F32),
            pltpu.VMEM((KINDS, LANES), F32),
            pltpu.VMEM((KINDS, PATCH, PATCH), F32),
            pltpu.VMEM(tile, jnp.int32),
            pltpu.VMEM(tile, F32),
            pltpu.VMEM(tile, jnp.int32),
            pltpu.VMEM((ROWS, LANES), jnp.int32),
            pltpu.VMEM((4, ROWS * LANES), F32),
            pltpu.VMEM((4, ROWS * LANES), F32),
            pltpu.VMEM((ROWS, LANES), F32),
            dma((12,)),
            dma((BINS // 8,)),
            pltpu.VMEM((n_rows, LANES), F32),
            pltpu.VMEM((KINDS * PATCH, 3 * PATCH), BF16),
            pltpu.VMEM((3 * PATCH, CHUNK * LANES), BF16),
            pltpu.VMEM((LANES, 1024), BF16),
            pltpu.VMEM((1024, LANES), BF16),
            pltpu.VMEM((1024, LANES), BF16),
            pltpu.VMEM((LANES, 1024), BF16),
            pltpu.VMEM((ROWS, 1024), F32),
            pltpu.VMEM((G, ROWS * LANES, WIDE), BF16),
            pltpu.VMEM((OFF[G], ROWS * LANES), BF16),
            pltpu.VMEM((4 * OFF[G], ROWS * LANES), BF16),
            pltpu.VMEM((9 * ROWS, 1024), BF16),
            pltpu.VMEM((16, 1024), BF16),
            pltpu.VMEM((8, ROWS, LANES), F32),
            pltpu.VMEM((2, ROWS, LANES), F32),
            pltpu.VMEM((2, G + 1, G + 1, ROWS, LANES), F32),
            pltpu.VMEM((G, 3, 8, WIDE), F32),
            pltpu.VMEM((3, 8, WIDE), F32),
            pltpu.VMEM((G + 1, ROWS, LANES), jnp.int32),
            pltpu.VMEM((G, 2, ROWS, LANES), F32),
            dma((G,)), dma((G,)),
            pltpu.VMEM((8, *tile), F32),
            pltpu.VMEM((NA, *tile), F32),
            pltpu.VMEM((NB, *tile), F32),
            pltpu.VMEM((NB, *tile), F32),
            pltpu.VMEM((NB, *tile), F32),
            pltpu.VMEM((NB, *tile), F32),
            pltpu.VMEM(tile, F32),
            pltpu.VMEM((NA, *tile), F32),
            pltpu.VMEM((STEPS, G, 2, 8, WIDE), F32),
            pltpu.VMEM((STEPS, G, 2, 8, WIDE), F32),
            dma((NA,)), dma((NA,)), dma((NB,)), dma((NB,)), dma((NB,)), dma((NB,)), dma((NA,)), dma((NA,)),
            dma((STEPS, G)), dma((STEPS, G)),
        ],
        compiler_params=pltpu.CompilerParams(
            collective_id=0, has_side_effects=True, vmem_limit_bytes=60 * 1024 * 1024),
        name="hour",
    )(
        biomass, patch_area, cohort_traits, cell_forcing, disturb_weight, transitions,
        land_source.reshape(8, LANES), pair_share.reshape(8, LANES), river_target.reshape(8, LANES),
        downstream_step.reshape(ROWS, LANES), river_water, river_rates, capacity.reshape(ROWS, LANES),
    )
    new_biomass, flooded, river_state = pl.pallas_call(
        survive_kernel,
        out_shape=(
            jax.ShapeDtypeStruct((n_rows, LANES), F32),
            jax.ShapeDtypeStruct((1, LANES), F32),
            jax.ShapeDtypeStruct((4, ROWS * LANES), F32),
        ),
        in_specs=[hbm] * 4,
        out_specs=(hbm, hbm, hbm),
        scratch_shapes=[
            pltpu.VMEM((n_rows, LANES), F32),
            pltpu.VMEM((4, BINS), F32),
            pltpu.VMEM((1, LANES), F32),
            pltpu.VMEM((BINS, LANES), F32),
            dma((8,)),
            dma((8,)),
        ],
        compiler_params=pltpu.CompilerParams(vmem_limit_bytes=60 * 1024 * 1024),
        name="survive",
    )(transited, cohort_traits, flooded, river_state)
    return new_biomass.reshape(PATCH, BINS, LANES), flooded.reshape(LANES), river_state


def solution(mesh):
    both = ("comp", "cell")
    return jax.shard_map(
        shards,
        mesh=mesh,
        in_specs=(
            P(None, None, both), P(None, both), P(), P(None, both), P(None, both), P(), P(both), P(both), P(both),
            P(both), P(None, both), P(None, both), P(both),
        ),
        out_specs=(P(None, None, both), P(both), P(None, both)),
        check_vma=False,
    )
```
